32 devices in a mesh: pipe: 4 (over y, core), seq: 8 (over z, x).
Axes of the slice: x: 2, y: 2, z: 4, core: 2. Of those that a mesh axis runs over, the one named last changes fastest.
Arguments:
- act_in: bfloat16 [4, 1024, 2048], P('pipe', 'seq'), may hold values from -20 to 20
- saved_in: bfloat16 [4, 1024, 2048], P('pipe', 'seq'), may hold values from -20 to 20
- grad_in: bfloat16 [4, 1024, 2048], P('pipe', 'seq'), may hold values from -18 to 18
- gain: float32 [4, 2048], P('pipe'), may hold values from 0.5 to 1.5
- weight: bfloat16 [4, 512, 4, 512], P('pipe', 'seq'), may hold values from -0.25 to 0.25
- left_blocks: bfloat16 [4, 16, 64, 64], P('pipe', 'seq'), may hold values from -0.75 to 0.75
- right_blocks: bfloat16 [4, 64, 16, 16], P('pipe', 'seq'), may hold values from -1.5 to 1.5
Outputs:
- handed_on: bfloat16 [4, 1024, 2048], P('pipe', 'seq')
- grad_handed: bfloat16 [4, 1024, 2048], P('pipe', 'seq')
- grad_weight: float32 [4, 512, 4, 512], P('pipe', 'seq')
- grad_gain: float32 [4, 2048], P('pipe')
- grad_left: float32 [4, 16, 64, 64], P('pipe', 'seq')
- grad_right: float32 [4, 64, 16, 16], P('pipe', 'seq')
The draws below stay inside these ranges and needn't reach their ends.
All inputs are finite; a program needn't handle non-finite values.
Results may differ from the reference program's by a relative error of at most 0.0076.
Values may be sent and summed in bfloat16 or wider, within the bound.
No kernel may reach another device: no remote copies, remote signals or barrier semaphores. Data moves between devices by JAX's collectives and lax.ppermute only.
A program may use at most 64 MiB of HBM per device.

```python
import jax
import jax.numpy as jnp
from jax import lax

D = 2048
NB = 4
BD = 512
BLOCK = 64
TOKENS = 1024
SEQ_BLOCKS = 16
N_PIPE = 4


def activation_field(key):
    key_scale, key_base = jax.random.split(key, 2)
    shape = (N_PIPE, TOKENS, D)
    row_scale = jnp.exp(jax.random.uniform(key_scale, (N_PIPE, TOKENS, 1), jnp.float32, jnp.log(0.5), jnp.log(5.0)))
    values = jax.random.normal(key_base, shape, jnp.float32)
    values = jnp.clip(values, -4.0, 4.0)
    return (values * row_scale).astype(jnp.bfloat16)


def draw_act_in(key, part):
    return activation_field(jax.random.fold_in(key, 101))


def draw_saved_in(key, part):
    return activation_field(jax.random.fold_in(key, 202))


def draw_grad_in(key, part):
    key_scale, key_base = jax.random.split(jax.random.fold_in(key, 303), 2)
    shape = (N_PIPE, TOKENS, D)
    position = jnp.arange(TOKENS, dtype=jnp.float32).reshape(1, TOKENS, 1)
    trend = 1.0 + 2.0 * position / (TOKENS - 1)
    row_scale = jnp.exp(jax.random.uniform(key_scale, (N_PIPE, TOKENS, 1), jnp.float32, jnp.log(0.5), jnp.log(1.5))) * trend
    values = jax.random.normal(key_base, shape, jnp.float32)
    values = jnp.clip(values, -4.0, 4.0)
    return (values * row_scale).astype(jnp.bfloat16)


def steps_of(rng, extent, pieces, least, high):
    def one(dim, shards_of):
        draws = jax.random.uniform(jax.random.fold_in(jax.random.fold_in(rng, 6), dim), (shards_of,), jnp.float32, least / len(pieces), high / len(pieces))
        return jnp.repeat(jnp.exp(draws), extent[dim] // shards_of).reshape((-1,) + (1,) * (len(extent) - dim - 1))

    level = one(*pieces[0])
    for cut in pieces[1:]:
        level = level * one(*cut)
    return level


def gaussian(key, dims, scale, bound, cuts=(), kind=jnp.bfloat16):
    drawn = scale * jax.random.normal(key, dims, jnp.float32)
    if cuts:
        drawn = drawn * steps_of(key, dims, cuts, -0.22, 0.18)
    return jnp.clip(drawn, -bound, bound).astype(kind)


def setup_inputs(seed: int = 0) -> dict:
    keys = jax.random.split(jax.random.key(seed), 8)
    return {
        "act_in": draw_act_in(jax.random.fold_in(keys[7], 71), 0),
        "saved_in": draw_saved_in(jax.random.fold_in(keys[7], 71), 0),
        "grad_in": draw_grad_in(jax.random.fold_in(keys[7], 71), 0),
        "gain": jnp.clip(1.0 + 0.1 * jax.random.normal(keys[3], (N_PIPE, D), jnp.float32), 0.5, 1.5),
        "weight": gaussian(keys[4], (N_PIPE, BD, NB, BD), BD ** -0.5, 0.25, ((0, 4), (1, 8))),
        "left_blocks": gaussian(keys[5], (N_PIPE, SEQ_BLOCKS, BLOCK, BLOCK), BLOCK ** -0.5, 0.75, ((0, 4), (1, 8))),
        "right_blocks": gaussian(keys[6], (N_PIPE, BLOCK, SEQ_BLOCKS, SEQ_BLOCKS), SEQ_BLOCKS ** -0.5, 1.5, ((0, 4), (1, 8))),
    }


def normalize(rows, gain_row):
    widened = rows.astype(jnp.float32)
    inv_rms = lax.rsqrt(lax.optimization_barrier(jnp.mean(widened * widened, axis=-1, keepdims=True)) + 1e-06)
    normed = widened * inv_rms
    return (inv_rms, normed, (normed * gain_row).astype(jnp.bfloat16))

def section(operands):
    current, stored, upstream, gain_row, weight, left_factor, right_factor = operands
    tokens_all, model_width = current.shape
    nblocks = weight.shape[1]
    inner_width = weight.shape[2]
    groups = left_factor.shape[0]
    block_len = left_factor.shape[1]
    wide_weight = weight.astype(jnp.float32)
    left_wide = left_factor.astype(jnp.float32)
    right_wide = right_factor.astype(jnp.float32)

    def project_in(normin):
        split_rows = normin.reshape(tokens_all, nblocks, inner_width).astype(jnp.float32)
        proj = jnp.einsum('tki,ikj->tkj', split_rows, wide_weight).astype(jnp.bfloat16)
        return proj.reshape(groups, block_len, model_width)

    def first_factor(proj):
        return jnp.einsum('abc,acd->abd', left_wide, proj.astype(jnp.float32)).astype(jnp.bfloat16)

    def second_factor(first_mix):
        return jnp.einsum('bxy,ybd->xbd', right_wide, first_mix.astype(jnp.float32)).astype(jnp.bfloat16)
    cur_scale, cur_norm, cur_in = normalize(current, gain_row)
    sto_scale, sto_norm, sto_in = normalize(stored, gain_row)
    cur_proj = project_in(cur_in)
    cur_mix = second_factor(first_factor(cur_proj))
    output = (current.astype(jnp.float32) + cur_proj.reshape(tokens_all, model_width).astype(jnp.float32) * cur_mix.reshape(tokens_all, model_width).astype(jnp.float32)).astype(jnp.bfloat16)
    sto_proj = project_in(sto_in)
    sto_first = first_factor(sto_proj)
    sto_mix = second_factor(sto_first)
    upstream_g = upstream.reshape(groups, block_len, model_width).astype(jnp.float32)
    adjoint_mix = (upstream_g * sto_proj.astype(jnp.float32)).astype(jnp.bfloat16)
    adjoint_first = jnp.einsum('bxy,xbd->ybd', right_wide, adjoint_mix.astype(jnp.float32)).astype(jnp.bfloat16)
    right_grad = jnp.einsum('xbd,ybd->bxy', adjoint_mix.astype(jnp.float32), sto_first.astype(jnp.float32))
    local_grad = upstream_g * sto_mix.astype(jnp.float32) + jnp.einsum('abc,abd->acd', left_wide, adjoint_first.astype(jnp.float32))
    proj_grad = local_grad.astype(jnp.bfloat16).reshape(tokens_all, nblocks, inner_width).astype(jnp.float32)
    left_grad = jnp.einsum('abd,acd->abc', adjoint_first.astype(jnp.float32), sto_proj.astype(jnp.float32))
    normed_grad = jnp.einsum('tkj,ikj->tki', proj_grad, wide_weight).reshape(tokens_all, model_width)
    sto_split = sto_in.reshape(tokens_all, nblocks, inner_width).astype(jnp.float32)
    weight_grad = jnp.einsum('tki,tkj->ikj', sto_split, proj_grad)
    gain_grad = lax.optimization_barrier(jnp.sum(normed_grad * sto_norm, axis=0))
    scaled = normed_grad * gain_row
    input_grad = (upstream.astype(jnp.float32) + sto_scale * (scaled - sto_norm * lax.optimization_barrier(jnp.mean(scaled * sto_norm, axis=-1, keepdims=True)))).astype(jnp.bfloat16)
    return (output, input_grad, weight_grad, gain_grad, left_grad, right_grad)

def reference(act_in, saved_in, grad_in, gain, weight, left_blocks, right_blocks):
    results = lax.map(section, (act_in, saved_in, grad_in, gain, weight, left_blocks, right_blocks))
    handed_on = jnp.roll(results[0], 1, axis=0)
    grad_handed = jnp.roll(results[1], -1, axis=0)
    return (handed_on, grad_handed, results[2], results[3], results[4], results[5])
```

```python
import functools

import jax
import jax.numpy as jnp
from jax import lax
from jax.experimental import pallas as pl
from jax.experimental.pallas import tpu as pltpu
from jax.sharding import PartitionSpec as P

BF = jnp.bfloat16
F32 = jnp.float32
LANE = 128
SUB = 16
EPS = 1e-06
VMEM = 48 * 1024 * 1024


def position(nb):
    me = lax.axis_index("seq")
    group = me // nb
    place = me % nb
    block = place ^ ((nb // 2) * (group % 2))
    return group, place, block


def split3(x):
    hi = x.astype(BF).astype(F32)
    mid = (x - hi).astype(BF).astype(F32)
    return hi, mid, x - hi - mid


def eye(n):
    return lax.broadcasted_iota(jnp.int32, (n, n), 0) == lax.broadcasted_iota(jnp.int32, (n, n), 1)


def to_row(col):
    return jnp.sum(jnp.where(eye(col.shape[0]), col, 0.0), axis=0, keepdims=True)


def to_col(row):
    return jnp.sum(jnp.where(eye(row.shape[1]), row, 0.0), axis=1, keepdims=True)


def mm(a, b, ca=1, cb=0):
    return lax.dot_general(a, b, (((ca,), (cb,)), ((), ())), preferred_element_type=F32)


def rows(start, size):
    return pl.ds(pl.multiple_of(start, size), size)


def call(body, outs, scratch=(), flops=0, name=None):
    def run(*args):
        nbytes = sum(a.size * a.dtype.itemsize for a in args) + sum(
            o.size * o.dtype.itemsize for o in outs
        )
        return pl.pallas_call(
            body,
            out_shape=list(outs),
            in_specs=[pl.BlockSpec(memory_space=pltpu.VMEM)] * len(args),
            out_specs=[pl.BlockSpec(memory_space=pltpu.VMEM)] * len(outs),
            scratch_shapes=list(scratch),
            compiler_params=pltpu.CompilerParams(vmem_limit_bytes=VMEM),
            cost_estimate=pl.CostEstimate(flops=flops, bytes_accessed=nbytes, transcendentals=0),
            name=name,
        )(*args)

    return run


def sds(shape, dtype=BF):
    return jax.ShapeDtypeStruct(shape, dtype)


def pack_weight_body(nb, w_ref, l_ref, r_ref, *outs):
    _, _, block = position(nb)
    r, bd = w_ref.shape[1], w_ref.shape[2]
    chunks = bd // LANE
    bl, ext = l_ref.shape[1], r_ref.shape[1]
    left = jnp.concatenate([l_ref[j].astype(F32) for j in range(l_ref.shape[0])], axis=1).astype(BF)
    right = jnp.concatenate([r_ref[j].astype(F32) for j in range(r_ref.shape[0])], axis=1).astype(BF)
    for d in range(nb):
        for ch in range(chunks):
            outs[d][ch * r : (ch + 1) * r, :] = w_ref[block ^ d, :, ch * LANE : (ch + 1) * LANE]
        outs[d][chunks * r : chunks * r + bl, :] = left
        outs[d][chunks * r + bl :, :] = right


def pack_tokens_body(nb, with_scale, x_ref, *outs):
    _, _, block = position(nb)
    t, width = x_ref.shape
    bd = width // nb
    chunks = bd // LANE
    if with_scale:
        x = x_ref[...].astype(F32)
        inv = lax.rsqrt(jnp.mean(x * x, axis=-1, keepdims=True) + EPS)
        parts = split3(to_row(inv))
        tile = jnp.concatenate(list(parts) + [jnp.zeros((SUB - 3, t), F32)], axis=0).astype(BF)
    for d in range(nb):
        for ch in range(chunks):
            lanes = pl.ds(pl.multiple_of((block ^ d) * bd + ch * LANE, LANE), LANE)
            outs[d][ch * t : (ch + 1) * t, :] = x_ref[:, lanes]
        if with_scale:
            outs[d][chunks * t :, :] = tile


def relay_body(nb, r4, ext, *refs):
    _, place, _ = position(nb)
    out = refs[nb]
    for d in range(nb):
        to = place ^ d
        out[rows(to * r4, r4), :] = refs[d][:r4, :]
        out[pl.ds(pl.multiple_of(nb * r4 + to * ext, ext), ext), :] = refs[d][refs[d].shape[0] - ext :, :]


def expand_matrix(ext):
    n = SUB * ext
    row = lax.broadcasted_iota(jnp.int32, (n, n), 0)
    col = lax.broadcasted_iota(jnp.int32, (n, n), 1)
    return jnp.where((row // ext == col % SUB) & (row % ext == col // SUB), 1.0, 0.0).astype(BF)


def same_position(n):
    row = lax.broadcasted_iota(jnp.int32, (n, n), 0)
    col = lax.broadcasted_iota(jnp.int32, (n, n), 1)
    return row % SUB == col % SUB


def assemble_body(nb, ngroups, r, ext, bl, *refs):
    group, place, _ = position(nb)
    msgs, relays = refs[:nb], refs[nb : nb + ngroups]
    wk_ref, mq_ref, bd_ref, all_ref = refs[nb + ngroups :]
    chunks = wk_ref.shape[1] // LANE
    r4 = chunks * r
    for e in range(ngroups):
        g = group ^ e
        for c in range(nb):
            for ch in range(chunks):
                wk_ref[rows((g * nb + c) * r, r), ch * LANE : (ch + 1) * LANE] = relays[e][
                    c * r4 + ch * r : c * r4 + (ch + 1) * r, :
                ]
            all_ref[g * nb + c] = relays[e][nb * r4 + c * ext : nb * r4 + (c + 1) * ext, :]
    nq = mq_ref.shape[0]
    per = nb * ngroups // nq
    n = SUB * ext
    turn = expand_matrix(ext)
    spread = jnp.where(
        lax.broadcasted_iota(jnp.int32, (n, ext), 0) // SUB
        == lax.broadcasted_iota(jnp.int32, (n, ext), 1),
        1.0,
        0.0,
    ).astype(BF)
    same = same_position(n)
    for q in range(nq):
        tiles = jnp.concatenate([all_ref[q * per + i] for i in range(per)], axis=1)
        wide = mm(tiles, turn).astype(BF)
        mq_ref[q] = jnp.where(same, mm(spread, wide), 0.0).astype(BF)
    half_row = lax.broadcasted_iota(jnp.int32, (LANE, LANE), 0) // bl
    half_col = lax.broadcasted_iota(jnp.int32, (LANE, LANE), 1) // bl
    for d in range(nb):
        tile = msgs[d][r4 : r4 + bl, :].astype(F32)
        both = jnp.concatenate([tile] * (LANE // bl), axis=0)
        bd_ref[place ^ d] = jnp.where(half_row == half_col, both, 0.0).astype(BF)


def unpack(msg, t, chunks):
    return jnp.concatenate([msg[ch * t : (ch + 1) * t, :] for ch in range(chunks)], axis=1)


def scale_of(msg, t, chunks):
    tile = msg[chunks * t : chunks * t + SUB, :].astype(F32)
    return to_col(tile[0:1] + tile[1:2] + tile[2:3])


def project_body(nb, *refs):
    _, place, block = position(nb)
    msgs = refs[:nb]
    gain_ref, wk_ref, bd_ref, normin_ref, proj_ref, first_ref = refs[nb:]
    t = LANE
    bd = wk_ref.shape[0]
    chunks = bd // LANE
    gain = gain_ref[:, pl.ds(pl.multiple_of(block * bd, LANE), bd)]
    for d in range(nb):
        x = unpack(msgs[d], t, chunks).astype(F32)
        normed = x * scale_of(msgs[d], t, chunks)
        normin_ref[rows((place ^ d) * t, t), :] = (normed * gain).astype(BF)
    proj_ref[...] = mm(normin_ref[...], wk_ref[...]).astype(BF)
    for c in range(nb):
        first_ref[c * t : (c + 1) * t, :] = mm(bd_ref[c], proj_ref[c * t : (c + 1) * t, :]).astype(BF)


def adjoint_body(nb, *refs):
    _, place, _ = position(nb)
    msgs = refs[:nb]
    proj_ref, adj_ref, grad_ref = refs[nb:]
    t = LANE
    chunks = proj_ref.shape[1] // LANE
    for d in range(nb):
        at = rows((place ^ d) * t, t)
        g = unpack(msgs[d], t, chunks)
        grad_ref[at, :] = g
        adj_ref[at, :] = (g.astype(F32) * proj_ref[at, :].astype(F32)).astype(BF)


def gather_positions(group, bl, parts, out_ref):
    blocks = parts[0].shape[0] // bl
    for e, part in enumerate(parts):
        base = (group ^ e) * blocks * SUB
        for q in range(bl // SUB):
            for a in range(blocks):
                out_ref[q, pl.ds(pl.multiple_of(base + a * SUB, SUB), SUB), :] = part[
                    a * bl + q * SUB : a * bl + (q + 1) * SUB, :
                ]


def forward_body(nb, ngroups, bl, *refs):
    group, place, _ = position(nb)
    firsts, rest = refs[:ngroups], refs[ngroups:]
    mq_ref, proj_ref = rest[:2]
    msgs = rest[2 : 2 + nb]
    outs = rest[2 + nb : 2 + 2 * nb]
    f_ref, mixed_ref = rest[2 + 2 * nb :]
    t = LANE
    chunks = proj_ref.shape[1] // LANE
    gather_positions(group, bl, firsts, f_ref)
    blocks = firsts[0].shape[0] // bl
    own = rows(group * blocks * SUB, blocks * SUB)
    for q in range(bl // SUB):
        mixed = mm(mq_ref[q, own, :], f_ref[q]).astype(BF)
        for a in range(blocks):
            mixed_ref[a * bl + q * SUB : a * bl + (q + 1) * SUB, :] = mixed[a * SUB : (a + 1) * SUB, :]
    for d in range(nb):
        at = rows((place ^ d) * t, t)
        x = unpack(msgs[d], t, chunks).astype(F32)
        outs[d][...] = (x + proj_ref[at, :].astype(F32) * mixed_ref[at, :].astype(F32)).astype(BF)


def backward_body(nb, ngroups, bl, ext, *refs):
    group, place, _ = position(nb)
    firsts, adjs, rest = refs[:ngroups], refs[ngroups : 2 * ngroups], refs[2 * ngroups :]
    mq_ref, bd_ref, proj_ref, grad_ref = rest[:4]
    adj_proj_ref = rest[4]
    outs = rest[5 : 5 + nb]
    f_ref, a_ref, mixed_ref, adj_first_ref, left_ref, right_ref = rest[5 + nb :]
    t = LANE
    gather_positions(group, bl, firsts, f_ref)
    gather_positions(group, bl, adjs, a_ref)
    blocks = firsts[0].shape[0] // bl
    own = rows(group * blocks * SUB, blocks * SUB)
    nq = bl // SUB
    n = SUB * ext
    for q in range(nq):
        mixed = mm(mq_ref[q, own, :], f_ref[q]).astype(BF)
        adj_first = mm(mq_ref[q, :, own], a_ref[q], 0, 0).astype(BF)
        for a in range(blocks):
            at = slice(a * bl + q * SUB, a * bl + (q + 1) * SUB)
            mixed_ref[at, :] = mixed[a * SUB : (a + 1) * SUB, :]
            adj_first_ref[at, :] = adj_first[a * SUB : (a + 1) * SUB, :]
    sums = []
    upper = lax.broadcasted_iota(jnp.int32, (bl, LANE), 1) < bl
    for c in range(nb):
        at = slice(c * t, (c + 1) * t)
        grad = grad_ref[at, :].astype(F32)
        proj = proj_ref[at, :]
        adj_first = adj_first_ref[at, :]
        adj_proj = (grad * mixed_ref[at, :].astype(F32) + mm(bd_ref[c], adj_first, 0, 0)).astype(BF)
        adj_proj_ref[at, :] = adj_proj
        sums.append(
            split3(to_row(jnp.sum(adj_proj.astype(F32) * proj.astype(F32), axis=1, keepdims=True)))
        )
        both = mm(adj_first, proj, 1, 1)
        left_ref[c] = jnp.where(upper, both[:bl, :], both[bl:, :]).astype(BF)
    tile = jnp.concatenate(
        [s for three in sums for s in three] + [jnp.zeros((SUB - 3 * nb, t), F32)], axis=0
    ).astype(BF)
    turn = expand_matrix(ext)
    same = same_position(n)
    per = right_ref.shape[0] // nq
    for q in range(nq):
        pairs = jnp.where(same, mm(a_ref[q], f_ref[q], 1, 1), 0.0)
        summed = jnp.sum(pairs.reshape(ext, SUB, n), axis=1).astype(BF)
        turned = mm(summed, turn, 1, 1).astype(BF)
        for i in range(per):
            right_ref[q * per + i] = turned[:, i * LANE : (i + 1) * LANE]
    for d in range(nb):
        to = place ^ d
        outs[d][:bl, :] = left_ref[to]
        outs[d][bl : bl + ext, :] = right_ref[group * nb + to]
        outs[d][bl + ext :, :] = tile


def weight_grad_body(nb, ngroups, normin_ref, adj_proj_ref, wk_ref, gain_ref, *refs):
    group, _, block = position(nb)
    own_ref, gain_part_ref, adj_norm_ref = refs[:3]
    sends = refs[3 : 3 + ngroups - 1]
    gw_ref = refs[3 + ngroups - 1]
    bd = wk_ref.shape[0]
    share = bd // ngroups
    adj_proj = adj_proj_ref[...]
    gw_ref[...] = mm(normin_ref[...], adj_proj, 0, 0)
    adj_norm = mm(adj_proj, wk_ref[...], 1, 1)
    adj_norm_ref[...] = adj_norm
    gain = gain_ref[:, pl.ds(pl.multiple_of(block * bd, LANE), bd)]
    part = jnp.sum(adj_norm * normin_ref[...].astype(F32), axis=0, keepdims=True) / gain
    gain_part_ref[...] = part
    tile = jnp.concatenate(list(split3(part)) + [jnp.zeros((SUB - 3, bd), F32)], axis=0).astype(BF)
    own_ref[...] = gw_ref[rows(group * share, share), :]
    for e in range(1, ngroups):
        sends[e - 1][:share, :] = gw_ref[rows((group ^ e) * share, share), :].astype(BF)
        sends[e - 1][share:, :] = tile


def weight_sum_body(nb, ngroups, own_ref, gain_part_ref, *refs):
    group, place, _ = position(nb)
    recvs = refs[: ngroups - 1]
    outs = refs[ngroups - 1 : ngroups - 1 + nb]
    total_ref, gains_ref = refs[ngroups - 1 + nb :]
    share, bd = own_ref.shape
    r = share // nb
    total = own_ref[...]
    gains_ref[group] = gain_part_ref[...]
    for e in range(1, ngroups):
        total = total + recvs[e - 1][:share, :].astype(F32)
        three = recvs[e - 1][share:, :].astype(F32)
        gains_ref[group ^ e] = three[0:1] + three[1:2] + three[2:3]
    total_ref[...] = total
    gain = gains_ref[0]
    for g in range(1, ngroups):
        gain = gain + gains_ref[g]
    tile = jnp.concatenate(list(split3(gain)) + [jnp.zeros((SUB - 3, bd), F32)], axis=0).astype(BF)
    for d in range(nb):
        outs[d][:r, :] = total_ref[rows((place ^ d) * r, r), :].astype(BF)
        outs[d][r:, :] = tile


def input_grad_body(nb, bl, ext, adj_norm_ref, grad_ref, gain_ref, *refs):
    _, place, block = position(nb)
    msgs, smalls, outs = refs[:nb], refs[nb : 2 * nb], refs[2 * nb :]
    t = LANE
    bd = adj_norm_ref.shape[1]
    chunks = bd // LANE
    width = bd * nb
    gain = gain_ref[:, pl.ds(pl.multiple_of(block * bd, LANE), bd)]
    tile = smalls[0][bl + ext :, :].astype(F32)
    for d in range(1, nb):
        tile = tile + smalls[d][bl + ext :, :].astype(F32)
    means = [
        to_col((tile[3 * c : 3 * c + 1] + tile[3 * c + 1 : 3 * c + 2] + tile[3 * c + 2 : 3 * c + 3]))
        * (1.0 / width)
        for c in range(nb)
    ]
    for d in range(nb):
        to = place ^ d
        at = rows(to * t, t)
        mean = means[0]
        for c in range(1, nb):
            mean = jnp.where(to == c, means[c], mean)
        inv = scale_of(msgs[d], t, chunks)
        normed = unpack(msgs[d], t, chunks).astype(F32) * inv
        scaled = adj_norm_ref[at, :] * gain
        outs[d][...] = (grad_ref[at, :].astype(F32) + inv * (scaled - normed * mean)).astype(BF)


def factors_body(nb, *refs):
    smalls = refs[:nb]
    left_ref, right_ref = refs[nb:]
    na, bl, _ = left_ref.shape
    npos, ext, _ = right_ref.shape
    left = smalls[0][:bl, :].astype(F32)
    right = smalls[0][bl : bl + ext, :].astype(F32)
    for d in range(1, nb):
        left = left + smalls[d][:bl, :].astype(F32)
        right = right + smalls[d][bl : bl + ext, :].astype(F32)
    for j in range(na):
        left_ref[j] = left[:, j * bl : (j + 1) * bl]
    for j in range(npos):
        right_ref[j] = right[:, j * ext : (j + 1) * ext]


def join_body(nb, *refs):
    _, _, block = position(nb)
    out = refs[nb]
    bd = refs[0].shape[1]
    for d in range(nb):
        out[:, pl.ds(pl.multiple_of((block ^ d) * bd, LANE), bd)] = refs[d][...]


def join_weight_body(nb, *refs):
    _, _, block = position(nb)
    gw_ref, gain_ref, by_block = refs[nb:]
    bd = gw_ref.shape[2]
    r = gw_ref.shape[0]
    for d in range(nb):
        by_block[block ^ d] = refs[d][:r, :].astype(F32)
        three = refs[d][r:, :].astype(F32)
        gain_ref[:, pl.ds(pl.multiple_of((block ^ d) * bd, LANE), bd)] = (
            three[0:1] + three[1:2] + three[2:3]
        )
    for k in range(nb):
        gw_ref[:, k, :] = by_block[k]


def shards(act_in, saved_in, grad_in, gain, weight, left_blocks, right_blocks):
    nseq = lax.axis_size("seq")
    npipe = lax.axis_size("pipe")
    _, t, width = act_in.shape
    _, r, nb, bd = weight.shape
    ngroups = nseq // nb
    bl = left_blocks.shape[2]
    ext = right_blocks.shape[2]
    npos = right_blocks.shape[1]
    chunks = bd // LANE
    tg = nb * t
    r4 = chunks * r
    nq = bl // SUB
    n = SUB * ext

    def within(parts):
        return [parts[0]] + [
            lax.ppermute(parts[d], "seq", [(s, s ^ d) for s in range(nseq)]) for d in range(1, nb)
        ]

    def across(block, e):
        mask = nb * e + (nb // 2) * (e % 2)
        return lax.ppermute(block, "seq", [(s, s ^ mask) for s in range(nseq)])

    def handed(parts, step):
        return [
            lax.ppermute(
                parts[d],
                ("pipe", "seq"),
                [
                    (p * nseq + s, ((p + step) % npipe) * nseq + (s ^ d))
                    for p in range(npipe)
                    for s in range(nseq)
                ],
            )
            for d in range(nb)
        ]

    part = functools.partial
    w_msgs = call(
        part(pack_weight_body, nb), [sds((r4 + bl + ext, LANE))] * nb, name="pack_weight"
    )(jnp.transpose(weight[0], (1, 0, 2)), left_blocks[0], right_blocks[0])
    w_msgs = within(w_msgs)
    sto_msgs = within(
        call(part(pack_tokens_body, nb, True), [sds((chunks * t + SUB, LANE))] * nb, name="pack_saved")(
            saved_in[0]
        )
    )
    grad_msgs = within(
        call(part(pack_tokens_body, nb, False), [sds((chunks * t, LANE))] * nb, name="pack_grad")(
            grad_in[0]
        )
    )
    cur_msgs = within(
        call(part(pack_tokens_body, nb, True), [sds((chunks * t + SUB, LANE))] * nb, name="pack_act")(
            act_in[0]
        )
    )
    (relay,) = call(part(relay_body, nb, r4, ext), [sds((nb * (r4 + ext), LANE))], name="relay")(*w_msgs)
    relays = [relay] + [across(relay, e) for e in range(1, ngroups)]
    wk, mq, bd_left = call(
        part(assemble_body, nb, ngroups, r, ext, bl),
        [sds((bd, bd)), sds((nq, n, n)), sds((nb, LANE, LANE))],
        [pltpu.VMEM((nseq, ext, LANE), BF)],
        name="assemble",
    )(*w_msgs, *relays)

    token_arrays = [sds((tg, bd))]
    proj_flops = 2 * tg * bd * bd
    sto_normin, sto_proj, sto_first = call(
        part(project_body, nb), token_arrays * 3, flops=proj_flops, name="project_saved"
    )(*sto_msgs, gain, wk, bd_left)
    sto_firsts = [sto_first] + [across(sto_first, e) for e in range(1, ngroups)]
    adj_mix, grad = call(part(adjoint_body, nb), token_arrays * 2, name="adjoint")(*grad_msgs, sto_proj)
    adj_mixes = [adj_mix] + [across(adj_mix, e) for e in range(1, ngroups)]
    _, cur_proj, cur_first = call(
        part(project_body, nb), token_arrays * 3, flops=proj_flops, name="project_act"
    )(*cur_msgs, gain, wk, bd_left)
    cur_firsts = [cur_first] + [across(cur_first, e) for e in range(1, ngroups)]

    wide = pltpu.VMEM((nq, n, bd), BF)
    tokens = pltpu.VMEM((tg, bd), BF)
    adj_proj, *smalls = call(
        part(backward_body, nb, ngroups, bl, ext),
        token_arrays + [sds((bl + ext + SUB, LANE))] * nb,
        [wide, wide, tokens, tokens, pltpu.VMEM((nb, bl, LANE), BF), pltpu.VMEM((nseq, ext, LANE), BF)],
        flops=nq * n * n * bd * 4,
        name="backward",
    )(*sto_firsts, *adj_mixes, mq, bd_left, sto_proj, grad)
    smalls = within(smalls)
    share = bd // ngroups
    own_gw, gain_part, adj_norm, *sends = call(
        part(weight_grad_body, nb, ngroups),
        [sds((share, bd), F32), sds((1, bd), F32), sds((tg, bd), F32)]
        + [sds((share + SUB, bd))] * (ngroups - 1),
        [pltpu.VMEM((bd, bd), F32)],
        flops=2 * proj_flops,
        name="weight_grad",
    )(sto_normin, adj_proj, wk, gain)
    recvs = [across(sends[e - 1], e) for e in range(1, ngroups)]
    adj_parts = call(
        part(input_grad_body, nb, bl, ext), [sds((t, bd))] * nb, name="input_grad"
    )(adj_norm, grad, gain, *sto_msgs, *smalls)
    adj_parts = handed(adj_parts, -1)
    out_parts = call(
        part(forward_body, nb, ngroups, bl),
        [sds((t, bd))] * nb,
        [wide, tokens],
        flops=nq * n * n * bd * 2,
        name="forward",
    )(*cur_firsts, mq, cur_proj, *cur_msgs)
    out_parts = handed(out_parts, 1)
    gw_parts = within(
        call(
            part(weight_sum_body, nb, ngroups),
            [sds((r + SUB, bd))] * nb,
            [pltpu.VMEM((share, bd), F32), pltpu.VMEM((ngroups, 1, bd), F32)],
            name="weight_sum",
        )(own_gw, gain_part, *recvs)
    )
    left_grad, right_grad = call(
        part(factors_body, nb),
        [sds((left_blocks.shape[1], bl, bl), F32), sds((npos, ext, ext), F32)],
        name="factors",
    )(*smalls)
    (handed_on,) = call(part(join_body, nb), [sds((t, width))], name="join_out")(*out_parts)
    (grad_handed,) = call(part(join_body, nb), [sds((t, width))], name="join_grad")(*adj_parts)
    weight_grad, gain_grad = call(
        part(join_weight_body, nb),
        [sds((r, nb, bd), F32), sds((1, width), F32)],
        [pltpu.VMEM((nb, r, bd), F32)],
        name="join_weight",
    )(*gw_parts)
    return (
        handed_on[None],
        grad_handed[None],
        weight_grad[None],
        gain_grad,
        left_grad[None],
        right_grad[None],
    )


def solution(mesh):
    tokens = P("pipe", "seq", None)
    factor = P("pipe", "seq", None, None)
    return jax.shard_map(
        shards,
        mesh=mesh,
        in_specs=(tokens, tokens, tokens, P("pipe", None), factor, factor, factor),
        out_specs=(tokens, tokens, factor, P("pipe", None), factor, factor),
        check_vma=False,
    )
```

```python
import functools

import jax
import jax.numpy as jnp
from jax import lax
from jax.experimental import pallas as pl
from jax.experimental.pallas import tpu as pltpu
from jax.sharding import PartitionSpec as P

BF = jnp.bfloat16
F32 = jnp.float32
LANE = 128
SUB = 16
EPS = 1e-06
COST = {"norm_saved": 2.0, "adjoint": 6.0, "mix_saved": 1, "norm_act": 3.0, "backward": 1, "mix_act": 2, "input_grad": 2}
VMEM = 48 * 1024 * 1024


def position(ngroups):
    me = lax.axis_index("seq")
    return me % ngroups, me // ngroups


def natural(pos, nb, ngroups, na):
    return ((pos // na % nb) * ngroups + pos // (nb * na)) * na + pos % na


def split3(x):
    hi = x.astype(BF).astype(F32)
    mid = (x - hi).astype(BF).astype(F32)
    return hi, mid, x - hi - mid


def eye(n):
    return lax.broadcasted_iota(jnp.int32, (n, n), 0) == lax.broadcasted_iota(jnp.int32, (n, n), 1)


def to_row(col):
    return jnp.sum(jnp.where(eye(col.shape[0]), col, 0.0), axis=0, keepdims=True)


def to_col(row):
    return jnp.sum(jnp.where(eye(row.shape[1]), row, 0.0), axis=1, keepdims=True)


def mm(a, b, ca=1, cb=0):
    return lax.dot_general(a, b, (((ca,), (cb,)), ((), ())), preferred_element_type=F32)


def rows(start, size):
    return pl.ds(pl.multiple_of(start, size), size)


def call(body, outs, scratch=(), flops=0, name=None):
    def run(*args, after=()):
        nin, nwait = len(args), len(after)

        def without_waits(*refs):
            return body(*refs[:nin], *refs[nin + nwait :])

        return pl.pallas_call(
            without_waits,
            out_shape=list(outs),
            in_specs=[pl.BlockSpec(memory_space=pltpu.VMEM)] * nin
            + [pl.BlockSpec(memory_space=pl.ANY)] * nwait,
            out_specs=[pl.BlockSpec(memory_space=pltpu.VMEM)] * len(outs),
            scratch_shapes=list(scratch),
            compiler_params=pltpu.CompilerParams(vmem_limit_bytes=VMEM),
            cost_estimate=pl.CostEstimate(flops=int(COST.get(name, 0.0) * 1e9), bytes_accessed=0, transcendentals=0),
            name=name,
        )(*args, *after)

    return run


def sds(shape, dtype=BF):
    return jax.ShapeDtypeStruct(shape, dtype)


def pack_weight_body(nb, ngroups, w_ref, l_ref, r_ref, *outs):
    _, block = position(ngroups)
    r, bd = w_ref.shape[1], w_ref.shape[2]
    chunks = bd // LANE
    bl, ext = l_ref.shape[1], r_ref.shape[1]
    left = jnp.concatenate([l_ref[j].astype(F32) for j in range(l_ref.shape[0])], axis=1).astype(BF)
    right = jnp.concatenate([r_ref[j].astype(F32) for j in range(r_ref.shape[0])], axis=1).astype(BF)
    for d in range(nb):
        for ch in range(chunks):
            outs[d][ch * r : (ch + 1) * r, :] = w_ref[block ^ d, :, ch * LANE : (ch + 1) * LANE]
        outs[d][chunks * r : chunks * r + bl, :] = left
        outs[d][chunks * r + bl :, :] = right


def pack_tokens_body(nb, ngroups, with_scale, x_ref, *outs):
    _, block = position(ngroups)
    t, width = x_ref.shape
    bd = width // nb
    chunks = bd // LANE
    if with_scale:
        x = x_ref[...].astype(F32)
        inv = lax.rsqrt(jnp.mean(x * x, axis=-1, keepdims=True) + EPS)
        parts = split3(to_row(inv))
        tile = jnp.concatenate(list(parts) + [jnp.zeros((SUB - 3, t), F32)], axis=0).astype(BF)
    for d in range(nb):
        for ch in range(chunks):
            lanes = pl.ds(pl.multiple_of((block ^ d) * bd + ch * LANE, LANE), LANE)
            outs[d][ch * t : (ch + 1) * t, :] = x_ref[:, lanes]
        if with_scale:
            outs[d][chunks * t :, :] = tile


def relay_body(nb, ngroups, r4, ext, *refs):
    _, place = position(ngroups)
    out = refs[nb]
    for d in range(nb):
        to = place ^ d
        out[rows(to * r4, r4), :] = refs[d][:r4, :]
        out[pl.ds(pl.multiple_of(nb * r4 + to * ext, ext), ext), :] = refs[d][refs[d].shape[0] - ext :, :]


def expand_matrix(ext, nb, ngroups, na):
    n = SUB * ext
    row = lax.broadcasted_iota(jnp.int32, (n, n), 0)
    col = lax.broadcasted_iota(jnp.int32, (n, n), 1)
    return jnp.where((row // ext == col % SUB) & (row % ext == natural(col // SUB, nb, ngroups, na)), 1.0, 0.0).astype(BF)


def same_position(n):
    row = lax.broadcasted_iota(jnp.int32, (n, n), 0)
    col = lax.broadcasted_iota(jnp.int32, (n, n), 1)
    return row % SUB == col % SUB


def assemble_body(nb, ngroups, r, ext, bl, *refs):
    group, place = position(ngroups)
    na = LANE // bl
    msgs, relays = refs[:nb], refs[nb : nb + ngroups]
    wk_ref, mq_ref, bd_ref, all_ref = refs[nb + ngroups :]
    chunks = wk_ref.shape[1] // LANE
    r4 = chunks * r
    for e in range(ngroups):
        g = group ^ e
        for c in range(nb):
            for ch in range(chunks):
                wk_ref[rows((c * ngroups + g) * r, r), ch * LANE : (ch + 1) * LANE] = relays[e][
                    c * r4 + ch * r : c * r4 + (ch + 1) * r, :
                ]
            all_ref[c * ngroups + g] = relays[e][nb * r4 + c * ext : nb * r4 + (c + 1) * ext, :]
    nq = mq_ref.shape[0]
    per = nb * ngroups // nq
    n = SUB * ext
    turn = expand_matrix(ext, nb, ngroups, na)
    spread = jnp.where(
        natural(lax.broadcasted_iota(jnp.int32, (n, ext), 0) // SUB, nb, ngroups, na)
        == lax.broadcasted_iota(jnp.int32, (n, ext), 1),
        1.0,
        0.0,
    ).astype(BF)
    same = same_position(n)
    for q in range(nq):
        tiles = jnp.concatenate([all_ref[q * per + i] for i in range(per)], axis=1)
        wide = mm(tiles, turn).astype(BF)
        mq_ref[q] = jnp.where(same, mm(spread, wide), 0.0).astype(BF)
    half_row = lax.broadcasted_iota(jnp.int32, (LANE, LANE), 0) // bl
    half_col = lax.broadcasted_iota(jnp.int32, (LANE, LANE), 1) // bl
    for d in range(nb):
        tile = msgs[d][r4 : r4 + bl, :].astype(F32)
        both = jnp.concatenate([tile] * (LANE // bl), axis=0)
        bd_ref[place ^ d] = jnp.where(half_row == half_col, both, 0.0).astype(BF)


def unpack(msg, t, chunks):
    return jnp.concatenate([msg[ch * t : (ch + 1) * t, :] for ch in range(chunks)], axis=1)


def scale_of(msg, t, chunks):
    tile = msg[chunks * t : chunks * t + SUB, :].astype(F32)
    return to_col(tile[0:1] + tile[1:2] + tile[2:3])


def norm_body(nb, ngroups, *refs):
    _, place = position(ngroups)
    msgs = refs[:nb]
    gain_ref, normin_ref = refs[nb:]
    t = LANE
    bd = normin_ref.shape[1]
    chunks = bd // LANE
    gain = gain_ref[:, pl.ds(pl.multiple_of(place * bd, LANE), bd)]
    for d in range(nb):
        x = unpack(msgs[d], t, chunks).astype(F32)
        normed = x * scale_of(msgs[d], t, chunks)
        normin_ref[rows((place ^ d) * t, t), :] = (normed * gain).astype(BF)


def project_body(normin_ref, wk_ref, bd_ref, proj_ref, first_ref):
    t = LANE
    proj_ref[...] = mm(normin_ref[...], wk_ref[...]).astype(BF)
    for c in range(bd_ref.shape[0]):
        at = slice(c * t, (c + 1) * t)
        first_ref[at, :] = mm(bd_ref[c], proj_ref[at, :]).astype(BF)


def adjoint_body(nb, ngroups, *refs):
    _, place = position(ngroups)
    msgs = refs[:nb]
    proj_ref, adj_ref, grad_ref = refs[nb:]
    t = LANE
    chunks = proj_ref.shape[1] // LANE
    for d in range(nb):
        at = rows((place ^ d) * t, t)
        g = unpack(msgs[d], t, chunks)
        grad_ref[at, :] = g
        adj_ref[at, :] = (g.astype(F32) * proj_ref[at, :].astype(F32)).astype(BF)


def gather_positions(group, bl, parts, out_ref):
    blocks = parts[0].shape[0] // bl
    for e, part in enumerate(parts):
        base = (group ^ e) * blocks * SUB
        for q in range(bl // SUB):
            for a in range(blocks):
                out_ref[q, pl.ds(pl.multiple_of(base + a * SUB, SUB), SUB), :] = part[
                    a * bl + q * SUB : a * bl + (q + 1) * SUB, :
                ]


def mix_body(ngroups, bl, *refs):
    group, _ = position(ngroups)
    firsts = refs[:ngroups]
    mq_ref, f_ref, mixed_ref = refs[ngroups:]
    gather_positions(group, bl, firsts, f_ref)
    blocks = firsts[0].shape[0] // bl
    own = rows(group * blocks * SUB, blocks * SUB)
    for q in range(bl // SUB):
        mixed = mm(mq_ref[q, own, :], f_ref[q]).astype(BF)
        for a in range(blocks):
            mixed_ref[a * bl + q * SUB : a * bl + (q + 1) * SUB, :] = mixed[a * SUB : (a + 1) * SUB, :]


def output_body(nb, ngroups, mixed_ref, proj_ref, *refs):
    _, place = position(ngroups)
    msgs, outs = refs[:nb], refs[nb:]
    t = LANE
    chunks = proj_ref.shape[1] // LANE
    for d in range(nb):
        at = rows((place ^ d) * t, t)
        x = unpack(msgs[d], t, chunks).astype(F32)
        outs[d][...] = (x + proj_ref[at, :].astype(F32) * mixed_ref[at, :].astype(F32)).astype(BF)


def backward_body(nb, ngroups, bl, *refs):
    group, _ = position(ngroups)
    adjs, rest = refs[:ngroups], refs[ngroups:]
    mixed_ref, mq_ref, bd_ref, grad_ref, adj_proj_ref, a_ref, adj_first_ref = rest
    t = LANE
    gather_positions(group, bl, adjs, a_ref)
    blocks = adjs[0].shape[0] // bl
    own = rows(group * blocks * SUB, blocks * SUB)
    for q in range(bl // SUB):
        adj_first = mm(mq_ref[q, :, own], a_ref[q], 0, 0).astype(BF)
        for a in range(blocks):
            at = slice(a * bl + q * SUB, a * bl + (q + 1) * SUB)
            adj_first_ref[at, :] = adj_first[a * SUB : (a + 1) * SUB, :]
    for c in range(nb):
        at = slice(c * t, (c + 1) * t)
        grad = grad_ref[at, :].astype(F32)
        adj_first = adj_first_ref[at, :]
        mixed = mixed_ref[at, :].astype(F32)
        adj_proj_ref[at, :] = (grad * mixed + mm(bd_ref[c], adj_first, 0, 0)).astype(BF)


def factor_grads_body(nb, ngroups, bl, ext, f_ref, a_ref, adj_first_ref, proj_ref, left_ref, right_ref):
    group, _ = position(ngroups)
    na = LANE // bl
    t = LANE
    nq = f_ref.shape[0]
    n = SUB * ext
    upper = lax.broadcasted_iota(jnp.int32, (bl, LANE), 1) < bl
    for c in range(nb):
        at = slice(c * t, (c + 1) * t)
        both = mm(adj_first_ref[at, :], proj_ref[at, :], 1, 1)
        left_ref[c] = jnp.where(upper, both[:bl, :], both[bl:, :]).astype(BF)
    turn = expand_matrix(ext, nb, ngroups, na)
    same = same_position(n)
    order = jnp.where(
        natural(lax.broadcasted_iota(jnp.int32, (ext, ext), 0), nb, ngroups, na)
        == lax.broadcasted_iota(jnp.int32, (ext, ext), 1),
        1.0,
        0.0,
    ).astype(BF)
    per = right_ref.shape[0] // nq
    for q in range(nq):
        pairs = jnp.where(same, mm(a_ref[q], f_ref[q], 1, 1), 0.0)
        summed = jnp.sum(pairs.reshape(ext, SUB, n), axis=1).astype(BF)
        turned = mm(order, mm(summed, turn, 1, 1).astype(BF), 0, 0).astype(BF)
        for i in range(per):
            right_ref[q * per + i] = turned[:, i * LANE : (i + 1) * LANE]


def adj_norm_body(nb, ngroups, normin_ref, adj_proj_ref, wk_ref, gain_ref, *refs):
    _, place = position(ngroups)
    gain_part_ref, outs, adj_norm_ref = refs[0], refs[1 : 1 + nb], refs[1 + nb]
    bd = wk_ref.shape[0]
    t = LANE
    adj_norm = mm(adj_proj_ref[...], wk_ref[...], 1, 1)
    adj_norm_ref[...] = adj_norm
    gain = gain_ref[:, pl.ds(pl.multiple_of(place * bd, LANE), bd)]
    gain_part_ref[...] = jnp.sum(adj_norm * normin_ref[...].astype(F32), axis=0, keepdims=True) / gain
    for d in range(nb):
        outs[d][...] = adj_norm_ref[rows((place ^ d) * t, t), :].astype(BF)


def weight_grad_body(nb, ngroups, normin_ref, adj_proj_ref, gain_part_ref, own_ref, *refs):
    group, _ = position(ngroups)
    sends, gw_ref = refs[: ngroups - 1], refs[ngroups - 1]
    share, bd = own_ref.shape
    r = share // nb
    gw_ref[...] = mm(normin_ref[...], adj_proj_ref[...], 0, 0)
    tile = jnp.concatenate(
        list(split3(gain_part_ref[...])) + [jnp.zeros((SUB - 3, bd), F32)], axis=0
    ).astype(BF)
    for c in range(nb):
        at = slice(c * r, (c + 1) * r)
        own_ref[at, :] = gw_ref[rows((c * ngroups + group) * r, r), :]
        for e in range(1, ngroups):
            sends[e - 1][at, :] = gw_ref[rows((c * ngroups + (group ^ e)) * r, r), :].astype(BF)
    for e in range(1, ngroups):
        sends[e - 1][share:, :] = tile


def weight_sum_body(nb, ngroups, own_ref, gain_part_ref, left_ref, right_ref, *refs):
    group, place = position(ngroups)
    recvs = refs[: ngroups - 1]
    outs = refs[ngroups - 1 : ngroups - 1 + nb]
    total_ref, gains_ref = refs[ngroups - 1 + nb :]
    share, bd = own_ref.shape
    chunks = bd // LANE
    bl, ext = left_ref.shape[1], right_ref.shape[1]
    r = share // nb
    total = own_ref[...]
    gains_ref[group] = gain_part_ref[...]
    for e in range(1, ngroups):
        total = total + recvs[e - 1][:share, :].astype(F32)
        three = recvs[e - 1][share:, :].astype(F32)
        gains_ref[group ^ e] = three[0:1] + three[1:2] + three[2:3]
    total_ref[...] = total.astype(BF)
    gain = gains_ref[0]
    for g in range(1, ngroups):
        gain = gain + gains_ref[g]
    three = split3(gain)
    parts = [p[:, ch * LANE : (ch + 1) * LANE] for p in three for ch in range(chunks)]
    tile = jnp.concatenate(parts + [jnp.zeros((SUB - len(parts), LANE), F32)], axis=0).astype(BF)
    for d in range(nb):
        to = place ^ d
        for ch in range(chunks):
            outs[d][ch * r : (ch + 1) * r, :] = total_ref[rows(to * r, r), ch * LANE : (ch + 1) * LANE]
        at = chunks * r
        outs[d][at : at + bl, :] = left_ref[to]
        outs[d][at + bl : at + bl + ext, :] = right_ref[to * ngroups + group]
        outs[d][at + bl + ext :, :] = tile


def input_grad_body(nb, ngroups, x_ref, grad_ref, gain_ref, *refs):
    _, place = position(ngroups)
    parts, out, adj_ref = refs[:nb], refs[nb], refs[nb + 1]
    bd = parts[0].shape[1]
    for d in range(nb):
        adj_ref[:, pl.ds(pl.multiple_of((place ^ d) * bd, LANE), bd)] = parts[d][...].astype(F32)
    x = x_ref[...].astype(F32)
    inv = lax.rsqrt(jnp.mean(x * x, axis=-1, keepdims=True) + EPS)
    normed = x * inv
    scaled = adj_ref[...] * gain_ref[...]
    mean = jnp.mean(scaled * normed, axis=-1, keepdims=True)
    out[...] = (grad_ref[...].astype(F32) + inv * (scaled - normed * mean)).astype(BF)


def join_body(nb, ngroups, *refs):
    _, block = position(ngroups)
    out = refs[nb]
    bd = refs[0].shape[1]
    for d in range(nb):
        out[:, pl.ds(pl.multiple_of((block ^ d) * bd, LANE), bd)] = refs[d][...]


def join_weight_body(nb, ngroups, *refs):
    _, block = position(ngroups)
    gw_ref, gain_ref, left_out, right_out, by_block = refs[nb:]
    r, _, bd = gw_ref.shape
    chunks = bd // LANE
    na, bl, _ = left_out.shape
    npos, ext, _ = right_out.shape
    at = chunks * r
    left = refs[0][at : at + bl, :].astype(F32)
    right = refs[0][at + bl : at + bl + ext, :].astype(F32)
    for d in range(1, nb):
        left = left + refs[d][at : at + bl, :].astype(F32)
        right = right + refs[d][at + bl : at + bl + ext, :].astype(F32)
    for j in range(na):
        left_out[j] = left[:, j * bl : (j + 1) * bl]
    for j in range(npos):
        right_out[j] = right[:, j * ext : (j + 1) * ext]
    for d in range(nb):
        k = block ^ d
        by_block[k] = unpack(refs[d], r, chunks).astype(F32)
        tile = refs[d][at + bl + ext :, :].astype(F32)
        for ch in range(chunks):
            gain_ref[:, pl.ds(pl.multiple_of(k * bd + ch * LANE, LANE), LANE)] = (
                tile[ch : ch + 1] + tile[chunks + ch : chunks + ch + 1] + tile[2 * chunks + ch : 2 * chunks + ch + 1]
            )
    for k in range(nb):
        gw_ref[:, k, :] = by_block[k]


def shards(act_in, saved_in, grad_in, gain, weight, left_blocks, right_blocks):
    nseq = lax.axis_size("seq")
    npipe = lax.axis_size("pipe")
    _, t, width = act_in.shape
    _, r, nb, bd = weight.shape
    ngroups = nseq // nb
    bl = left_blocks.shape[2]
    ext = right_blocks.shape[2]
    npos = right_blocks.shape[1]
    chunks = bd // LANE
    tg = nb * t
    r4 = chunks * r
    nq = bl // SUB
    n = SUB * ext

    def within(parts):
        return [parts[0]] + [
            lax.ppermute(parts[d], "seq", [(s, s ^ (d * ngroups)) for s in range(nseq)]) for d in range(1, nb)
        ]

    def across(block, e):
        return lax.ppermute(block, "seq", [(s, s ^ e) for s in range(nseq)])

    def gathered(block):
        return [block] + [across(block, e) for e in range(1, ngroups)]

    def handed(parts, step):
        return [
            lax.ppermute(
                parts[d],
                ("pipe", "seq"),
                [
                    (p * nseq + s, ((p + step) % npipe) * nseq + (s ^ (d * ngroups)))
                    for p in range(npipe)
                    for s in range(nseq)
                ],
            )
            for d in range(nb)
        ]

    part = functools.partial
    def run(name, body, outs, scratch=()):
        return call(body, outs, scratch, name=name)

    pack = part(pack_tokens_body, nb, ngroups)
    norm = part(norm_body, nb, ngroups)
    mix = part(mix_body, ngroups, bl)
    join = part(join_body, nb, ngroups)
    scaled_msgs, plain_msgs = [sds((chunks * t + SUB, LANE))] * nb, [sds((chunks * t, LANE))] * nb
    tokens = [sds((tg, bd))]
    pieces = [sds((t, bd))] * nb
    wide = [sds((nq, n, bd))]
    share = bd // ngroups

    w_msgs = run("pack_weight", part(pack_weight_body, nb, ngroups), [sds((r4 + bl + ext, LANE))] * nb)(
        jnp.transpose(weight[0], (1, 0, 2)), left_blocks[0], right_blocks[0]
    )
    sto_msgs = run("pack_saved", part(pack, True), scaled_msgs)(saved_in[0], after=w_msgs[:1])
    grad_msgs = run("pack_grad", part(pack, False), plain_msgs)(grad_in[0], after=sto_msgs[:1])
    w_msgs, sto_msgs, grad_msgs = within(w_msgs), within(sto_msgs), within(grad_msgs)
    (relay,) = run("relay", part(relay_body, nb, ngroups, r4, ext), [sds((nb * (r4 + ext), LANE))])(
        *w_msgs, after=grad_msgs[:1]
    )
    relays = gathered(relay)
    (sto_normin,) = run("norm_saved", norm, tokens)(*sto_msgs, gain)
    wk, mq, bd_left = run(
        "assemble",
        part(assemble_body, nb, ngroups, r, ext, bl),
        [sds((bd, bd)), sds((nq, n, n)), sds((nb, LANE, LANE))],
        [pltpu.VMEM((nseq, ext, LANE), BF)],
    )(*w_msgs, *relays, after=[sto_normin])
    sto_proj, sto_first = run("project_saved", project_body, tokens * 2)(sto_normin, wk, bd_left)
    sto_firsts = gathered(sto_first)
    cur_msgs = run("pack_act", part(pack, True), scaled_msgs)(act_in[0], after=[sto_first])
    adj_mix, grad = run("adjoint", part(adjoint_body, nb, ngroups), tokens * 2)(
        *grad_msgs, sto_proj, after=cur_msgs[:1]
    )
    cur_msgs = within(cur_msgs)
    adj_mixes = gathered(adj_mix)
    sto_f, sto_mixed = run("mix_saved", mix, wide + tokens)(*sto_firsts, mq, after=[adj_mix])
    (cur_normin,) = run("norm_act", norm, tokens)(*cur_msgs, gain, after=[sto_mixed])
    cur_proj, cur_first = run("project_act", project_body, tokens * 2)(cur_normin, wk, bd_left)
    cur_firsts = gathered(cur_first)
    adj_proj, adj_f, adj_first = run(
        "backward", part(backward_body, nb, ngroups, bl), tokens + wide + tokens
    )(*adj_mixes, sto_mixed, mq, bd_left, grad, after=[cur_first])
    gain_part, *adj_parts = run(
        "adj_norm",
        part(adj_norm_body, nb, ngroups),
        [sds((1, bd), F32)] + pieces,
        [pltpu.VMEM((tg, bd), F32)],
    )(sto_normin, adj_proj, wk, gain)
    adj_parts = within(adj_parts)
    own_gw, *sends = run(
        "weight_grad",
        part(weight_grad_body, nb, ngroups),
        [sds((share, bd), F32)] + [sds((share + SUB, bd))] * (ngroups - 1),
        [pltpu.VMEM((bd, bd), F32)],
    )(sto_normin, adj_proj, gain_part)
    recvs = [across(sends[e - 1], e) for e in range(1, ngroups)]
    left_tiles, right_tiles = run(
        "factor_grads",
        part(factor_grads_body, nb, ngroups, bl, ext),
        [sds((nb, bl, LANE)), sds((nseq, ext, LANE))],
    )(sto_f, adj_f, adj_first, sto_proj, after=[own_gw])
    _, cur_mixed = run("mix_act", mix, wide + tokens)(*cur_firsts, mq, after=[left_tiles])
    out_parts = run("output", part(output_body, nb, ngroups), pieces)(cur_mixed, cur_proj, *cur_msgs)
    gw_parts = run(
        "weight_sum",
        part(weight_sum_body, nb, ngroups),
        [sds((r4 + bl + ext + SUB, LANE))] * nb,
        [pltpu.VMEM((share, bd), BF), pltpu.VMEM((ngroups, 1, bd), F32)],
    )(own_gw, gain_part, left_tiles, right_tiles, *recvs, after=out_parts[:1])
    (adj_x,) = run(
        "input_grad", part(input_grad_body, nb, ngroups), [sds((t, width))], [pltpu.VMEM((t, width), F32)]
    )(saved_in[0], grad_in[0], gain, *adj_parts, after=gw_parts[:1])
    out_parts, gw_parts = handed(out_parts, 1), within(gw_parts)
    grad_handed = lax.ppermute(adj_x, "pipe", [(p, (p - 1) % npipe) for p in range(npipe)])
    (handed_on,) = run("join_out", join, [sds((t, width))])(*out_parts, after=[adj_x])
    weight_grad, gain_grad, left_grad, right_grad = run(
        "join_weight",
        part(join_weight_body, nb, ngroups),
        [
            sds((r, nb, bd), F32),
            sds((1, width), F32),
            sds((left_blocks.shape[1], bl, bl), F32),
            sds((npos, ext, ext), F32),
        ],
        [pltpu.VMEM((nb, r, bd), F32)],
    )(*gw_parts, after=[handed_on])
    return (
        handed_on[None],
        grad_handed[None],
        weight_grad[None],
        gain_grad,
        left_grad[None],
        right_grad[None],
    )


def solution(mesh):
    tokens = P("pipe", "seq", None)
    factor = P("pipe", "seq", None, None)
    return jax.shard_map(
        shards,
        mesh=mesh,
        in_specs=(tokens, tokens, tokens, P("pipe", None), factor, factor, factor),
        out_specs=(tokens, tokens, factor, P("pipe", None), factor, factor),
        check_vma=False,
    )
```

```python
import functools

import jax
import jax.numpy as jnp
from jax import lax
from jax.experimental import pallas as pl
from jax.experimental.pallas import tpu as pltpu
from jax.sharding import PartitionSpec as P

BF = jnp.bfloat16
F32 = jnp.float32
LANE = 128
SUB = 16
EPS = 1e-06
COST = {"norm_act": 3.0, "norm_saved": 6.0, "mix_act": 1.0, "take_grad": 8.0, "join_out": 2.0}
VMEM = 48 * 1024 * 1024


def position(ngroups):
    me = lax.axis_index("seq")
    return me % ngroups, me // ngroups


def far(d, nb):
    return (nb - d) % nb


def natural(pos, nb, ngroups, na):
    return ((pos // na % nb) * ngroups + pos // (nb * na)) * na + pos % na


def split3(x):
    hi = x.astype(BF).astype(F32)
    mid = (x - hi).astype(BF).astype(F32)
    return hi, mid, x - hi - mid


def eye(n):
    return lax.broadcasted_iota(jnp.int32, (n, n), 0) == lax.broadcasted_iota(jnp.int32, (n, n), 1)


def to_row(col):
    return jnp.sum(jnp.where(eye(col.shape[0]), col, 0.0), axis=0, keepdims=True)


def to_col(row):
    return jnp.sum(jnp.where(eye(row.shape[1]), row, 0.0), axis=1, keepdims=True)


def mm(a, b, ca=1, cb=0):
    return lax.dot_general(a, b, (((ca,), (cb,)), ((), ())), preferred_element_type=F32)


def rows(start, size):
    return pl.ds(pl.multiple_of(start, size), size)


def call(body, outs, scratch, direct, name):
    def run(*args, after=()):
        nin, nwait = len(args), len(after)
        vmem, anywhere = pl.BlockSpec(memory_space=pltpu.VMEM), pl.BlockSpec(memory_space=pl.ANY)

        def without_waits(*refs):
            return body(*refs[:nin], *refs[nin + nwait :])

        return pl.pallas_call(
            without_waits,
            out_shape=list(outs),
            in_specs=[anywhere] * direct + [vmem] * (nin - direct) + [anywhere] * nwait,
            out_specs=[anywhere] * direct + [vmem] * (len(outs) - direct),
            scratch_shapes=list(scratch),
            compiler_params=pltpu.CompilerParams(vmem_limit_bytes=VMEM),
            cost_estimate=pl.CostEstimate(
                flops=int(COST.get(name, 0.0) * 1e9), bytes_accessed=0, transcendentals=0
            ),
            name=name,
        )(*args, *after)

    return run


def sds(shape, dtype=BF):
    return jax.ShapeDtypeStruct(shape, dtype)


def pack_weight_body(nb, ngroups, w_ref, l_ref, r_ref, *outs):
    _, block = position(ngroups)
    r, bd = w_ref.shape[1], w_ref.shape[2]
    chunks = bd // LANE
    bl, ext = l_ref.shape[1], r_ref.shape[1]
    left = jnp.concatenate([l_ref[j].astype(F32) for j in range(l_ref.shape[0])], axis=1).astype(BF)
    right = jnp.concatenate([r_ref[j].astype(F32) for j in range(r_ref.shape[0])], axis=1).astype(BF)
    for d in range(nb):
        for ch in range(chunks):
            outs[d][ch * r : (ch + 1) * r, :] = w_ref[block ^ far(d, nb), :, ch * LANE : (ch + 1) * LANE]
        outs[d][chunks * r : chunks * r + bl, :] = left
        outs[d][chunks * r + bl :, :] = right


def pack_tokens_body(nb, ngroups, with_scale, x_ref, *outs):
    _, block = position(ngroups)
    t, width = x_ref.shape
    bd = width // nb
    chunks = bd // LANE
    if with_scale:
        x = x_ref[...].astype(F32)
        inv = lax.rsqrt(jnp.mean(x * x, axis=-1, keepdims=True) + EPS)
        parts = split3(to_row(inv))
        tile = jnp.concatenate(list(parts) + [jnp.zeros((SUB - 3, t), F32)], axis=0).astype(BF)
    for d in range(nb):
        for ch in range(chunks):
            lanes = pl.ds(pl.multiple_of((block ^ far(d, nb)) * bd + ch * LANE, LANE), LANE)
            outs[d][ch * t : (ch + 1) * t, :] = x_ref[:, lanes]
        if with_scale:
            outs[d][chunks * t :, :] = tile


def pick(n, part_of, part):
    row = lax.broadcasted_iota(jnp.int32, (n, part_of), 0)
    col = lax.broadcasted_iota(jnp.int32, (n, part_of), 1)
    return jnp.where(row == part * part_of + col, 1.0, 0.0).astype(BF)


def split_features_body(nb, ngroups, x_ref, *outs):
    group, _ = position(ngroups)
    part_of = outs[0].shape[2]
    bd = x_ref.shape[1] // nb
    for e in range(ngroups):
        take = pick(bd, part_of, group ^ e)
        for k in range(nb):
            outs[e][k] = mm(x_ref[:, k * bd : (k + 1) * bd], take).astype(BF)


def pack_shares_body(nb, ngroups, *refs):
    group, place = position(ngroups)
    shares, outs = refs[:ngroups], refs[ngroups:]
    t = shares[0].shape[1]
    for d in range(nb):
        for e in range(ngroups):
            outs[d][rows((group ^ e) * t, t), :] = shares[e][place ^ far(d, nb)]


def relay_body(nb, ngroups, r4, ext, *refs):
    _, place = position(ngroups)
    out = refs[nb]
    bl = refs[0].shape[0] - r4 - ext
    for d in range(nb):
        to = place ^ far(d, nb)
        out[rows(to * r4, r4), :] = refs[d][:r4, :]
        out[pl.ds(pl.multiple_of(nb * r4 + to * ext, ext), ext), :] = refs[d][r4 + bl :, :]
        out[pl.ds(pl.multiple_of(nb * (r4 + ext) + to * bl, bl), bl), :] = refs[d][r4 : r4 + bl, :]


def expand_matrix(ext, nb, ngroups, na):
    n = SUB * ext
    row = lax.broadcasted_iota(jnp.int32, (n, n), 0)
    col = lax.broadcasted_iota(jnp.int32, (n, n), 1)
    return jnp.where((row // ext == col % SUB) & (row % ext == natural(col // SUB, nb, ngroups, na)), 1.0, 0.0).astype(BF)


def same_position(n):
    row = lax.broadcasted_iota(jnp.int32, (n, n), 0)
    col = lax.broadcasted_iota(jnp.int32, (n, n), 1)
    return row % SUB == col % SUB


def assemble_body(nb, ngroups, r, ext, bl, *refs):
    group, _ = position(ngroups)
    na = LANE // bl
    relays = refs[:ngroups]
    wk_ref, mq_ref, bd_ref, all_ref = refs[ngroups:]
    chunks = wk_ref.shape[1] // LANE
    r4 = chunks * r
    for e in range(ngroups):
        g = group ^ e
        for c in range(nb):
            for ch in range(chunks):
                wk_ref[rows((c * ngroups + g) * r, r), ch * LANE : (ch + 1) * LANE] = relays[e][
                    c * r4 + ch * r : c * r4 + (ch + 1) * r, :
                ]
            all_ref[c * ngroups + g] = relays[e][nb * r4 + c * ext : nb * r4 + (c + 1) * ext, :]
    nq = mq_ref.shape[0]
    per = nb * ngroups // nq
    n = SUB * ext
    turn = expand_matrix(ext, nb, ngroups, na)
    spread = jnp.where(
        natural(lax.broadcasted_iota(jnp.int32, (n, ext), 0) // SUB, nb, ngroups, na)
        == lax.broadcasted_iota(jnp.int32, (n, ext), 1),
        1.0,
        0.0,
    ).astype(BF)
    same = same_position(n)
    for q in range(nq):
        tiles = jnp.concatenate([all_ref[q * per + i] for i in range(per)], axis=1)
        wide = mm(tiles, turn).astype(BF)
        mq_ref[q] = jnp.where(same, mm(spread, wide), 0.0).astype(BF)
    half_row = lax.broadcasted_iota(jnp.int32, (LANE, LANE), 0) // bl
    half_col = lax.broadcasted_iota(jnp.int32, (LANE, LANE), 1) // bl
    for e in range(ngroups):
        for c in range(nb):
            at = nb * (r4 + ext) + c * bl
            both = jnp.concatenate([relays[e][at : at + bl, :].astype(F32)] * na, axis=0)
            bd_ref[(group ^ e) * nb + c] = jnp.where(half_row == half_col, both, 0.0).astype(BF)


def unpack(msg, t, chunks):
    return jnp.concatenate([msg[ch * t : (ch + 1) * t, :] for ch in range(chunks)], axis=1)


def scale_of(msg, t, chunks):
    tile = msg[chunks * t : chunks * t + SUB, :].astype(F32)
    return to_col(tile[0:1] + tile[1:2] + tile[2:3])


def norm_body(nb, ngroups, *refs):
    _, place = position(ngroups)
    msgs = refs[:nb]
    gain_ref, normin_ref = refs[nb:]
    t = LANE
    bd = normin_ref.shape[1]
    chunks = bd // LANE
    gain = gain_ref[:, pl.ds(pl.multiple_of(place * bd, LANE), bd)]
    for d in range(nb):
        x = unpack(msgs[d], t, chunks).astype(F32)
        normed = x * scale_of(msgs[d], t, chunks)
        normin_ref[rows((place ^ far(d, nb)) * t, t), :] = (normed * gain).astype(BF)


def project_body(nb, ngroups, normin_ref, wk_ref, bd_ref, proj_ref, first_ref):
    group, _ = position(ngroups)
    t = LANE
    proj_ref[...] = mm(normin_ref[...], wk_ref[...]).astype(BF)
    for c in range(nb):
        at = slice(c * t, (c + 1) * t)
        first_ref[at, :] = mm(bd_ref[group * nb + c], proj_ref[at, :]).astype(BF)


def project_shares_body(ngroups, normin_ref, wk_ref, *outs):
    group, _ = position(ngroups)
    bd = wk_ref.shape[0]
    proj = mm(normin_ref[...], wk_ref[...]).astype(BF)
    for e in range(ngroups):
        outs[e][...] = mm(proj, pick(bd, bd // ngroups, group ^ e)).astype(BF)


def gather_positions(group, bl, parts, out_ref):
    blocks = parts[0].shape[0] // bl
    for e, part in enumerate(parts):
        base = (group ^ e) * blocks * SUB
        for q in range(bl // SUB):
            for a in range(blocks):
                out_ref[q, pl.ds(pl.multiple_of(base + a * SUB, SUB), SUB), :] = part[
                    a * bl + q * SUB : a * bl + (q + 1) * SUB, :
                ]


def mix_body(ngroups, bl, *refs):
    group, _ = position(ngroups)
    firsts = refs[:ngroups]
    mq_ref, mixed_ref, f_ref = refs[ngroups:]
    gather_positions(group, bl, firsts, f_ref)
    blocks = firsts[0].shape[0] // bl
    own = rows(group * blocks * SUB, blocks * SUB)
    for q in range(bl // SUB):
        mixed = mm(mq_ref[q, own, :], f_ref[q]).astype(BF)
        for a in range(blocks):
            mixed_ref[a * bl + q * SUB : a * bl + (q + 1) * SUB, :] = mixed[a * SUB : (a + 1) * SUB, :]


def output_body(nb, ngroups, mixed_ref, proj_ref, *refs):
    _, place = position(ngroups)
    msgs, outs = refs[:nb], refs[nb:]
    t = LANE
    chunks = proj_ref.shape[1] // LANE
    for d in range(nb):
        at = rows((place ^ far(d, nb)) * t, t)
        x = unpack(msgs[d], t, chunks).astype(F32)
        outs[d][...] = (x + proj_ref[at, :].astype(F32) * mixed_ref[at, :].astype(F32)).astype(BF)


def to_positions(x_ref, out_ref, bl):
    for q in range(bl // SUB):
        for a in range(x_ref.shape[0] // bl):
            out_ref[q, a * SUB : (a + 1) * SUB, :] = x_ref[a * bl + q * SUB : a * bl + (q + 1) * SUB, :]


def from_positions(x, q, out_ref, bl):
    for a in range(out_ref.shape[0] // bl):
        out_ref[a * bl + q * SUB : a * bl + (q + 1) * SUB, :] = x[a * SUB : (a + 1) * SUB, :]


def mix_shares_body(ngroups, bl, *refs):
    group, _ = position(ngroups)
    parts = refs[:ngroups]
    mq_ref, bd_ref, proj_ref, f_ref, mixed_ref, first_ref = refs[ngroups:]
    t = LANE
    tg = parts[0].shape[0]
    for e in range(ngroups):
        proj_ref[rows((group ^ e) * tg, tg), :] = parts[e][...]
    for c in range(bd_ref.shape[0]):
        at = slice(c * t, (c + 1) * t)
        first_ref[at, :] = mm(bd_ref[c], proj_ref[at, :]).astype(BF)
    to_positions(first_ref, f_ref, bl)
    for q in range(bl // SUB):
        from_positions(mm(mq_ref[q], f_ref[q]).astype(BF), q, mixed_ref, bl)


def take_grad_body(nb, ngroups, *refs):
    _, place = position(ngroups)
    grad_ref = refs[nb]
    t = LANE
    for d in range(nb):
        for g in range(ngroups):
            grad_ref[rows((g * nb + (place ^ far(d, nb))) * t, t), :] = refs[d][g * t : (g + 1) * t, :]


def backward_body(nb, ngroups, bl, *refs):
    group, _ = position(ngroups)
    grad_ref, proj_ref, mixed_ref, mq_ref, bd_ref = refs[:5]
    outs = refs[5 : 5 + ngroups]
    a_ref, adj_first_ref, adj_ref = refs[5 + ngroups :]
    t = LANE
    adj_ref[...] = (grad_ref[...].astype(F32) * proj_ref[...].astype(F32)).astype(BF)
    to_positions(adj_ref, a_ref, bl)
    for q in range(bl // SUB):
        from_positions(mm(mq_ref[q], a_ref[q], 0, 0).astype(BF), q, adj_first_ref, bl)
    for c in range(bd_ref.shape[0]):
        at = slice(c * t, (c + 1) * t)
        grad = grad_ref[at, :].astype(F32)
        mixed = mixed_ref[at, :].astype(F32)
        adj_ref[at, :] = (grad * mixed + mm(bd_ref[c], adj_first_ref[at, :], 0, 0)).astype(BF)
    tg = nb * t
    for e in range(ngroups):
        outs[e][...] = adj_ref[rows((group ^ e) * tg, tg), :]


def factor_grads_body(nb, ngroups, bl, ext, f_ref, a_ref, adj_first_ref, proj_ref, *refs):
    group, _ = position(ngroups)
    outs, right_ref, left_ref = refs[:ngroups], refs[ngroups], refs[ngroups + 1]
    na = LANE // bl
    t = LANE
    nq = f_ref.shape[0]
    n = SUB * ext
    upper = lax.broadcasted_iota(jnp.int32, (bl, LANE), 1) < bl
    for g in range(ngroups):
        for c in range(nb):
            at = slice((g * nb + c) * t, (g * nb + c + 1) * t)
            both = mm(adj_first_ref[at, :], proj_ref[at, :], 1, 1)
            left_ref[g, c * bl : (c + 1) * bl, :] = jnp.where(upper, both[:bl, :], both[bl:, :]).astype(BF)
    turn = expand_matrix(ext, nb, ngroups, na)
    same = same_position(n)
    order = jnp.where(
        natural(lax.broadcasted_iota(jnp.int32, (ext, ext), 0), nb, ngroups, na)
        == lax.broadcasted_iota(jnp.int32, (ext, ext), 1),
        1.0,
        0.0,
    ).astype(BF)
    per = nb * ngroups // nq
    for q in range(nq):
        pairs = jnp.where(same, mm(a_ref[q], f_ref[q], 1, 1), 0.0)
        summed = jnp.sum(pairs.reshape(ext, SUB, n), axis=1).astype(BF)
        turned = mm(order, mm(summed, turn, 1, 1).astype(BF), 0, 0).astype(BF)
        for i in range(per):
            s = q * per + i
            right_ref[s % ngroups, (s // ngroups) * ext : (s // ngroups + 1) * ext, :] = turned[
                :, i * LANE : (i + 1) * LANE
            ]
    for e in range(ngroups):
        outs[e][: nb * bl, :] = left_ref[group ^ e]
        outs[e][nb * bl :, :] = right_ref[group ^ e]


def adj_norm_body(nb, ngroups, normin_ref, wk_ref, gain_ref, *refs):
    group, place = position(ngroups)
    shares, rest = refs[:ngroups], refs[ngroups:]
    adj_proj_ref, gain_part_ref, outs, adj_norm_ref = rest[0], rest[1], rest[2 : 2 + nb], rest[2 + nb]
    bd = wk_ref.shape[0]
    t = LANE
    adj_proj = jnp.zeros(adj_proj_ref.shape, F32)
    for e in range(ngroups):
        adj_proj = adj_proj + mm(shares[e][...], pick(bd, bd // ngroups, group ^ e), 1, 1)
    adj_proj_ref[...] = adj_proj.astype(BF)
    adj_norm = mm(adj_proj_ref[...], wk_ref[...], 1, 1)
    adj_norm_ref[...] = adj_norm
    gain = gain_ref[:, pl.ds(pl.multiple_of(place * bd, LANE), bd)]
    gain_part_ref[...] = jnp.sum(adj_norm * normin_ref[...].astype(F32), axis=0, keepdims=True) / gain
    for d in range(nb):
        outs[d][...] = adj_norm_ref[rows((place ^ far(d, nb)) * t, t), :].astype(BF)


def weight_grad_body(nb, ngroups, normin_ref, adj_proj_ref, gain_part_ref, own_ref, *refs):
    group, _ = position(ngroups)
    sends, gw_ref = refs[: ngroups - 1], refs[ngroups - 1]
    share, bd = own_ref.shape
    r = share // nb
    gw_ref[...] = mm(normin_ref[...], adj_proj_ref[...], 0, 0)
    tile = jnp.concatenate(
        list(split3(gain_part_ref[...])) + [jnp.zeros((SUB - 3, bd), F32)], axis=0
    ).astype(BF)
    for c in range(nb):
        at = slice(c * r, (c + 1) * r)
        own_ref[at, :] = gw_ref[rows((c * ngroups + group) * r, r), :]
        for e in range(1, ngroups):
            sends[e - 1][at, :] = gw_ref[rows((c * ngroups + (group ^ e)) * r, r), :].astype(BF)
    for e in range(1, ngroups):
        sends[e - 1][share:, :] = tile


def sum_tiles_body(*refs):
    total = refs[0][...].astype(F32)
    for ref in refs[1:-1]:
        total = total + ref[...].astype(F32)
    refs[-1][...] = total.astype(BF)


def weight_sum_body(nb, ngroups, bl, ext, own_ref, gain_part_ref, *refs):
    group, place = position(ngroups)
    recvs, tiles_ref = refs[: ngroups - 1], refs[ngroups - 1]
    outs = refs[ngroups : ngroups + nb]
    total_ref, gains_ref = refs[ngroups + nb :]
    share, bd = own_ref.shape
    chunks = bd // LANE
    r = share // nb
    total = own_ref[...]
    gains_ref[group] = gain_part_ref[...]
    for e in range(1, ngroups):
        total = total + recvs[e - 1][:share, :].astype(F32)
        three = recvs[e - 1][share:, :].astype(F32)
        gains_ref[group ^ e] = three[0:1] + three[1:2] + three[2:3]
    total_ref[...] = total.astype(BF)
    gain = gains_ref[0]
    for g in range(1, ngroups):
        gain = gain + gains_ref[g]
    three = split3(gain)
    parts = [p[:, ch * LANE : (ch + 1) * LANE] for p in three for ch in range(chunks)]
    tile = jnp.concatenate(parts + [jnp.zeros((SUB - len(parts), LANE), F32)], axis=0).astype(BF)
    for d in range(nb):
        to = place ^ far(d, nb)
        for ch in range(chunks):
            outs[d][ch * r : (ch + 1) * r, :] = total_ref[rows(to * r, r), ch * LANE : (ch + 1) * LANE]
        at = chunks * r
        outs[d][at : at + bl, :] = tiles_ref[rows(to * bl, bl), :]
        outs[d][at + bl : at + bl + ext, :] = tiles_ref[
            pl.ds(pl.multiple_of(nb * bl + to * ext, ext), ext), :
        ]
        outs[d][at + bl + ext :, :] = tile


def input_grad_body(nb, ngroups, x_ref, grad_ref, gain_ref, *refs):
    _, place = position(ngroups)
    parts, out, adj_ref = refs[:nb], refs[nb], refs[nb + 1]
    bd = parts[0].shape[1]
    for d in range(nb):
        adj_ref[:, pl.ds(pl.multiple_of((place ^ far(d, nb)) * bd, LANE), bd)] = parts[d][...].astype(F32)
    x = x_ref[...].astype(F32)
    inv = lax.rsqrt(jnp.mean(x * x, axis=-1, keepdims=True) + EPS)
    normed = x * inv
    scaled = adj_ref[...] * gain_ref[...]
    mean = jnp.mean(scaled * normed, axis=-1, keepdims=True)
    out[...] = (grad_ref[...].astype(F32) + inv * (scaled - normed * mean)).astype(BF)


def join_body(nb, ngroups, *refs):
    _, block = position(ngroups)
    out = refs[nb]
    bd = refs[0].shape[1]
    for d in range(nb):
        out[:, pl.ds(pl.multiple_of((block ^ far(d, nb)) * bd, LANE), bd)] = refs[d][...]


def join_weight_body(nb, ngroups, *refs):
    _, block = position(ngroups)
    gw_ref, gain_ref, left_out, right_out, by_block = refs[nb:]
    r, _, bd = gw_ref.shape
    chunks = bd // LANE
    na, bl, _ = left_out.shape
    npos, ext, _ = right_out.shape
    at = chunks * r
    left = refs[0][at : at + bl, :].astype(F32)
    right = refs[0][at + bl : at + bl + ext, :].astype(F32)
    for d in range(1, nb):
        left = left + refs[d][at : at + bl, :].astype(F32)
        right = right + refs[d][at + bl : at + bl + ext, :].astype(F32)
    for j in range(na):
        left_out[j] = left[:, j * bl : (j + 1) * bl]
    for j in range(npos):
        right_out[j] = right[:, j * ext : (j + 1) * ext]
    for d in range(nb):
        k = block ^ far(d, nb)
        by_block[k] = unpack(refs[d], r, chunks).astype(F32)
        tile = refs[d][at + bl + ext :, :].astype(F32)
        for ch in range(chunks):
            gain_ref[:, pl.ds(pl.multiple_of(k * bd + ch * LANE, LANE), LANE)] = (
                tile[ch : ch + 1] + tile[chunks + ch : chunks + ch + 1] + tile[2 * chunks + ch : 2 * chunks + ch + 1]
            )
    for k in range(nb):
        gw_ref[:, k, :] = by_block[k]


def shards(act_in, saved_in, grad_in, gain, weight, left_blocks, right_blocks):
    nseq = lax.axis_size("seq")
    npipe = lax.axis_size("pipe")
    _, t, width = act_in.shape
    _, r, nb, bd = weight.shape
    ngroups = nseq // nb
    bl = left_blocks.shape[2]
    ext = right_blocks.shape[2]
    npos = right_blocks.shape[1]
    chunks = bd // LANE
    tg = nb * t
    r4 = chunks * r
    nq = bl // SUB
    n = SUB * ext

    def within(parts):
        return [parts[0]] + [
            lax.ppermute(parts[d], "seq", [(s, s ^ (far(d, nb) * ngroups)) for s in range(nseq)])
            for d in range(1, nb)
        ]

    def across(block, e):
        return lax.ppermute(block, "seq", [(s, s ^ e) for s in range(nseq)])

    def gathered(block):
        return [block] + [across(block, e) for e in range(1, ngroups)]

    def exchanged(parts):
        return list(parts[:1]) + [across(parts[e], e) for e in range(1, ngroups)]

    part = functools.partial
    def run(name, body, outs, scratch=(), direct=0):
        return call(body, outs, scratch, direct, name)

    pack = part(pack_tokens_body, nb, ngroups)
    norm = part(norm_body, nb, ngroups)
    join = part(join_body, nb, ngroups)
    scaled_msgs = [sds((chunks * t + SUB, LANE))] * nb
    tokens = [sds((tg, bd))]
    pieces = [sds((t, bd))] * nb
    rows_of = bd // ngroups
    part_of = bd // ngroups
    shares = [sds((tg, part_of))] * ngroups
    every = [sds((ngroups * tg, part_of))]
    by_position = [sds((nq, n, part_of))]

    def scratch(structs):
        return [pltpu.VMEM(s.shape, s.dtype) for s in structs]

    w_msgs = run("pack_weight", part(pack_weight_body, nb, ngroups), [sds((r4 + bl + ext, LANE))] * nb)(
        jnp.transpose(weight[0], (1, 0, 2)), left_blocks[0], right_blocks[0]
    )
    cur_msgs = run("pack_act", part(pack, True), scaled_msgs)(act_in[0], after=w_msgs[:1])
    grad_shares = run(
        "split_grad", part(split_features_body, nb, ngroups), [sds((nb, t, part_of))] * ngroups
    )(grad_in[0], after=cur_msgs[:1])
    sto_msgs = run("pack_saved", part(pack, True), scaled_msgs)(saved_in[0], after=grad_shares[:1])
    early = sto_msgs[:1]
    w_msgs, cur_msgs = within(w_msgs), within(cur_msgs)
    grad_shares = exchanged(grad_shares)
    sto_msgs = within(sto_msgs)
    (relay,) = run("relay", part(relay_body, nb, ngroups, r4, ext), [sds((nb * (r4 + ext + bl), LANE))])(
        *w_msgs, after=early
    )
    relays = gathered(relay)
    (cur_normin,) = run("norm_act", norm, tokens)(*cur_msgs, gain, after=[relay])
    wk, mq, bd_left = run(
        "assemble",
        part(assemble_body, nb, ngroups, r, ext, bl),
        [sds((bd, bd)), sds((nq, n, n)), sds((nseq, LANE, LANE))],
        [pltpu.VMEM((nseq, ext, LANE), BF)],
    )(*relays, after=[cur_normin])
    cur_proj, cur_first = run("project_act", part(project_body, nb, ngroups), tokens * 2)(
        cur_normin, wk, bd_left
    )
    cur_firsts = gathered(cur_first)
    grad_msgs = run("pack_grad", part(pack_shares_body, nb, ngroups), [sds((ngroups * t, part_of))] * nb)(
        *grad_shares, after=[cur_first]
    )
    grad_msgs = within(grad_msgs)
    (sto_normin,) = run("norm_saved", norm, tokens)(*sto_msgs, gain, after=grad_msgs[:1])
    sto_shares = run("project_saved", part(project_shares_body, ngroups), shares)(sto_normin, wk)
    sto_wait = sto_shares[:1]
    sto_shares = exchanged(sto_shares)
    (cur_mixed,) = run(
        "mix_act", part(mix_body, ngroups, bl), tokens, scratch([sds((nq, n, bd))])
    )(*cur_firsts, mq, after=sto_wait)
    out_parts = run("output", part(output_body, nb, ngroups), pieces)(cur_mixed, cur_proj, *cur_msgs)
    (grad,) = run("take_grad", part(take_grad_body, nb, ngroups), every)(*grad_msgs, after=out_parts[:1])
    sto_proj, sto_f, sto_mixed = run(
        "mix_saved", part(mix_shares_body, ngroups, bl), every + by_position + every, scratch(every)
    )(*sto_shares, mq, bd_left, after=[grad])
    out_parts = within(out_parts)
    *adj_shares, adj_f, adj_first = run(
        "backward", part(backward_body, nb, ngroups, bl), shares + by_position + every, scratch(every)
    )(grad, sto_proj, sto_mixed, mq, bd_left)
    adj_wait = adj_shares[:1]
    adj_shares = exchanged(adj_shares)
    tiles = run(
        "factor_grads",
        part(factor_grads_body, nb, ngroups, bl, ext),
        [sds((nb * (bl + ext), LANE))] * ngroups,
        scratch([sds((ngroups, nb * ext, LANE)), sds((ngroups, nb * bl, LANE))]),
    )(sto_f, adj_f, adj_first, sto_proj, after=adj_wait)
    tiles_wait = tiles[:1]
    tiles = exchanged(tiles)
    (out,) = run("join_out", join, [sds((t, width))])(*out_parts, after=tiles_wait)
    adj_proj, gain_part, *adj_parts = run(
        "adj_norm",
        part(adj_norm_body, nb, ngroups),
        tokens + [sds((1, bd), F32)] + pieces,
        scratch([sds((tg, bd), F32)]),
    )(sto_normin, wk, gain, *adj_shares, after=[out])
    adj_wait = adj_parts[:1]
    adj_parts = within(adj_parts)
    (tile_sum,) = run("sum_tiles", sum_tiles_body, [sds((nb * (bl + ext), LANE))])(*tiles, after=adj_wait)
    own_gw, *sends = run(
        "weight_grad",
        part(weight_grad_body, nb, ngroups),
        [sds((rows_of, bd), F32)] + [sds((rows_of + SUB, bd))] * (ngroups - 1),
        scratch([sds((bd, bd), F32)]),
    )(sto_normin, adj_proj, gain_part, after=[tile_sum])
    recvs = [across(sends[e - 1], e) for e in range(1, ngroups)]
    gw_parts = run(
        "weight_sum",
        part(weight_sum_body, nb, ngroups, bl, ext),
        [sds((r4 + bl + ext + SUB, LANE))] * nb,
        scratch([sds((rows_of, bd)), sds((ngroups, 1, bd), F32)]),
    )(own_gw, gain_part, *recvs, tile_sum)
    handed_on = lax.ppermute(out, "pipe", [(p, (p + 1) % npipe) for p in range(npipe)])
    (adj_x,) = run(
        "input_grad", part(input_grad_body, nb, ngroups), [sds((t, width))], scratch([sds((t, width), F32)])
    )(saved_in[0], grad_in[0], gain, *adj_parts, after=gw_parts[:1])
    gw_parts = within(gw_parts)
    grad_handed = lax.ppermute(adj_x, "pipe", [(p, (p - 1) % npipe) for p in range(npipe)])
    weight_grad, gain_grad, left_grad, right_grad = run(
        "join_weight",
        part(join_weight_body, nb, ngroups),
        [
            sds((r, nb, bd), F32),
            sds((1, width), F32),
            sds((left_blocks.shape[1], bl, bl), F32),
            sds((npos, ext, ext), F32),
        ],
        scratch([sds((nb, r, bd), F32)]),
    )(*gw_parts, after=[adj_x])
    return (
        handed_on[None],
        grad_handed[None],
        weight_grad[None],
        gain_grad,
        left_grad[None],
        right_grad[None],
    )


def solution(mesh):
    tokens = P("pipe", "seq", None)
    factor = P("pipe", "seq", None, None)
    return jax.shard_map(
        shards,
        mesh=mesh,
        in_specs=(tokens, tokens, tokens, P("pipe", None), factor, factor, factor),
        out_specs=(tokens, tokens, factor, P("pipe", None), factor, factor),
        check_vma=False,
    )
```

```python
import functools

import jax
import jax.numpy as jnp
from jax import lax
from jax.experimental import pallas as pl
from jax.experimental.pallas import tpu as pltpu
from jax.sharding import PartitionSpec as P

BF = jnp.bfloat16
F32 = jnp.float32
LANE = 128
SUB = 16
EPS = 1e-06
COST = {"relay": 3, "norm_saved": 3.0, "take_grad": 6.0, "far_act": 3, "norm_act": 2, "weight_sum": 2, "join_weight": 5.9}
VMEM = 48 * 1024 * 1024


def position(ngroups):
    me = lax.axis_index("seq")
    return me % ngroups, me // ngroups


def far(d, nb):
    return (nb - d) % nb


def natural(pos, nb, ngroups, na):
    return ((pos // na % nb) * ngroups + pos // (nb * na)) * na + pos % na


def split3(x):
    hi = x.astype(BF).astype(F32)
    mid = (x - hi).astype(BF).astype(F32)
    return hi, mid, x - hi - mid


def eye(n):
    return lax.broadcasted_iota(jnp.int32, (n, n), 0) == lax.broadcasted_iota(jnp.int32, (n, n), 1)


def to_row(col):
    return jnp.sum(jnp.where(eye(col.shape[0]), col, 0.0), axis=0, keepdims=True)


def to_col(row):
    return jnp.sum(jnp.where(eye(row.shape[1]), row, 0.0), axis=1, keepdims=True)


def mm(a, b, ca=1, cb=0):
    return lax.dot_general(a, b, (((ca,), (cb,)), ((), ())), preferred_element_type=F32)


def rows(start, size):
    return pl.ds(pl.multiple_of(start, size), size)


def call(body, outs, scratch, direct, name):
    def run(*args, after=()):
        nin, nwait = len(args), len(after)
        vmem, anywhere = pl.BlockSpec(memory_space=pltpu.VMEM), pl.BlockSpec(memory_space=pl.ANY)

        def without_waits(*refs):
            return body(*refs[:nin], *refs[nin + nwait :])

        return pl.pallas_call(
            without_waits,
            out_shape=list(outs),
            in_specs=[anywhere] * direct + [vmem] * (nin - direct) + [anywhere] * nwait,
            out_specs=[pl.BlockSpec(memory_space=pltpu.HBM)] * direct + [vmem] * (len(outs) - direct),
            scratch_shapes=list(scratch),
            compiler_params=pltpu.CompilerParams(vmem_limit_bytes=VMEM),
            cost_estimate=pl.CostEstimate(
                flops=int(COST.get(name, 0.0) * 1e9), bytes_accessed=0, transcendentals=0
            ),
            name=name,
        )(*args, *after)

    return run


def sds(shape, dtype=BF):
    return jax.ShapeDtypeStruct(shape, dtype)


def pack_weight_body(nb, ngroups, w_ref, l_ref, r_ref, *outs):
    _, block = position(ngroups)
    r, bd = w_ref.shape[1], w_ref.shape[2]
    chunks = bd // LANE
    bl, ext = l_ref.shape[1], r_ref.shape[1]
    left = jnp.concatenate([l_ref[j].astype(F32) for j in range(l_ref.shape[0])], axis=1).astype(BF)
    right = jnp.concatenate([r_ref[j].astype(F32) for j in range(r_ref.shape[0])], axis=1).astype(BF)
    for d in range(nb):
        for ch in range(chunks):
            outs[d][ch * r : (ch + 1) * r, :] = w_ref[block ^ far(d, nb), :, ch * LANE : (ch + 1) * LANE]
        outs[d][chunks * r : chunks * r + bl, :] = left
        outs[d][chunks * r + bl :, :] = right


def pack_tokens_body(nb, ngroups, with_scale, x_ref, *outs):
    _, block = position(ngroups)
    t, width = x_ref.shape
    bd = width // nb
    chunks = bd // LANE
    if with_scale:
        x = x_ref[...].astype(F32)
        inv = lax.rsqrt(jnp.mean(x * x, axis=-1, keepdims=True) + EPS)
        parts = split3(to_row(inv))
        tile = jnp.concatenate(list(parts) + [jnp.zeros((SUB - 3, t), F32)], axis=0).astype(BF)
    for d in range(nb):
        for ch in range(chunks):
            lanes = pl.ds(pl.multiple_of((block ^ far(d, nb)) * bd + ch * LANE, LANE), LANE)
            outs[d][ch * t : (ch + 1) * t, :] = x_ref[:, lanes]
        if with_scale:
            outs[d][chunks * t :, :] = tile


def pick(n, part_of, part):
    row = lax.broadcasted_iota(jnp.int32, (n, part_of), 0)
    col = lax.broadcasted_iota(jnp.int32, (n, part_of), 1)
    return jnp.where(row == part * part_of + col, 1.0, 0.0).astype(BF)


def split_features_body(nb, ngroups, x_ref, *outs):
    group, _ = position(ngroups)
    part_of = outs[0].shape[2]
    bd = x_ref.shape[1] // nb
    for e in range(ngroups):
        take = pick(bd, part_of, group ^ e)
        for k in range(nb):
            outs[e][k] = mm(x_ref[:, k * bd : (k + 1) * bd], take).astype(BF)


def pack_shares_body(nb, ngroups, *refs):
    group, place = position(ngroups)
    shares, outs = refs[:ngroups], refs[ngroups:]
    t = shares[0].shape[1]
    for d in range(nb):
        for e in range(ngroups):
            outs[d][rows((group ^ e) * t, t), :] = shares[e][place ^ far(d, nb)]


def relay_body(nb, ngroups, r4, ext, *refs):
    _, place = position(ngroups)
    out = refs[nb]
    bl = refs[0].shape[0] - r4 - ext
    for d in range(nb):
        to = place ^ far(d, nb)
        out[rows(to * r4, r4), :] = refs[d][:r4, :]
        out[pl.ds(pl.multiple_of(nb * r4 + to * ext, ext), ext), :] = refs[d][r4 + bl :, :]
        out[pl.ds(pl.multiple_of(nb * (r4 + ext) + to * bl, bl), bl), :] = refs[d][r4 : r4 + bl, :]


def expand_matrix(ext, nb, ngroups, na):
    n = SUB * ext
    row = lax.broadcasted_iota(jnp.int32, (n, n), 0)
    col = lax.broadcasted_iota(jnp.int32, (n, n), 1)
    return jnp.where((row // ext == col % SUB) & (row % ext == natural(col // SUB, nb, ngroups, na)), 1.0, 0.0).astype(BF)


def same_position(n):
    row = lax.broadcasted_iota(jnp.int32, (n, n), 0)
    col = lax.broadcasted_iota(jnp.int32, (n, n), 1)
    return row % SUB == col % SUB


def assemble_body(nb, ngroups, r, ext, bl, *refs):
    group, _ = position(ngroups)
    na = LANE // bl
    relays = refs[:ngroups]
    wk_ref, mq_ref, bd_ref, all_ref = refs[ngroups:]
    chunks = wk_ref.shape[1] // LANE
    r4 = chunks * r
    for e in range(ngroups):
        g = group ^ e
        for c in range(nb):
            for ch in range(chunks):
                wk_ref[rows((c * ngroups + g) * r, r), ch * LANE : (ch + 1) * LANE] = relays[e][
                    c * r4 + ch * r : c * r4 + (ch + 1) * r, :
                ]
            all_ref[c * ngroups + g] = relays[e][nb * r4 + c * ext : nb * r4 + (c + 1) * ext, :]
    nq = mq_ref.shape[0]
    per = nb * ngroups // nq
    n = SUB * ext
    turn = expand_matrix(ext, nb, ngroups, na)
    spread = jnp.where(
        natural(lax.broadcasted_iota(jnp.int32, (n, ext), 0) // SUB, nb, ngroups, na)
        == lax.broadcasted_iota(jnp.int32, (n, ext), 1),
        1.0,
        0.0,
    ).astype(BF)
    same = same_position(n)
    for q in range(nq):
        tiles = jnp.concatenate([all_ref[q * per + i] for i in range(per)], axis=1)
        wide = mm(tiles, turn).astype(BF)
        mq_ref[q] = jnp.where(same, mm(spread, wide), 0.0).astype(BF)
    half_row = lax.broadcasted_iota(jnp.int32, (LANE, LANE), 0) // bl
    half_col = lax.broadcasted_iota(jnp.int32, (LANE, LANE), 1) // bl
    for e in range(ngroups):
        for c in range(nb):
            at = nb * (r4 + ext) + c * bl
            both = jnp.concatenate([relays[e][at : at + bl, :].astype(F32)] * na, axis=0)
            bd_ref[(group ^ e) * nb + c] = jnp.where(half_row == half_col, both, 0.0).astype(BF)


def unpack(msg, t, chunks):
    return jnp.concatenate([msg[ch * t : (ch + 1) * t, :] for ch in range(chunks)], axis=1)


def scale_of(msg, t, chunks):
    tile = msg[chunks * t : chunks * t + SUB, :].astype(F32)
    return to_col(tile[0:1] + tile[1:2] + tile[2:3])


def norm_body(nb, ngroups, *refs):
    _, place = position(ngroups)
    msgs = refs[:nb]
    gain_ref, normin_ref = refs[nb:]
    t = LANE
    bd = normin_ref.shape[1]
    chunks = bd // LANE
    gain = gain_ref[:, pl.ds(pl.multiple_of(place * bd, LANE), bd)]
    for d in range(nb):
        x = unpack(msgs[d], t, chunks).astype(F32)
        normed = x * scale_of(msgs[d], t, chunks)
        normin_ref[rows((place ^ far(d, nb)) * t, t), :] = (normed * gain).astype(BF)


def project_body(nb, ngroups, normin_ref, wk_ref, bd_ref, proj_ref, first_ref):
    group, _ = position(ngroups)
    t = LANE
    proj_ref[...] = mm(normin_ref[...], wk_ref[...]).astype(BF)
    for c in range(nb):
        at = slice(c * t, (c + 1) * t)
        first_ref[at, :] = mm(bd_ref[group * nb + c], proj_ref[at, :]).astype(BF)


def project_shares_body(ngroups, normin_ref, wk_ref, *outs):
    group, _ = position(ngroups)
    bd = wk_ref.shape[0]
    proj = mm(normin_ref[...], wk_ref[...]).astype(BF)
    for e in range(ngroups):
        outs[e][...] = mm(proj, pick(bd, bd // ngroups, group ^ e)).astype(BF)


def gather_positions(group, bl, parts, out_ref):
    blocks = parts[0].shape[0] // bl
    for e, part in enumerate(parts):
        base = (group ^ e) * blocks * SUB
        for q in range(bl // SUB):
            for a in range(blocks):
                out_ref[q, pl.ds(pl.multiple_of(base + a * SUB, SUB), SUB), :] = part[
                    a * bl + q * SUB : a * bl + (q + 1) * SUB, :
                ]


def mix_body(ngroups, bl, *refs):
    group, _ = position(ngroups)
    firsts = refs[:ngroups]
    mq_ref, mixed_ref, f_ref = refs[ngroups:]
    gather_positions(group, bl, firsts, f_ref)
    blocks = firsts[0].shape[0] // bl
    own = rows(group * blocks * SUB, blocks * SUB)
    for q in range(bl // SUB):
        mixed = mm(mq_ref[q, own, :], f_ref[q]).astype(BF)
        for a in range(blocks):
            mixed_ref[a * bl + q * SUB : a * bl + (q + 1) * SUB, :] = mixed[a * SUB : (a + 1) * SUB, :]


def output_body(nb, ngroups, mixed_ref, proj_ref, *refs):
    _, place = position(ngroups)
    msgs, outs = refs[:nb], refs[nb:]
    t = LANE
    chunks = proj_ref.shape[1] // LANE
    for d in range(nb):
        at = rows((place ^ far(d, nb)) * t, t)
        x = unpack(msgs[d], t, chunks).astype(F32)
        outs[d][...] = (x + proj_ref[at, :].astype(F32) * mixed_ref[at, :].astype(F32)).astype(BF)


def to_positions(x_ref, out_ref, bl):
    for q in range(bl // SUB):
        for a in range(x_ref.shape[0] // bl):
            out_ref[q, a * SUB : (a + 1) * SUB, :] = x_ref[a * bl + q * SUB : a * bl + (q + 1) * SUB, :]


def from_positions(x, q, out_ref, bl):
    for a in range(out_ref.shape[0] // bl):
        out_ref[a * bl + q * SUB : a * bl + (q + 1) * SUB, :] = x[a * SUB : (a + 1) * SUB, :]


def mix_shares_body(ngroups, bl, *refs):
    group, _ = position(ngroups)
    parts = refs[:ngroups]
    mq_ref, bd_ref, proj_ref, f_ref, mixed_ref, first_ref = refs[ngroups:]
    t = LANE
    tg = parts[0].shape[0]
    for e in range(ngroups):
        proj_ref[rows((group ^ e) * tg, tg), :] = parts[e][...]
    for c in range(bd_ref.shape[0]):
        at = slice(c * t, (c + 1) * t)
        first_ref[at, :] = mm(bd_ref[c], proj_ref[at, :]).astype(BF)
    to_positions(first_ref, f_ref, bl)
    for q in range(bl // SUB):
        from_positions(mm(mq_ref[q], f_ref[q]).astype(BF), q, mixed_ref, bl)


def take_grad_body(nb, ngroups, *refs):
    _, place = position(ngroups)
    grad_ref = refs[nb]
    t = LANE
    for d in range(nb):
        for g in range(ngroups):
            grad_ref[rows((g * nb + (place ^ far(d, nb))) * t, t), :] = refs[d][g * t : (g + 1) * t, :]


def backward_body(nb, ngroups, bl, *refs):
    group, _ = position(ngroups)
    grad_ref, proj_ref, mixed_ref, mq_ref, bd_ref = refs[:5]
    outs = refs[5 : 5 + ngroups]
    a_ref, adj_first_ref, adj_ref = refs[5 + ngroups :]
    t = LANE
    adj_ref[...] = (grad_ref[...].astype(F32) * proj_ref[...].astype(F32)).astype(BF)
    to_positions(adj_ref, a_ref, bl)
    for q in range(bl // SUB):
        from_positions(mm(mq_ref[q], a_ref[q], 0, 0).astype(BF), q, adj_first_ref, bl)
    for c in range(bd_ref.shape[0]):
        at = slice(c * t, (c + 1) * t)
        grad = grad_ref[at, :].astype(F32)
        mixed = mixed_ref[at, :].astype(F32)
        adj_ref[at, :] = (grad * mixed + mm(bd_ref[c], adj_first_ref[at, :], 0, 0)).astype(BF)
    tg = nb * t
    for e in range(ngroups):
        outs[e][...] = adj_ref[rows((group ^ e) * tg, tg), :]


def factor_grads_body(nb, ngroups, bl, ext, f_ref, a_ref, adj_first_ref, proj_ref, *refs):
    group, _ = position(ngroups)
    outs, right_ref, left_ref = refs[:ngroups], refs[ngroups], refs[ngroups + 1]
    na = LANE // bl
    t = LANE
    nq = f_ref.shape[0]
    n = SUB * ext
    upper = lax.broadcasted_iota(jnp.int32, (bl, LANE), 1) < bl
    for g in range(ngroups):
        for c in range(nb):
            at = slice((g * nb + c) * t, (g * nb + c + 1) * t)
            both = mm(adj_first_ref[at, :], proj_ref[at, :], 1, 1)
            left_ref[g, c * bl : (c + 1) * bl, :] = jnp.where(upper, both[:bl, :], both[bl:, :]).astype(BF)
    turn = expand_matrix(ext, nb, ngroups, na)
    same = same_position(n)
    order = jnp.where(
        natural(lax.broadcasted_iota(jnp.int32, (ext, ext), 0), nb, ngroups, na)
        == lax.broadcasted_iota(jnp.int32, (ext, ext), 1),
        1.0,
        0.0,
    ).astype(BF)
    per = nb * ngroups // nq
    for q in range(nq):
        pairs = jnp.where(same, mm(a_ref[q], f_ref[q], 1, 1), 0.0)
        summed = jnp.sum(pairs.reshape(ext, SUB, n), axis=1).astype(BF)
        turned = mm(order, mm(summed, turn, 1, 1).astype(BF), 0, 0).astype(BF)
        for i in range(per):
            s = q * per + i
            right_ref[s % ngroups, (s // ngroups) * ext : (s // ngroups + 1) * ext, :] = turned[
                :, i * LANE : (i + 1) * LANE
            ]
    for e in range(ngroups):
        outs[e][: nb * bl, :] = left_ref[group ^ e]
        outs[e][nb * bl :, :] = right_ref[group ^ e]


def adj_norm_body(nb, ngroups, normin_ref, wk_ref, gain_ref, *refs):
    group, place = position(ngroups)
    shares, rest = refs[:ngroups], refs[ngroups:]
    adj_proj_ref, gain_part_ref, outs, adj_norm_ref = rest[0], rest[1], rest[2 : 2 + nb], rest[2 + nb]
    bd = wk_ref.shape[0]
    t = LANE
    adj_proj = jnp.zeros(adj_proj_ref.shape, F32)
    for e in range(ngroups):
        adj_proj = adj_proj + mm(shares[e][...], pick(bd, bd // ngroups, group ^ e), 1, 1)
    adj_proj_ref[...] = adj_proj.astype(BF)
    adj_norm = mm(adj_proj_ref[...], wk_ref[...], 1, 1)
    adj_norm_ref[...] = adj_norm
    gain = gain_ref[:, pl.ds(pl.multiple_of(place * bd, LANE), bd)]
    gain_part_ref[...] = jnp.sum(adj_norm * normin_ref[...].astype(F32), axis=0, keepdims=True) / gain
    for d in range(nb):
        outs[d][...] = adj_norm_ref[rows((place ^ far(d, nb)) * t, t), :].astype(BF)


def weight_grad_body(nb, ngroups, normin_ref, adj_proj_ref, gain_part_ref, *refs):
    group, _ = position(ngroups)
    tiles, own_ref = refs[: ngroups - 1], refs[ngroups - 1]
    sends, gw_ref = refs[ngroups : 2 * ngroups - 1], refs[2 * ngroups - 1]
    share, bd = own_ref.shape
    r = share // nb
    gw_ref[...] = mm(normin_ref[...], adj_proj_ref[...], 0, 0)
    tile = jnp.concatenate(
        list(split3(gain_part_ref[...])) + [jnp.zeros((SUB - 3, bd), F32)], axis=0
    ).astype(BF)
    for c in range(nb):
        at = slice(c * r, (c + 1) * r)
        own_ref[at, :] = gw_ref[rows((c * ngroups + group) * r, r), :]
        for e in range(1, ngroups):
            sends[e - 1][at, :] = gw_ref[rows((c * ngroups + (group ^ e)) * r, r), :].astype(BF)
    for e in range(1, ngroups):
        sends[e - 1][share : share + SUB, :] = tile
        high = tiles[e - 1].shape[0] * LANE // bd
        for ch in range(bd // LANE):
            sends[e - 1][share + SUB :, ch * LANE : (ch + 1) * LANE] = tiles[e - 1][
                ch * high : (ch + 1) * high, :
            ]


def weight_sum_body(nb, ngroups, bl, ext, own_ref, gain_part_ref, *refs):
    group, place = position(ngroups)
    recvs, tiles_ref = refs[: ngroups - 1], refs[ngroups - 1]
    high = tiles_ref.shape[0] * LANE // own_ref.shape[1]
    outs = refs[ngroups : ngroups + nb]
    total_ref, gains_ref, sums_ref = refs[ngroups + nb :]
    share, bd = own_ref.shape
    chunks = bd // LANE
    r = share // nb
    total = own_ref[...]
    gains_ref[group] = gain_part_ref[...]
    for e in range(1, ngroups):
        total = total + recvs[e - 1][:share, :].astype(F32)
        three = recvs[e - 1][share : share + SUB, :].astype(F32)
        gains_ref[group ^ e] = three[0:1] + three[1:2] + three[2:3]
    total_ref[...] = total.astype(BF)
    for ch in range(chunks):
        at = slice(ch * high, (ch + 1) * high)
        tile_sum = tiles_ref[at, :].astype(F32)
        for recv in recvs:
            tile_sum = tile_sum + recv[share + SUB :, ch * LANE : (ch + 1) * LANE].astype(F32)
        sums_ref[at, :] = tile_sum.astype(BF)
    gain = gains_ref[0]
    for g in range(1, ngroups):
        gain = gain + gains_ref[g]
    three = split3(gain)
    parts = [p[:, ch * LANE : (ch + 1) * LANE] for p in three for ch in range(chunks)]
    tile = jnp.concatenate(parts + [jnp.zeros((SUB - len(parts), LANE), F32)], axis=0).astype(BF)
    for d in range(nb):
        to = place ^ far(d, nb)
        for ch in range(chunks):
            outs[d][ch * r : (ch + 1) * r, :] = total_ref[rows(to * r, r), ch * LANE : (ch + 1) * LANE]
        at = chunks * r
        outs[d][at : at + bl, :] = sums_ref[rows(to * bl, bl), :]
        outs[d][at + bl : at + bl + ext, :] = sums_ref[
            pl.ds(pl.multiple_of(nb * bl + to * ext, ext), ext), :
        ]
        outs[d][at + bl + ext :, :] = tile


def input_grad_body(nb, ngroups, x_ref, grad_ref, gain_ref, *refs):
    _, place = position(ngroups)
    parts, out, adj_ref = refs[:nb], refs[nb], refs[nb + 1]
    bd = parts[0].shape[1]
    for d in range(nb):
        adj_ref[:, pl.ds(pl.multiple_of((place ^ far(d, nb)) * bd, LANE), bd)] = parts[d][...].astype(F32)
    x = x_ref[...].astype(F32)
    inv = lax.rsqrt(jnp.mean(x * x, axis=-1, keepdims=True) + EPS)
    normed = x * inv
    scaled = adj_ref[...] * gain_ref[...]
    mean = jnp.mean(scaled * normed, axis=-1, keepdims=True)
    out[...] = (grad_ref[...].astype(F32) + inv * (scaled - normed * mean)).astype(BF)


def join_body(nb, ngroups, *refs):
    _, block = position(ngroups)
    out = refs[nb]
    bd = refs[0].shape[1]
    for d in range(nb):
        out[:, pl.ds(pl.multiple_of((block ^ far(d, nb)) * bd, LANE), bd)] = refs[d][...]


def join_weight_body(nb, ngroups, *refs):
    _, block = position(ngroups)
    gw_ref, gain_ref, left_out, right_out, done_ref, by_block = refs[nb:]
    done_ref[...] = jnp.zeros(done_ref.shape, done_ref.dtype)
    r, _, bd = gw_ref.shape
    chunks = bd // LANE
    na, bl, _ = left_out.shape
    npos, ext, _ = right_out.shape
    at = chunks * r
    left = refs[0][at : at + bl, :].astype(F32)
    right = refs[0][at + bl : at + bl + ext, :].astype(F32)
    for d in range(1, nb):
        left = left + refs[d][at : at + bl, :].astype(F32)
        right = right + refs[d][at + bl : at + bl + ext, :].astype(F32)
    for j in range(na):
        left_out[j] = left[:, j * bl : (j + 1) * bl]
    for j in range(npos):
        right_out[j] = right[:, j * ext : (j + 1) * ext]
    for d in range(nb):
        k = block ^ far(d, nb)
        by_block[k] = unpack(refs[d], r, chunks).astype(F32)
        tile = refs[d][at + bl + ext :, :].astype(F32)
        for ch in range(chunks):
            gain_ref[:, pl.ds(pl.multiple_of(k * bd + ch * LANE, LANE), LANE)] = (
                tile[ch : ch + 1] + tile[chunks + ch : chunks + ch + 1] + tile[2 * chunks + ch : 2 * chunks + ch + 1]
            )
    for k in range(nb):
        gw_ref[:, k, :] = by_block[k]


def arrived_body(out_ref):
    out_ref[...] = jnp.zeros(out_ref.shape, out_ref.dtype)


def store_body(x_ref, out_ref, done_ref):
    out_ref[...] = x_ref[...]
    done_ref[...] = jnp.zeros(done_ref.shape, done_ref.dtype)


def shards(act_in, saved_in, grad_in, gain, weight, left_blocks, right_blocks):
    nseq = lax.axis_size("seq")
    npipe = lax.axis_size("pipe")
    _, t, width = act_in.shape
    _, r, nb, bd = weight.shape
    ngroups = nseq // nb
    bl = left_blocks.shape[2]
    ext = right_blocks.shape[2]
    npos = right_blocks.shape[1]
    chunks = bd // LANE
    tg = nb * t
    r4 = chunks * r
    nq = bl // SUB
    n = SUB * ext

    def within(parts):
        return [parts[0]] + [
            lax.ppermute(parts[d], "seq", [(s, s ^ (far(d, nb) * ngroups)) for s in range(nseq)])
            for d in range(1, nb)
        ]

    def across(block, e):
        return lax.ppermute(block, "seq", [(s, s ^ e) for s in range(nseq)])

    def gathered(block):
        return [block] + [across(block, e) for e in range(1, ngroups)]

    def handed(parts, step):
        return [
            lax.ppermute(
                parts[d],
                ("pipe", "seq"),
                [
                    (p * nseq + s, (p + step) % npipe * nseq + (s ^ (far(d, nb) * ngroups)))
                    for p in range(npipe)
                    for s in range(nseq)
                ],
            )
            for d in range(nb)
        ]

    def exchanged(parts):
        return list(parts[:1]) + [across(parts[e], e) for e in range(1, ngroups)]

    part = functools.partial
    def run(name, body, outs, scratch=(), direct=0):
        return call(body, outs, scratch, direct, name)

    pack = part(pack_tokens_body, nb, ngroups)
    norm = part(norm_body, nb, ngroups)
    join = part(join_body, nb, ngroups)
    scaled_msgs = [sds((chunks * t + SUB, LANE))] * nb
    tokens = [sds((tg, bd))]
    pieces = [sds((t, bd))] * nb
    rows_of = bd // ngroups
    part_of = bd // ngroups
    shares = [sds((tg, part_of))] * ngroups
    every = [sds((ngroups * tg, part_of))]
    by_position = [sds((nq, n, part_of))]

    def scratch(structs):
        return [pltpu.VMEM(s.shape, s.dtype) for s in structs]

    w_msgs = run("pack_weight", part(pack_weight_body, nb, ngroups), [sds((r4 + bl + ext, LANE))] * nb)(
        jnp.transpose(weight[0], (1, 0, 2)), left_blocks[0], right_blocks[0]
    )
    grad_shares = run(
        "split_grad", part(split_features_body, nb, ngroups), [sds((nb, t, part_of))] * ngroups
    )(grad_in[0], after=w_msgs[:1])
    sto_msgs = run("pack_saved", part(pack, True), scaled_msgs)(saved_in[0], after=grad_shares[:1])
    early = sto_msgs[:1]
    w_msgs, grad_shares, sto_msgs = within(w_msgs), exchanged(grad_shares), within(sto_msgs)
    (relay,) = run("relay", part(relay_body, nb, ngroups, r4, ext), [sds((nb * (r4 + ext + bl), LANE))])(
        *w_msgs, after=early
    )
    relays = gathered(relay)
    grad_msgs = run("pack_grad", part(pack_shares_body, nb, ngroups), [sds((ngroups * t, part_of))] * nb)(
        *grad_shares, after=[relay]
    )
    (sto_normin,) = run("norm_saved", norm, tokens)(*sto_msgs, gain, after=grad_msgs[:1])
    wk, mq, bd_left = run(
        "assemble",
        part(assemble_body, nb, ngroups, r, ext, bl),
        [sds((bd, bd)), sds((nq, n, n)), sds((nseq, LANE, LANE))],
        [pltpu.VMEM((nseq, ext, LANE), BF)],
    )(*relays, after=[sto_normin])
    sto_shares = run("project_saved", part(project_shares_body, ngroups), shares)(sto_normin, wk)
    cur_msgs = run("pack_act", part(pack, True), scaled_msgs)(act_in[0], after=sto_shares[:1])
    grad_msgs = within(grad_msgs)
    (grad,) = run("take_grad", part(take_grad_body, nb, ngroups), every)(*grad_msgs, after=cur_msgs[:1])
    sto_shares, cur_msgs = exchanged(sto_shares), within(cur_msgs)
    sto_proj, sto_f, sto_mixed = run(
        "mix_saved", part(mix_shares_body, ngroups, bl), every + by_position + every, scratch(every)
    )(*sto_shares, mq, bd_left, after=[grad])
    *adj_shares, adj_f, adj_first = run(
        "backward", part(backward_body, nb, ngroups, bl), shares + by_position + every, scratch(every)
    )(grad, sto_proj, sto_mixed, mq, bd_left)
    adj_wait = adj_shares[:1]
    adj_shares = exchanged(adj_shares)
    tiles = run(
        "factor_grads",
        part(factor_grads_body, nb, ngroups, bl, ext),
        [sds((nb * (bl + ext), LANE))] * ngroups,
        scratch([sds((ngroups, nb * ext, LANE)), sds((ngroups, nb * bl, LANE))]),
    )(sto_f, adj_f, adj_first, sto_proj, after=adj_wait)
    tiles_wait = tiles[:1]
    (act_arrived,) = run("far_act", arrived_body, [sds((8, LANE), F32)])(after=[*tiles_wait, *cur_msgs[1:3]])
    adj_proj, gain_part, *adj_parts = run(
        "adj_norm",
        part(adj_norm_body, nb, ngroups),
        tokens + [sds((1, bd), F32)] + pieces,
        scratch([sds((tg, bd), F32)]),
    )(sto_normin, wk, gain, *adj_shares, after=[act_arrived])
    adj_wait = adj_parts[:1]
    adj_parts = within(adj_parts)
    own_gw, *sends = run(
        "weight_grad",
        part(weight_grad_body, nb, ngroups),
        [sds((rows_of, bd), F32)] + [sds((rows_of + SUB + nb * (bl + ext) // chunks, bd))] * (ngroups - 1),
        scratch([sds((bd, bd), F32)]),
    )(sto_normin, adj_proj, gain_part, *tiles[1:], after=adj_wait)
    recvs = [across(sends[e - 1], e) for e in range(1, ngroups)]
    (cur_normin,) = run("norm_act", norm, tokens)(*cur_msgs, gain, after=[own_gw])
    cur_proj, cur_first = run("project_act", part(project_body, nb, ngroups), tokens * 2)(
        cur_normin, wk, bd_left
    )
    cur_firsts = gathered(cur_first)
    (adj_arrived,) = run("far_adj", arrived_body, [sds((8, LANE), F32)])(after=[cur_first, *adj_parts[1:3]])
    gw_parts = run(
        "weight_sum",
        part(weight_sum_body, nb, ngroups, bl, ext),
        [sds((r4 + bl + ext + SUB, LANE))] * nb,
        scratch([sds((rows_of, bd)), sds((ngroups, 1, bd), F32), sds((nb * (bl + ext), LANE))]),
    )(own_gw, gain_part, *recvs, tiles[0], after=[adj_arrived])
    (adj_x,) = run(
        "input_grad", part(input_grad_body, nb, ngroups), [sds((t, width))], scratch([sds((t, width), F32)])
    )(saved_in[0], grad_in[0], gain, *adj_parts, after=gw_parts[:1])
    (cur_mixed,) = run(
        "mix_act", part(mix_body, ngroups, bl), tokens, scratch([sds((nq, n, bd))])
    )(*cur_firsts, mq, after=[adj_x])
    gw_parts = within(gw_parts)
    out_parts = run("output", part(output_body, nb, ngroups), pieces)(cur_mixed, cur_proj, *cur_msgs)
    out_wait = out_parts[:1]
    out_parts = handed(out_parts, 1)
    grad_handed = lax.ppermute(adj_x, "pipe", [(p, (p - 1) % npipe) for p in range(npipe)])
    weight_grad, gain_grad, left_grad, right_grad, done = run(
        "join_weight",
        part(join_weight_body, nb, ngroups),
        [
            sds((r, nb, bd), F32),
            sds((1, width), F32),
            sds((left_blocks.shape[1], bl, bl), F32),
            sds((npos, ext, ext), F32),
            sds((8, LANE), F32),
        ],
        scratch([sds((nb, r, bd), F32)]),
    )(*gw_parts, after=out_wait)
    grad_handed, done = run("store", store_body, [sds((t, width)), sds((8, LANE), F32)])(
        grad_handed, after=[done]
    )
    (handed_on,) = run("join_out", join, [sds((t, width))])(*out_parts, after=[done])
    return (
        handed_on[None],
        grad_handed[None],
        weight_grad[None],
        gain_grad,
        left_grad[None],
        right_grad[None],
    )


def solution(mesh):
    tokens = P("pipe", "seq", None)
    factor = P("pipe", "seq", None, None)
    return jax.shard_map(
        shards,
        mesh=mesh,
        in_specs=(tokens, tokens, tokens, P("pipe", None), factor, factor, factor),
        out_specs=(tokens, tokens, factor, P("pipe", None), factor, factor),
        check_vma=False,
    )
```

```python
import functools

import jax
import jax.numpy as jnp
from jax import lax
from jax.experimental import pallas as pl
from jax.experimental.pallas import tpu as pltpu
from jax.sharding import PartitionSpec as P

BF = jnp.bfloat16
F32 = jnp.float32
LANE = 128
SUB = 16
EPS = 1e-06
COST = {"relay": 3, "norm_saved": 3.0, "take_grad": 6.0, "norm_act": 3, "join_weight": 3, "join_out": 5, "far_adj": 2}
VMEM = 48 * 1024 * 1024


def position(ngroups):
    me = lax.axis_index("seq")
    return me % ngroups, me // ngroups


def far(d, nb):
    return (nb - d) % nb


def natural(pos, nb, ngroups, na):
    return ((pos // na % nb) * ngroups + pos // (nb * na)) * na + pos % na


def split3(x):
    hi = x.astype(BF).astype(F32)
    mid = (x - hi).astype(BF).astype(F32)
    return hi, mid, x - hi - mid


def eye(n):
    return lax.broadcasted_iota(jnp.int32, (n, n), 0) == lax.broadcasted_iota(jnp.int32, (n, n), 1)


def to_row(col):
    return jnp.sum(jnp.where(eye(col.shape[0]), col, 0.0), axis=0, keepdims=True)


def to_col(row):
    return jnp.sum(jnp.where(eye(row.shape[1]), row, 0.0), axis=1, keepdims=True)


def mm(a, b, ca=1, cb=0):
    return lax.dot_general(a, b, (((ca,), (cb,)), ((), ())), preferred_element_type=F32)


def rows(start, size):
    return pl.ds(pl.multiple_of(start, size), size)


def call(body, outs, scratch, direct, name):
    def run(*args, after=()):
        nin, nwait = len(args), len(after)
        vmem, anywhere = pl.BlockSpec(memory_space=pltpu.VMEM), pl.BlockSpec(memory_space=pl.ANY)

        def without_waits(*refs):
            return body(*refs[:nin], *refs[nin + nwait :])

        return pl.pallas_call(
            without_waits,
            out_shape=list(outs),
            in_specs=[anywhere] * direct + [vmem] * (nin - direct) + [anywhere] * nwait,
            out_specs=[pl.BlockSpec(memory_space=pltpu.HBM)] * direct + [vmem] * (len(outs) - direct),
            scratch_shapes=list(scratch),
            compiler_params=pltpu.CompilerParams(vmem_limit_bytes=VMEM),
            cost_estimate=pl.CostEstimate(
                flops=int(COST.get(name, 0.0) * 1e9), bytes_accessed=0, transcendentals=0
            ),
            name=name,
        )(*args, *after)

    return run


def sds(shape, dtype=BF):
    return jax.ShapeDtypeStruct(shape, dtype)


def pack_weight_body(nb, ngroups, w_ref, l_ref, r_ref, *outs):
    _, block = position(ngroups)
    r, bd = w_ref.shape[1], w_ref.shape[2]
    chunks = bd // LANE
    bl, ext = l_ref.shape[1], r_ref.shape[1]
    left = jnp.concatenate([l_ref[j].astype(F32) for j in range(l_ref.shape[0])], axis=1).astype(BF)
    right = jnp.concatenate([r_ref[j].astype(F32) for j in range(r_ref.shape[0])], axis=1).astype(BF)
    for d in range(nb):
        for ch in range(chunks):
            outs[d][ch * r : (ch + 1) * r, :] = w_ref[block ^ far(d, nb), :, ch * LANE : (ch + 1) * LANE]
        outs[d][chunks * r : chunks * r + bl, :] = left
        outs[d][chunks * r + bl :, :] = right


def pack_tokens_body(nb, ngroups, with_scale, x_ref, *outs):
    _, block = position(ngroups)
    t, width = x_ref.shape
    bd = width // nb
    chunks = bd // LANE
    if with_scale:
        x = x_ref[...].astype(F32)
        inv = lax.rsqrt(jnp.mean(x * x, axis=-1, keepdims=True) + EPS)
        parts = split3(to_row(inv))
        tile = jnp.concatenate(list(parts) + [jnp.zeros((SUB - 3, t), F32)], axis=0).astype(BF)
    for d in range(nb):
        for ch in range(chunks):
            lanes = pl.ds(pl.multiple_of((block ^ far(d, nb)) * bd + ch * LANE, LANE), LANE)
            outs[d][ch * t : (ch + 1) * t, :] = x_ref[:, lanes]
        if with_scale:
            outs[d][chunks * t :, :] = tile


def pick(n, part_of, part):
    row = lax.broadcasted_iota(jnp.int32, (n, part_of), 0)
    col = lax.broadcasted_iota(jnp.int32, (n, part_of), 1)
    return jnp.where(row == part * part_of + col, 1.0, 0.0).astype(BF)


def split_features_body(nb, ngroups, x_ref, *outs):
    group, _ = position(ngroups)
    part_of = outs[0].shape[2]
    bd = x_ref.shape[1] // nb
    for e in range(ngroups):
        take = pick(bd, part_of, group ^ e)
        for k in range(nb):
            outs[e][k] = mm(x_ref[:, k * bd : (k + 1) * bd], take).astype(BF)


def pack_shares_body(nb, ngroups, *refs):
    group, place = position(ngroups)
    shares, outs = refs[:ngroups], refs[ngroups:]
    t = shares[0].shape[1]
    for d in range(nb):
        for e in range(ngroups):
            outs[d][rows((group ^ e) * t, t), :] = shares[e][place ^ far(d, nb)]


def relay_body(nb, ngroups, r4, ext, *refs):
    _, place = position(ngroups)
    out = refs[nb]
    bl = refs[0].shape[0] - r4 - ext
    for d in range(nb):
        to = place ^ far(d, nb)
        out[rows(to * r4, r4), :] = refs[d][:r4, :]
        out[pl.ds(pl.multiple_of(nb * r4 + to * ext, ext), ext), :] = refs[d][r4 + bl :, :]
        out[pl.ds(pl.multiple_of(nb * (r4 + ext) + to * bl, bl), bl), :] = refs[d][r4 : r4 + bl, :]


def expand_matrix(ext, nb, ngroups, na):
    n = SUB * ext
    row = lax.broadcasted_iota(jnp.int32, (n, n), 0)
    col = lax.broadcasted_iota(jnp.int32, (n, n), 1)
    return jnp.where((row // ext == col % SUB) & (row % ext == natural(col // SUB, nb, ngroups, na)), 1.0, 0.0).astype(BF)


def same_position(n):
    row = lax.broadcasted_iota(jnp.int32, (n, n), 0)
    col = lax.broadcasted_iota(jnp.int32, (n, n), 1)
    return row % SUB == col % SUB


def assemble_body(nb, ngroups, r, ext, bl, *refs):
    group, _ = position(ngroups)
    na = LANE // bl
    relays = refs[:ngroups]
    wk_ref, mq_ref, bd_ref, all_ref = refs[ngroups:]
    chunks = wk_ref.shape[1] // LANE
    r4 = chunks * r
    for e in range(ngroups):
        g = group ^ e
        for c in range(nb):
            for ch in range(chunks):
                wk_ref[rows((c * ngroups + g) * r, r), ch * LANE : (ch + 1) * LANE] = relays[e][
                    c * r4 + ch * r : c * r4 + (ch + 1) * r, :
                ]
            all_ref[c * ngroups + g] = relays[e][nb * r4 + c * ext : nb * r4 + (c + 1) * ext, :]
    nq = mq_ref.shape[0]
    per = nb * ngroups // nq
    n = SUB * ext
    turn = expand_matrix(ext, nb, ngroups, na)
    spread = jnp.where(
        natural(lax.broadcasted_iota(jnp.int32, (n, ext), 0) // SUB, nb, ngroups, na)
        == lax.broadcasted_iota(jnp.int32, (n, ext), 1),
        1.0,
        0.0,
    ).astype(BF)
    same = same_position(n)
    for q in range(nq):
        tiles = jnp.concatenate([all_ref[q * per + i] for i in range(per)], axis=1)
        wide = mm(tiles, turn).astype(BF)
        mq_ref[q] = jnp.where(same, mm(spread, wide), 0.0).astype(BF)
    half_row = lax.broadcasted_iota(jnp.int32, (LANE, LANE), 0) // bl
    half_col = lax.broadcasted_iota(jnp.int32, (LANE, LANE), 1) // bl
    for e in range(ngroups):
        for c in range(nb):
            at = nb * (r4 + ext) + c * bl
            both = jnp.concatenate([relays[e][at : at + bl, :].astype(F32)] * na, axis=0)
            bd_ref[(group ^ e) * nb + c] = jnp.where(half_row == half_col, both, 0.0).astype(BF)


def unpack(msg, t, chunks):
    return jnp.concatenate([msg[ch * t : (ch + 1) * t, :] for ch in range(chunks)], axis=1)


def scale_of(msg, t, chunks):
    tile = msg[chunks * t : chunks * t + SUB, :].astype(F32)
    return to_col(tile[0:1] + tile[1:2] + tile[2:3])


def norm_body(nb, ngroups, *refs):
    _, place = position(ngroups)
    msgs = refs[:nb]
    gain_ref, normin_ref = refs[nb:]
    t = LANE
    bd = normin_ref.shape[1]
    chunks = bd // LANE
    gain = gain_ref[:, pl.ds(pl.multiple_of(place * bd, LANE), bd)]
    for d in range(nb):
        x = unpack(msgs[d], t, chunks).astype(F32)
        normed = x * scale_of(msgs[d], t, chunks)
        normin_ref[rows((place ^ far(d, nb)) * t, t), :] = (normed * gain).astype(BF)


def project_body(nb, ngroups, normin_ref, wk_ref, bd_ref, proj_ref, first_ref):
    group, _ = position(ngroups)
    t = LANE
    proj_ref[...] = mm(normin_ref[...], wk_ref[...]).astype(BF)
    for c in range(nb):
        at = slice(c * t, (c + 1) * t)
        first_ref[at, :] = mm(bd_ref[group * nb + c], proj_ref[at, :]).astype(BF)


def project_shares_body(ngroups, normin_ref, wk_ref, *outs):
    group, _ = position(ngroups)
    bd = wk_ref.shape[0]
    proj = mm(normin_ref[...], wk_ref[...]).astype(BF)
    for e in range(ngroups):
        outs[e][...] = mm(proj, pick(bd, bd // ngroups, group ^ e)).astype(BF)


def gather_positions(group, bl, parts, out_ref):
    blocks = parts[0].shape[0] // bl
    for e, part in enumerate(parts):
        base = (group ^ e) * blocks * SUB
        for q in range(bl // SUB):
            for a in range(blocks):
                out_ref[q, pl.ds(pl.multiple_of(base + a * SUB, SUB), SUB), :] = part[
                    a * bl + q * SUB : a * bl + (q + 1) * SUB, :
                ]


def mix_body(ngroups, bl, *refs):
    group, _ = position(ngroups)
    firsts = refs[:ngroups]
    mq_ref, mixed_ref, f_ref = refs[ngroups:]
    gather_positions(group, bl, firsts, f_ref)
    blocks = firsts[0].shape[0] // bl
    own = rows(group * blocks * SUB, blocks * SUB)
    for q in range(bl // SUB):
        mixed = mm(mq_ref[q, own, :], f_ref[q]).astype(BF)
        for a in range(blocks):
            mixed_ref[a * bl + q * SUB : a * bl + (q + 1) * SUB, :] = mixed[a * SUB : (a + 1) * SUB, :]


def output_body(nb, ngroups, mixed_ref, proj_ref, *refs):
    _, place = position(ngroups)
    msgs, outs = refs[:nb], refs[nb:]
    t = LANE
    chunks = proj_ref.shape[1] // LANE
    for d in range(nb):
        at = rows((place ^ far(d, nb)) * t, t)
        x = unpack(msgs[d], t, chunks).astype(F32)
        outs[d][...] = (x + proj_ref[at, :].astype(F32) * mixed_ref[at, :].astype(F32)).astype(BF)


def to_positions(x_ref, out_ref, bl):
    for q in range(bl // SUB):
        for a in range(x_ref.shape[0] // bl):
            out_ref[q, a * SUB : (a + 1) * SUB, :] = x_ref[a * bl + q * SUB : a * bl + (q + 1) * SUB, :]


def from_positions(x, q, out_ref, bl):
    for a in range(out_ref.shape[0] // bl):
        out_ref[a * bl + q * SUB : a * bl + (q + 1) * SUB, :] = x[a * SUB : (a + 1) * SUB, :]


def mix_shares_body(ngroups, bl, *refs):
    group, _ = position(ngroups)
    parts = refs[:ngroups]
    mq_ref, bd_ref, proj_ref, f_ref, mixed_ref, first_ref = refs[ngroups:]
    t = LANE
    tg = parts[0].shape[0]
    for e in range(ngroups):
        proj_ref[rows((group ^ e) * tg, tg), :] = parts[e][...]
    for c in range(bd_ref.shape[0]):
        at = slice(c * t, (c + 1) * t)
        first_ref[at, :] = mm(bd_ref[c], proj_ref[at, :]).astype(BF)
    to_positions(first_ref, f_ref, bl)
    for q in range(bl // SUB):
        from_positions(mm(mq_ref[q], f_ref[q]).astype(BF), q, mixed_ref, bl)


def take_grad_body(nb, ngroups, *refs):
    _, place = position(ngroups)
    grad_ref = refs[nb]
    t = LANE
    for d in range(nb):
        for g in range(ngroups):
            grad_ref[rows((g * nb + (place ^ far(d, nb))) * t, t), :] = refs[d][g * t : (g + 1) * t, :]


def backward_body(nb, ngroups, bl, *refs):
    group, _ = position(ngroups)
    grad_ref, proj_ref, mixed_ref, mq_ref, bd_ref = refs[:5]
    outs = refs[5 : 5 + ngroups]
    a_ref, adj_first_ref, adj_ref = refs[5 + ngroups :]
    t = LANE
    adj_ref[...] = (grad_ref[...].astype(F32) * proj_ref[...].astype(F32)).astype(BF)
    to_positions(adj_ref, a_ref, bl)
    for q in range(bl // SUB):
        from_positions(mm(mq_ref[q], a_ref[q], 0, 0).astype(BF), q, adj_first_ref, bl)
    for c in range(bd_ref.shape[0]):
        at = slice(c * t, (c + 1) * t)
        grad = grad_ref[at, :].astype(F32)
        mixed = mixed_ref[at, :].astype(F32)
        adj_ref[at, :] = (grad * mixed + mm(bd_ref[c], adj_first_ref[at, :], 0, 0)).astype(BF)
    tg = nb * t
    for e in range(ngroups):
        outs[e][...] = adj_ref[rows((group ^ e) * tg, tg), :]


def factor_grads_body(nb, ngroups, bl, ext, f_ref, a_ref, adj_first_ref, proj_ref, *refs):
    group, _ = position(ngroups)
    outs, right_ref, left_ref = refs[:ngroups], refs[ngroups], refs[ngroups + 1]
    na = LANE // bl
    t = LANE
    nq = f_ref.shape[0]
    n = SUB * ext
    upper = lax.broadcasted_iota(jnp.int32, (bl, LANE), 1) < bl
    for g in range(ngroups):
        for c in range(nb):
            at = slice((g * nb + c) * t, (g * nb + c + 1) * t)
            both = mm(adj_first_ref[at, :], proj_ref[at, :], 1, 1)
            left_ref[g, c * bl : (c + 1) * bl, :] = jnp.where(upper, both[:bl, :], both[bl:, :]).astype(BF)
    turn = expand_matrix(ext, nb, ngroups, na)
    same = same_position(n)
    order = jnp.where(
        natural(lax.broadcasted_iota(jnp.int32, (ext, ext), 0), nb, ngroups, na)
        == lax.broadcasted_iota(jnp.int32, (ext, ext), 1),
        1.0,
        0.0,
    ).astype(BF)
    per = nb * ngroups // nq
    for q in range(nq):
        pairs = jnp.where(same, mm(a_ref[q], f_ref[q], 1, 1), 0.0)
        summed = jnp.sum(pairs.reshape(ext, SUB, n), axis=1).astype(BF)
        turned = mm(order, mm(summed, turn, 1, 1).astype(BF), 0, 0).astype(BF)
        for i in range(per):
            s = q * per + i
            right_ref[s % ngroups, (s // ngroups) * ext : (s // ngroups + 1) * ext, :] = turned[
                :, i * LANE : (i + 1) * LANE
            ]
    for e in range(ngroups):
        outs[e][: nb * bl, :] = left_ref[group ^ e]
        outs[e][nb * bl :, :] = right_ref[group ^ e]


def adj_norm_body(nb, ngroups, normin_ref, wk_ref, gain_ref, *refs):
    group, place = position(ngroups)
    shares, rest = refs[:ngroups], refs[ngroups:]
    adj_proj_ref, gain_part_ref, outs, adj_norm_ref = rest[0], rest[1], rest[2 : 2 + nb], rest[2 + nb]
    bd = wk_ref.shape[0]
    t = LANE
    adj_proj = jnp.zeros(adj_proj_ref.shape, F32)
    for e in range(ngroups):
        adj_proj = adj_proj + mm(shares[e][...], pick(bd, bd // ngroups, group ^ e), 1, 1)
    adj_proj_ref[...] = adj_proj.astype(BF)
    adj_norm = mm(adj_proj_ref[...], wk_ref[...], 1, 1)
    adj_norm_ref[...] = adj_norm
    gain = gain_ref[:, pl.ds(pl.multiple_of(place * bd, LANE), bd)]
    gain_part_ref[...] = jnp.sum(adj_norm * normin_ref[...].astype(F32), axis=0, keepdims=True) / gain
    for d in range(nb):
        outs[d][...] = adj_norm_ref[rows((place ^ far(d, nb)) * t, t), :].astype(BF)


def weight_grad_body(nb, ngroups, normin_ref, adj_proj_ref, gain_part_ref, *refs):
    group, _ = position(ngroups)
    tiles, own_ref = refs[: ngroups - 1], refs[ngroups - 1]
    sends, gw_ref = refs[ngroups : 2 * ngroups - 1], refs[2 * ngroups - 1]
    share, bd = own_ref.shape
    r = share // nb
    gw_ref[...] = mm(normin_ref[...], adj_proj_ref[...], 0, 0)
    tile = jnp.concatenate(
        list(split3(gain_part_ref[...])) + [jnp.zeros((SUB - 3, bd), F32)], axis=0
    ).astype(BF)
    for c in range(nb):
        at = slice(c * r, (c + 1) * r)
        own_ref[at, :] = gw_ref[rows((c * ngroups + group) * r, r), :]
        for e in range(1, ngroups):
            sends[e - 1][at, :] = gw_ref[rows((c * ngroups + (group ^ e)) * r, r), :].astype(BF)
    for e in range(1, ngroups):
        sends[e - 1][share : share + SUB, :] = tile
        high = tiles[e - 1].shape[0] * LANE // bd
        for ch in range(bd // LANE):
            sends[e - 1][share + SUB :, ch * LANE : (ch + 1) * LANE] = tiles[e - 1][
                ch * high : (ch + 1) * high, :
            ]


def weight_sum_body(nb, ngroups, bl, ext, own_ref, gain_part_ref, *refs):
    group, place = position(ngroups)
    recvs, tiles_ref = refs[: ngroups - 1], refs[ngroups - 1]
    high = tiles_ref.shape[0] * LANE // own_ref.shape[1]
    outs = refs[ngroups : ngroups + nb]
    total_ref, gains_ref, sums_ref = refs[ngroups + nb :]
    share, bd = own_ref.shape
    chunks = bd // LANE
    r = share // nb
    total = own_ref[...]
    gains_ref[group] = gain_part_ref[...]
    for e in range(1, ngroups):
        total = total + recvs[e - 1][:share, :].astype(F32)
        three = recvs[e - 1][share : share + SUB, :].astype(F32)
        gains_ref[group ^ e] = three[0:1] + three[1:2] + three[2:3]
    total_ref[...] = total.astype(BF)
    for ch in range(chunks):
        at = slice(ch * high, (ch + 1) * high)
        tile_sum = tiles_ref[at, :].astype(F32)
        for recv in recvs:
            tile_sum = tile_sum + recv[share + SUB :, ch * LANE : (ch + 1) * LANE].astype(F32)
        sums_ref[at, :] = tile_sum.astype(BF)
    gain = gains_ref[0]
    for g in range(1, ngroups):
        gain = gain + gains_ref[g]
    three = split3(gain)
    parts = [p[:, ch * LANE : (ch + 1) * LANE] for p in three for ch in range(chunks)]
    tile = jnp.concatenate(parts + [jnp.zeros((SUB - len(parts), LANE), F32)], axis=0).astype(BF)
    for d in range(nb):
        to = place ^ far(d, nb)
        for ch in range(chunks):
            outs[d][ch * r : (ch + 1) * r, :] = total_ref[rows(to * r, r), ch * LANE : (ch + 1) * LANE]
        at = chunks * r
        outs[d][at : at + bl, :] = sums_ref[rows(to * bl, bl), :]
        outs[d][at + bl : at + bl + ext, :] = sums_ref[
            pl.ds(pl.multiple_of(nb * bl + to * ext, ext), ext), :
        ]
        outs[d][at + bl + ext :, :] = tile


def input_grad_body(nb, ngroups, x_ref, grad_ref, gain_ref, *refs):
    _, place = position(ngroups)
    parts, out, adj_ref = refs[:nb], refs[nb], refs[nb + 1]
    bd = parts[0].shape[1]
    for d in range(nb):
        adj_ref[:, pl.ds(pl.multiple_of((place ^ far(d, nb)) * bd, LANE), bd)] = parts[d][...].astype(F32)
    x = x_ref[...].astype(F32)
    inv = lax.rsqrt(jnp.mean(x * x, axis=-1, keepdims=True) + EPS)
    normed = x * inv
    scaled = adj_ref[...] * gain_ref[...]
    mean = jnp.mean(scaled * normed, axis=-1, keepdims=True)
    out[...] = (grad_ref[...].astype(F32) + inv * (scaled - normed * mean)).astype(BF)


def join_body(nb, ngroups, *refs):
    _, block = position(ngroups)
    out, done_ref = refs[nb:]
    done_ref[...] = jnp.zeros(done_ref.shape, done_ref.dtype)
    bd = refs[0].shape[1]
    for d in range(nb):
        out[:, pl.ds(pl.multiple_of((block ^ far(d, nb)) * bd, LANE), bd)] = refs[d][...]


def join_weight_body(nb, ngroups, *refs):
    _, block = position(ngroups)
    gw_ref, gain_ref, left_out, right_out, by_block = refs[nb:]
    r, _, bd = gw_ref.shape
    chunks = bd // LANE
    na, bl, _ = left_out.shape
    npos, ext, _ = right_out.shape
    at = chunks * r
    left = refs[0][at : at + bl, :].astype(F32)
    right = refs[0][at + bl : at + bl + ext, :].astype(F32)
    for d in range(1, nb):
        left = left + refs[d][at : at + bl, :].astype(F32)
        right = right + refs[d][at + bl : at + bl + ext, :].astype(F32)
    for j in range(na):
        left_out[j] = left[:, j * bl : (j + 1) * bl]
    for j in range(npos):
        right_out[j] = right[:, j * ext : (j + 1) * ext]
    for d in range(nb):
        k = block ^ far(d, nb)
        by_block[k] = unpack(refs[d], r, chunks).astype(F32)
        tile = refs[d][at + bl + ext :, :].astype(F32)
        for ch in range(chunks):
            gain_ref[:, pl.ds(pl.multiple_of(k * bd + ch * LANE, LANE), LANE)] = (
                tile[ch : ch + 1] + tile[chunks + ch : chunks + ch + 1] + tile[2 * chunks + ch : 2 * chunks + ch + 1]
            )
    for k in range(nb):
        gw_ref[:, k, :] = by_block[k]


def arrived_body(out_ref):
    out_ref[...] = jnp.zeros(out_ref.shape, out_ref.dtype)


def store_body(x_ref, out_ref, done_ref):
    out_ref[...] = x_ref[...]
    done_ref[...] = jnp.zeros(done_ref.shape, done_ref.dtype)


def shards(act_in, saved_in, grad_in, gain, weight, left_blocks, right_blocks):
    nseq = lax.axis_size("seq")
    npipe = lax.axis_size("pipe")
    _, t, width = act_in.shape
    _, r, nb, bd = weight.shape
    ngroups = nseq // nb
    bl = left_blocks.shape[2]
    ext = right_blocks.shape[2]
    npos = right_blocks.shape[1]
    chunks = bd // LANE
    tg = nb * t
    r4 = chunks * r
    nq = bl // SUB
    n = SUB * ext

    def within(parts):
        return [parts[0]] + [
            lax.ppermute(parts[d], "seq", [(s, s ^ (far(d, nb) * ngroups)) for s in range(nseq)])
            for d in range(1, nb)
        ]

    def across(block, e):
        return lax.ppermute(block, "seq", [(s, s ^ e) for s in range(nseq)])

    def gathered(block):
        return [block] + [across(block, e) for e in range(1, ngroups)]

    def handed(parts, step):
        return [
            lax.ppermute(
                parts[d],
                ("pipe", "seq"),
                [
                    (p * nseq + s, (p + step) % npipe * nseq + (s ^ (far(d, nb) * ngroups)))
                    for p in range(npipe)
                    for s in range(nseq)
                ],
            )
            for d in range(nb)
        ]

    def exchanged(parts):
        return list(parts[:1]) + [across(parts[e], e) for e in range(1, ngroups)]

    part = functools.partial
    def run(name, body, outs, scratch=(), direct=0):
        return call(body, outs, scratch, direct, name)

    pack = part(pack_tokens_body, nb, ngroups)
    norm = part(norm_body, nb, ngroups)
    join = part(join_body, nb, ngroups)
    scaled_msgs = [sds((chunks * t + SUB, LANE))] * nb
    tokens = [sds((tg, bd))]
    pieces = [sds((t, bd))] * nb
    rows_of = bd // ngroups
    part_of = bd // ngroups
    shares = [sds((tg, part_of))] * ngroups
    every = [sds((ngroups * tg, part_of))]
    by_position = [sds((nq, n, part_of))]

    def scratch(structs):
        return [pltpu.VMEM(s.shape, s.dtype) for s in structs]

    w_msgs = run("pack_weight", part(pack_weight_body, nb, ngroups), [sds((r4 + bl + ext, LANE))] * nb)(
        jnp.transpose(weight[0], (1, 0, 2)), left_blocks[0], right_blocks[0]
    )
    grad_shares = run(
        "split_grad", part(split_features_body, nb, ngroups), [sds((nb, t, part_of))] * ngroups
    )(grad_in[0], after=w_msgs[:1])
    sto_msgs = run("pack_saved", part(pack, True), scaled_msgs)(saved_in[0], after=grad_shares[:1])
    early = sto_msgs[:1]
    w_msgs, grad_shares, sto_msgs = within(w_msgs), exchanged(grad_shares), within(sto_msgs)
    (relay,) = run("relay", part(relay_body, nb, ngroups, r4, ext), [sds((nb * (r4 + ext + bl), LANE))])(
        *w_msgs, after=early
    )
    relays = gathered(relay)
    grad_msgs = run("pack_grad", part(pack_shares_body, nb, ngroups), [sds((ngroups * t, part_of))] * nb)(
        *grad_shares, after=[relay]
    )
    (sto_normin,) = run("norm_saved", norm, tokens)(*sto_msgs, gain, after=grad_msgs[:1])
    wk, mq, bd_left = run(
        "assemble",
        part(assemble_body, nb, ngroups, r, ext, bl),
        [sds((bd, bd)), sds((nq, n, n)), sds((nseq, LANE, LANE))],
        [pltpu.VMEM((nseq, ext, LANE), BF)],
    )(*relays, after=[sto_normin])
    sto_shares = run("project_saved", part(project_shares_body, ngroups), shares)(sto_normin, wk)
    cur_msgs = run("pack_act", part(pack, True), scaled_msgs)(act_in[0], after=sto_shares[:1])
    grad_msgs = within(grad_msgs)
    (grad,) = run("take_grad", part(take_grad_body, nb, ngroups), every)(*grad_msgs, after=cur_msgs[:1])
    sto_shares, cur_msgs = exchanged(sto_shares), within(cur_msgs)
    sto_proj, sto_f, sto_mixed = run(
        "mix_saved", part(mix_shares_body, ngroups, bl), every + by_position + every, scratch(every)
    )(*sto_shares, mq, bd_left, after=[grad])
    *adj_shares, adj_f, adj_first = run(
        "backward", part(backward_body, nb, ngroups, bl), shares + by_position + every, scratch(every)
    )(grad, sto_proj, sto_mixed, mq, bd_left)
    adj_wait = adj_shares[:1]
    adj_shares = exchanged(adj_shares)
    tiles = run(
        "factor_grads",
        part(factor_grads_body, nb, ngroups, bl, ext),
        [sds((nb * (bl + ext), LANE))] * ngroups,
        scratch([sds((ngroups, nb * ext, LANE)), sds((ngroups, nb * bl, LANE))]),
    )(sto_f, adj_f, adj_first, sto_proj, after=adj_wait)
    tiles_wait = tiles[:1]
    (cur_normin,) = run("norm_act", norm, tokens)(*cur_msgs, gain, after=tiles_wait)
    cur_proj, cur_first = run("project_act", part(project_body, nb, ngroups), tokens * 2)(
        cur_normin, wk, bd_left
    )
    cur_firsts = gathered(cur_first)
    adj_proj, gain_part, *adj_parts = run(
        "adj_norm",
        part(adj_norm_body, nb, ngroups),
        tokens + [sds((1, bd), F32)] + pieces,
        scratch([sds((tg, bd), F32)]),
    )(sto_normin, wk, gain, *adj_shares, after=[cur_first])
    adj_wait = adj_parts[:1]
    adj_parts = within(adj_parts)
    own_gw, *sends = run(
        "weight_grad",
        part(weight_grad_body, nb, ngroups),
        [sds((rows_of, bd), F32)] + [sds((rows_of + SUB + nb * (bl + ext) // chunks, bd))] * (ngroups - 1),
        scratch([sds((bd, bd), F32)]),
    )(sto_normin, adj_proj, gain_part, *tiles[1:], after=adj_wait)
    recvs = [across(sends[e - 1], e) for e in range(1, ngroups)]
    (adj_arrived,) = run("far_adj", arrived_body, [sds((8, LANE), F32)])(after=[own_gw, *adj_parts[1:3]])
    (cur_mixed,) = run(
        "mix_act", part(mix_body, ngroups, bl), tokens, scratch([sds((nq, n, bd))])
    )(*cur_firsts, mq, after=[adj_arrived])
    out_parts = run("output", part(output_body, nb, ngroups), pieces)(cur_mixed, cur_proj, *cur_msgs)
    (adj_x,) = run(
        "input_grad", part(input_grad_body, nb, ngroups), [sds((t, width))], scratch([sds((t, width), F32)])
    )(saved_in[0], grad_in[0], gain, *adj_parts, after=out_parts[:1])
    gw_parts = run(
        "weight_sum",
        part(weight_sum_body, nb, ngroups, bl, ext),
        [sds((r4 + bl + ext + SUB, LANE))] * nb,
        scratch([sds((rows_of, bd)), sds((ngroups, 1, bd), F32), sds((nb * (bl + ext), LANE))]),
    )(own_gw, gain_part, *recvs, tiles[0], after=[adj_x])
    gw_wait = gw_parts[:1]
    gw_parts = within(gw_parts)
    out_parts = handed(out_parts, 1)
    grad_handed = lax.ppermute(adj_x, "pipe", [(p, (p - 1) % npipe) for p in range(npipe)])
    handed_on, done = run("join_out", join, [sds((t, width)), sds((8, LANE), F32)])(
        *out_parts, after=gw_wait
    )
    grad_handed, done = run("store", store_body, [sds((t, width)), sds((8, LANE), F32)])(
        grad_handed, after=[done]
    )
    weight_grad, gain_grad, left_grad, right_grad = run(
        "join_weight",
        part(join_weight_body, nb, ngroups),
        [
            sds((r, nb, bd), F32),
            sds((1, width), F32),
            sds((left_blocks.shape[1], bl, bl), F32),
            sds((npos, ext, ext), F32),
        ],
        scratch([sds((nb, r, bd), F32)]),
    )(*gw_parts, after=[done])
    return (
        handed_on[None],
        grad_handed[None],
        weight_grad[None],
        gain_grad,
        left_grad[None],
        right_grad[None],
    )


def solution(mesh):
    tokens = P("pipe", "seq", None)
    factor = P("pipe", "seq", None, None)
    return jax.shard_map(
        shards,
        mesh=mesh,
        in_specs=(tokens, tokens, tokens, P("pipe", None), factor, factor, factor),
        out_specs=(tokens, tokens, factor, P("pipe", None), factor, factor),
        check_vma=False,
    )
```

```python
import functools

import jax
import jax.numpy as jnp
from jax import lax
from jax.experimental import pallas as pl
from jax.experimental.pallas import tpu as pltpu
from jax.sharding import PartitionSpec as P

BF = jnp.bfloat16
F32 = jnp.float32
LANE = 128
SUB = 16
EPS = 1e-06
COST = {"relay": 3, "far_saved": 3, "far_grad": 6.0, "norm_act": 3, "join_weight": 3, "join_out": 5, "far_adj": 2}
VMEM = 48 * 1024 * 1024


def position(ngroups):
    me = lax.axis_index("seq")
    return me % ngroups, me // ngroups


def far(d, nb):
    return (nb - d) % nb


def natural(pos, nb, ngroups, na):
    return ((pos // na % nb) * ngroups + pos // (nb * na)) * na + pos % na


def split3(x):
    hi = x.astype(BF).astype(F32)
    mid = (x - hi).astype(BF).astype(F32)
    return hi, mid, x - hi - mid


def eye(n):
    return lax.broadcasted_iota(jnp.int32, (n, n), 0) == lax.broadcasted_iota(jnp.int32, (n, n), 1)


def to_row(col):
    return jnp.sum(jnp.where(eye(col.shape[0]), col, 0.0), axis=0, keepdims=True)


def to_col(row):
    return jnp.sum(jnp.where(eye(row.shape[1]), row, 0.0), axis=1, keepdims=True)


def mm(a, b, ca=1, cb=0):
    return lax.dot_general(a, b, (((ca,), (cb,)), ((), ())), preferred_element_type=F32)


def rows(start, size):
    return pl.ds(pl.multiple_of(start, size), size)


def call(body, outs, scratch, direct, name):
    def run(*args, after=()):
        nin, nwait = len(args), len(after)
        vmem, anywhere = pl.BlockSpec(memory_space=pltpu.VMEM), pl.BlockSpec(memory_space=pl.ANY)

        def without_waits(*refs):
            return body(*refs[:nin], *refs[nin + nwait :])

        return pl.pallas_call(
            without_waits,
            out_shape=list(outs),
            in_specs=[anywhere] * direct + [vmem] * (nin - direct) + [anywhere] * nwait,
            out_specs=[pl.BlockSpec(memory_space=pltpu.HBM)] * direct + [vmem] * (len(outs) - direct),
            scratch_shapes=list(scratch),
            compiler_params=pltpu.CompilerParams(vmem_limit_bytes=VMEM),
            cost_estimate=pl.CostEstimate(
                flops=int(COST.get(name, 0.0) * 1e9), bytes_accessed=0, transcendentals=0
            ),
            name=name,
        )(*args, *after)

    return run


def sds(shape, dtype=BF):
    return jax.ShapeDtypeStruct(shape, dtype)


def pack_weight_body(nb, ngroups, w_ref, l_ref, r_ref, *outs):
    _, block = position(ngroups)
    r, bd = w_ref.shape[1], w_ref.shape[2]
    chunks = bd // LANE
    bl, ext = l_ref.shape[1], r_ref.shape[1]
    left = jnp.concatenate([l_ref[j].astype(F32) for j in range(l_ref.shape[0])], axis=1).astype(BF)
    right = jnp.concatenate([r_ref[j].astype(F32) for j in range(r_ref.shape[0])], axis=1).astype(BF)
    for d in range(nb):
        for ch in range(chunks):
            outs[d][ch * r : (ch + 1) * r, :] = w_ref[block ^ far(d, nb), :, ch * LANE : (ch + 1) * LANE]
        outs[d][chunks * r : chunks * r + bl, :] = left
        outs[d][chunks * r + bl :, :] = right


def pack_tokens_body(nb, ngroups, with_scale, x_ref, *outs):
    _, block = position(ngroups)
    t, width = x_ref.shape
    bd = width // nb
    chunks = bd // LANE
    if with_scale:
        x = x_ref[...].astype(F32)
        inv = lax.rsqrt(jnp.mean(x * x, axis=-1, keepdims=True) + EPS)
        parts = split3(to_row(inv))
        tile = jnp.concatenate(list(parts) + [jnp.zeros((SUB - 3, t), F32)], axis=0).astype(BF)
    for d in range(nb):
        for ch in range(chunks):
            lanes = pl.ds(pl.multiple_of((block ^ far(d, nb)) * bd + ch * LANE, LANE), LANE)
            outs[d][ch * t : (ch + 1) * t, :] = x_ref[:, lanes]
        if with_scale:
            outs[d][chunks * t :, :] = tile


def pick(n, part_of, part):
    row = lax.broadcasted_iota(jnp.int32, (n, part_of), 0)
    col = lax.broadcasted_iota(jnp.int32, (n, part_of), 1)
    return jnp.where(row == part * part_of + col, 1.0, 0.0).astype(BF)


def share_of(ref, first, n, part_of, part):
    if part_of % LANE == 0:
        return ref[:, pl.ds(pl.multiple_of(first + part * part_of, LANE), part_of)]
    return mm(ref[:, first : first + n], pick(n, part_of, part)).astype(BF)


def split_features_body(nb, ngroups, x_ref, *outs):
    group, _ = position(ngroups)
    part_of = outs[0].shape[2]
    bd = x_ref.shape[1] // nb
    for e in range(ngroups):
        for k in range(nb):
            outs[e][k] = share_of(x_ref, k * bd, bd, part_of, group ^ e)


def pack_shares_body(nb, ngroups, which, *refs):
    group, place = position(ngroups)
    shares, outs = refs[:ngroups], refs[ngroups:]
    t = shares[0].shape[1]
    for d, out in zip(which, outs):
        for e in range(ngroups):
            out[rows((group ^ e) * t, t), :] = shares[e][place ^ far(d, nb)]


def relay_body(nb, ngroups, r4, ext, *refs):
    _, place = position(ngroups)
    out = refs[nb]
    bl = refs[0].shape[0] - r4 - ext
    for d in range(nb):
        to = place ^ far(d, nb)
        out[rows(to * r4, r4), :] = refs[d][:r4, :]
        out[pl.ds(pl.multiple_of(nb * r4 + to * ext, ext), ext), :] = refs[d][r4 + bl :, :]
        out[pl.ds(pl.multiple_of(nb * (r4 + ext) + to * bl, bl), bl), :] = refs[d][r4 : r4 + bl, :]


def expand_matrix(ext, nb, ngroups, na):
    n = SUB * ext
    row = lax.broadcasted_iota(jnp.int32, (n, n), 0)
    col = lax.broadcasted_iota(jnp.int32, (n, n), 1)
    return jnp.where((row // ext == col % SUB) & (row % ext == natural(col // SUB, nb, ngroups, na)), 1.0, 0.0).astype(BF)


def same_position(n):
    row = lax.broadcasted_iota(jnp.int32, (n, n), 0)
    col = lax.broadcasted_iota(jnp.int32, (n, n), 1)
    return row % SUB == col % SUB


def assemble_body(nb, ngroups, r, ext, bl, *refs):
    group, _ = position(ngroups)
    na = LANE // bl
    relays = refs[:ngroups]
    wk_ref, mq_ref, bd_ref, all_ref = refs[ngroups:]
    chunks = wk_ref.shape[1] // LANE
    r4 = chunks * r
    for e in range(ngroups):
        g = group ^ e
        for c in range(nb):
            for ch in range(chunks):
                wk_ref[rows((c * ngroups + g) * r, r), ch * LANE : (ch + 1) * LANE] = relays[e][
                    c * r4 + ch * r : c * r4 + (ch + 1) * r, :
                ]
            all_ref[c * ngroups + g] = relays[e][nb * r4 + c * ext : nb * r4 + (c + 1) * ext, :]
    nq = mq_ref.shape[0]
    per = nb * ngroups // nq
    n = SUB * ext
    turn = expand_matrix(ext, nb, ngroups, na)
    spread = jnp.where(
        natural(lax.broadcasted_iota(jnp.int32, (n, ext), 0) // SUB, nb, ngroups, na)
        == lax.broadcasted_iota(jnp.int32, (n, ext), 1),
        1.0,
        0.0,
    ).astype(BF)
    same = same_position(n)
    for q in range(nq):
        tiles = jnp.concatenate([all_ref[q * per + i] for i in range(per)], axis=1)
        wide = mm(tiles, turn).astype(BF)
        mq_ref[q] = jnp.where(same, mm(spread, wide), 0.0).astype(BF)
    half_row = lax.broadcasted_iota(jnp.int32, (LANE, LANE), 0) // bl
    half_col = lax.broadcasted_iota(jnp.int32, (LANE, LANE), 1) // bl
    for e in range(ngroups):
        for c in range(nb):
            at = nb * (r4 + ext) + c * bl
            both = jnp.concatenate([relays[e][at : at + bl, :].astype(F32)] * na, axis=0)
            bd_ref[(group ^ e) * nb + c] = jnp.where(half_row == half_col, both, 0.0).astype(BF)


def unpack(msg, t, chunks):
    return jnp.concatenate([msg[ch * t : (ch + 1) * t, :] for ch in range(chunks)], axis=1)


def scale_of(msg, t, chunks):
    tile = msg[chunks * t : chunks * t + SUB, :].astype(F32)
    return to_col(tile[0:1] + tile[1:2] + tile[2:3])


def norm_body(nb, ngroups, *refs):
    _, place = position(ngroups)
    msgs = refs[:nb]
    gain_ref, normin_ref = refs[nb:]
    t = LANE
    bd = normin_ref.shape[1]
    chunks = bd // LANE
    gain = gain_ref[:, pl.ds(pl.multiple_of(place * bd, LANE), bd)]
    for d in range(nb):
        x = unpack(msgs[d], t, chunks).astype(F32)
        normed = x * scale_of(msgs[d], t, chunks)
        normin_ref[rows((place ^ far(d, nb)) * t, t), :] = (normed * gain).astype(BF)


def project_body(nb, ngroups, normin_ref, wk_ref, bd_ref, proj_ref, first_ref):
    group, _ = position(ngroups)
    t = LANE
    proj_ref[...] = mm(normin_ref[...], wk_ref[...]).astype(BF)
    for c in range(nb):
        at = slice(c * t, (c + 1) * t)
        first_ref[at, :] = mm(bd_ref[group * nb + c], proj_ref[at, :]).astype(BF)


def project_shares_body(ngroups, normin_ref, wk_ref, *refs):
    group, _ = position(ngroups)
    outs, proj_ref = refs[:ngroups], refs[ngroups]
    bd = wk_ref.shape[0]
    proj_ref[...] = mm(normin_ref[...], wk_ref[...]).astype(BF)
    for e in range(ngroups):
        outs[e][...] = share_of(proj_ref, 0, bd, bd // ngroups, group ^ e)


def gather_positions(group, bl, parts, out_ref):
    blocks = parts[0].shape[0] // bl
    for e, part in enumerate(parts):
        base = (group ^ e) * blocks * SUB
        for q in range(bl // SUB):
            for a in range(blocks):
                out_ref[q, pl.ds(pl.multiple_of(base + a * SUB, SUB), SUB), :] = part[
                    a * bl + q * SUB : a * bl + (q + 1) * SUB, :
                ]


def mix_body(ngroups, bl, *refs):
    group, _ = position(ngroups)
    firsts = refs[:ngroups]
    mq_ref, mixed_ref, f_ref = refs[ngroups:]
    gather_positions(group, bl, firsts, f_ref)
    blocks = firsts[0].shape[0] // bl
    own = rows(group * blocks * SUB, blocks * SUB)
    for q in range(bl // SUB):
        mixed = mm(mq_ref[q, own, :], f_ref[q]).astype(BF)
        for a in range(blocks):
            mixed_ref[a * bl + q * SUB : a * bl + (q + 1) * SUB, :] = mixed[a * SUB : (a + 1) * SUB, :]


def output_body(nb, ngroups, mixed_ref, proj_ref, *refs):
    _, place = position(ngroups)
    msgs, outs = refs[:nb], refs[nb:]
    t = LANE
    chunks = proj_ref.shape[1] // LANE
    for d in range(nb):
        at = rows((place ^ far(d, nb)) * t, t)
        x = unpack(msgs[d], t, chunks).astype(F32)
        outs[d][...] = (x + proj_ref[at, :].astype(F32) * mixed_ref[at, :].astype(F32)).astype(BF)


def to_positions(x_ref, out_ref, bl):
    for q in range(bl // SUB):
        for a in range(x_ref.shape[0] // bl):
            out_ref[q, a * SUB : (a + 1) * SUB, :] = x_ref[a * bl + q * SUB : a * bl + (q + 1) * SUB, :]


def from_positions(x, q, out_ref, bl):
    for a in range(out_ref.shape[0] // bl):
        out_ref[a * bl + q * SUB : a * bl + (q + 1) * SUB, :] = x[a * SUB : (a + 1) * SUB, :]


def mix_shares_body(ngroups, bl, *refs):
    group, _ = position(ngroups)
    parts = refs[:ngroups]
    mq_ref, bd_ref, proj_ref, f_ref, mixed_ref, first_ref = refs[ngroups:]
    t = LANE
    tg = parts[0].shape[0]
    for e in range(ngroups):
        proj_ref[rows((group ^ e) * tg, tg), :] = parts[e][...]
    for c in range(bd_ref.shape[0]):
        at = slice(c * t, (c + 1) * t)
        first_ref[at, :] = mm(bd_ref[c], proj_ref[at, :]).astype(BF)
    to_positions(first_ref, f_ref, bl)
    for q in range(bl // SUB):
        from_positions(mm(mq_ref[q], f_ref[q]).astype(BF), q, mixed_ref, bl)


def take_grad_body(nb, ngroups, *refs):
    _, place = position(ngroups)
    grad_ref = refs[nb]
    t = LANE
    for d in range(nb):
        for g in range(ngroups):
            grad_ref[rows((g * nb + (place ^ far(d, nb))) * t, t), :] = refs[d][g * t : (g + 1) * t, :]


def backward_body(nb, ngroups, bl, *refs):
    group, _ = position(ngroups)
    grad_ref, proj_ref, mixed_ref, mq_ref, bd_ref = refs[:5]
    outs = refs[5 : 5 + ngroups]
    a_ref, adj_first_ref, adj_ref = refs[5 + ngroups :]
    t = LANE
    adj_ref[...] = (grad_ref[...].astype(F32) * proj_ref[...].astype(F32)).astype(BF)
    to_positions(adj_ref, a_ref, bl)
    for q in range(bl // SUB):
        from_positions(mm(mq_ref[q], a_ref[q], 0, 0).astype(BF), q, adj_first_ref, bl)
    for c in range(bd_ref.shape[0]):
        at = slice(c * t, (c + 1) * t)
        grad = grad_ref[at, :].astype(F32)
        mixed = mixed_ref[at, :].astype(F32)
        adj_ref[at, :] = (grad * mixed + mm(bd_ref[c], adj_first_ref[at, :], 0, 0)).astype(BF)
    tg = nb * t
    for e in range(ngroups):
        outs[e][...] = adj_ref[rows((group ^ e) * tg, tg), :]


def factor_grads_body(nb, ngroups, bl, ext, f_ref, a_ref, adj_first_ref, proj_ref, *refs):
    group, _ = position(ngroups)
    outs, right_ref, left_ref = refs[:ngroups], refs[ngroups], refs[ngroups + 1]
    na = LANE // bl
    t = LANE
    nq = f_ref.shape[0]
    n = SUB * ext
    upper = lax.broadcasted_iota(jnp.int32, (bl, LANE), 1) < bl
    for g in range(ngroups):
        for c in range(nb):
            at = slice((g * nb + c) * t, (g * nb + c + 1) * t)
            both = mm(adj_first_ref[at, :], proj_ref[at, :], 1, 1)
            left_ref[g, c * bl : (c + 1) * bl, :] = jnp.where(upper, both[:bl, :], both[bl:, :]).astype(BF)
    turn = expand_matrix(ext, nb, ngroups, na)
    same = same_position(n)
    order = jnp.where(
        natural(lax.broadcasted_iota(jnp.int32, (ext, ext), 0), nb, ngroups, na)
        == lax.broadcasted_iota(jnp.int32, (ext, ext), 1),
        1.0,
        0.0,
    ).astype(BF)
    per = nb * ngroups // nq
    for q in range(nq):
        pairs = jnp.where(same, mm(a_ref[q], f_ref[q], 1, 1), 0.0)
        summed = jnp.sum(pairs.reshape(ext, SUB, n), axis=1).astype(BF)
        turned = mm(order, mm(summed, turn, 1, 1).astype(BF), 0, 0).astype(BF)
        for i in range(per):
            s = q * per + i
            right_ref[s % ngroups, (s // ngroups) * ext : (s // ngroups + 1) * ext, :] = turned[
                :, i * LANE : (i + 1) * LANE
            ]
    for e in range(ngroups):
        outs[e][: nb * bl, :] = left_ref[group ^ e]
        outs[e][nb * bl :, :] = right_ref[group ^ e]


def adj_norm_body(nb, ngroups, normin_ref, wk_ref, gain_ref, *refs):
    group, place = position(ngroups)
    shares, rest = refs[:ngroups], refs[ngroups:]
    adj_proj_ref, gain_part_ref, outs, adj_norm_ref = rest[0], rest[1], rest[2 : 2 + nb], rest[2 + nb]
    bd = wk_ref.shape[0]
    t = LANE
    part_of = bd // ngroups
    if part_of % LANE == 0:
        for e in range(ngroups):
            adj_proj_ref[:, pl.ds(pl.multiple_of((group ^ e) * part_of, LANE), part_of)] = shares[e][...]
    else:
        adj_proj = jnp.zeros(adj_proj_ref.shape, F32)
        for e in range(ngroups):
            adj_proj = adj_proj + mm(shares[e][...], pick(bd, part_of, group ^ e), 1, 1)
        adj_proj_ref[...] = adj_proj.astype(BF)
    adj_norm = mm(adj_proj_ref[...], wk_ref[...], 1, 1)
    adj_norm_ref[...] = adj_norm
    gain = gain_ref[:, pl.ds(pl.multiple_of(place * bd, LANE), bd)]
    gain_part_ref[...] = jnp.sum(adj_norm * normin_ref[...].astype(F32), axis=0, keepdims=True) / gain
    for d in range(nb):
        outs[d][...] = adj_norm_ref[rows((place ^ far(d, nb)) * t, t), :].astype(BF)


def weight_grad_body(nb, ngroups, normin_ref, adj_proj_ref, gain_part_ref, *refs):
    group, _ = position(ngroups)
    tiles, own_ref = refs[: ngroups - 1], refs[ngroups - 1]
    sends, gw_ref = refs[ngroups : 2 * ngroups - 1], refs[2 * ngroups - 1]
    share, bd = own_ref.shape
    r = share // nb
    gw_ref[...] = mm(normin_ref[...], adj_proj_ref[...], 0, 0)
    tile = jnp.concatenate(
        list(split3(gain_part_ref[...])) + [jnp.zeros((SUB - 3, bd), F32)], axis=0
    ).astype(BF)
    for c in range(nb):
        at = slice(c * r, (c + 1) * r)
        own_ref[at, :] = gw_ref[rows((c * ngroups + group) * r, r), :]
        for e in range(1, ngroups):
            sends[e - 1][at, :] = gw_ref[rows((c * ngroups + (group ^ e)) * r, r), :].astype(BF)
    for e in range(1, ngroups):
        sends[e - 1][share : share + SUB, :] = tile
        high = tiles[e - 1].shape[0] * LANE // bd
        for ch in range(bd // LANE):
            sends[e - 1][share + SUB :, ch * LANE : (ch + 1) * LANE] = tiles[e - 1][
                ch * high : (ch + 1) * high, :
            ]


def weight_sum_body(nb, ngroups, bl, ext, own_ref, gain_part_ref, *refs):
    group, place = position(ngroups)
    recvs, tiles_ref = refs[: ngroups - 1], refs[ngroups - 1]
    high = tiles_ref.shape[0] * LANE // own_ref.shape[1]
    outs = refs[ngroups : ngroups + nb]
    total_ref, gains_ref, sums_ref = refs[ngroups + nb :]
    share, bd = own_ref.shape
    chunks = bd // LANE
    r = share // nb
    total = own_ref[...]
    gains_ref[group] = gain_part_ref[...]
    for e in range(1, ngroups):
        total = total + recvs[e - 1][:share, :].astype(F32)
        three = recvs[e - 1][share : share + SUB, :].astype(F32)
        gains_ref[group ^ e] = three[0:1] + three[1:2] + three[2:3]
    total_ref[...] = total.astype(BF)
    for ch in range(chunks):
        at = slice(ch * high, (ch + 1) * high)
        tile_sum = tiles_ref[at, :].astype(F32)
        for recv in recvs:
            tile_sum = tile_sum + recv[share + SUB :, ch * LANE : (ch + 1) * LANE].astype(F32)
        sums_ref[at, :] = tile_sum.astype(BF)
    gain = gains_ref[0]
    for g in range(1, ngroups):
        gain = gain + gains_ref[g]
    three = split3(gain)
    parts = [p[:, ch * LANE : (ch + 1) * LANE] for p in three for ch in range(chunks)]
    tile = jnp.concatenate(parts + [jnp.zeros((SUB - len(parts), LANE), F32)], axis=0).astype(BF)
    for d in range(nb):
        to = place ^ far(d, nb)
        for ch in range(chunks):
            outs[d][ch * r : (ch + 1) * r, :] = total_ref[rows(to * r, r), ch * LANE : (ch + 1) * LANE]
        at = chunks * r
        outs[d][at : at + bl, :] = sums_ref[rows(to * bl, bl), :]
        outs[d][at + bl : at + bl + ext, :] = sums_ref[
            pl.ds(pl.multiple_of(nb * bl + to * ext, ext), ext), :
        ]
        outs[d][at + bl + ext :, :] = tile


def input_grad_body(nb, ngroups, x_ref, grad_ref, gain_ref, *refs):
    _, place = position(ngroups)
    parts, out, adj_ref = refs[:nb], refs[nb], refs[nb + 1]
    bd = parts[0].shape[1]
    for d in range(nb):
        adj_ref[:, pl.ds(pl.multiple_of((place ^ far(d, nb)) * bd, LANE), bd)] = parts[d][...].astype(F32)
    x = x_ref[...].astype(F32)
    inv = lax.rsqrt(jnp.mean(x * x, axis=-1, keepdims=True) + EPS)
    normed = x * inv
    scaled = adj_ref[...] * gain_ref[...]
    mean = jnp.mean(scaled * normed, axis=-1, keepdims=True)
    out[...] = (grad_ref[...].astype(F32) + inv * (scaled - normed * mean)).astype(BF)


def join_body(nb, ngroups, *refs):
    _, block = position(ngroups)
    out, done_ref = refs[nb:]
    done_ref[...] = jnp.zeros(done_ref.shape, done_ref.dtype)
    bd = refs[0].shape[1]
    for d in range(nb):
        out[:, pl.ds(pl.multiple_of((block ^ far(d, nb)) * bd, LANE), bd)] = refs[d][...]


def join_weight_body(nb, ngroups, *refs):
    _, block = position(ngroups)
    gw_ref, gain_ref, left_out, right_out, by_block = refs[nb:]
    r, _, bd = gw_ref.shape
    chunks = bd // LANE
    na, bl, _ = left_out.shape
    npos, ext, _ = right_out.shape
    at = chunks * r
    left = refs[0][at : at + bl, :].astype(F32)
    right = refs[0][at + bl : at + bl + ext, :].astype(F32)
    for d in range(1, nb):
        left = left + refs[d][at : at + bl, :].astype(F32)
        right = right + refs[d][at + bl : at + bl + ext, :].astype(F32)
    for j in range(na):
        left_out[j] = left[:, j * bl : (j + 1) * bl]
    for j in range(npos):
        right_out[j] = right[:, j * ext : (j + 1) * ext]
    for d in range(nb):
        k = block ^ far(d, nb)
        by_block[k] = unpack(refs[d], r, chunks).astype(F32)
        tile = refs[d][at + bl + ext :, :].astype(F32)
        for ch in range(chunks):
            gain_ref[:, pl.ds(pl.multiple_of(k * bd + ch * LANE, LANE), LANE)] = (
                tile[ch : ch + 1] + tile[chunks + ch : chunks + ch + 1] + tile[2 * chunks + ch : 2 * chunks + ch + 1]
            )
    for k in range(nb):
        gw_ref[:, k, :] = by_block[k]


def arrived_body(out_ref):
    out_ref[...] = jnp.zeros(out_ref.shape, out_ref.dtype)


def store_body(x_ref, out_ref, done_ref):
    out_ref[...] = x_ref[...]
    done_ref[...] = jnp.zeros(done_ref.shape, done_ref.dtype)


def shards(act_in, saved_in, grad_in, gain, weight, left_blocks, right_blocks):
    nseq = lax.axis_size("seq")
    npipe = lax.axis_size("pipe")
    _, t, width = act_in.shape
    _, r, nb, bd = weight.shape
    ngroups = nseq // nb
    bl = left_blocks.shape[2]
    ext = right_blocks.shape[2]
    npos = right_blocks.shape[1]
    chunks = bd // LANE
    tg = nb * t
    r4 = chunks * r
    nq = bl // SUB
    n = SUB * ext

    def within(parts):
        return [parts[0]] + [
            lax.ppermute(parts[d], "seq", [(s, s ^ (far(d, nb) * ngroups)) for s in range(nseq)])
            for d in range(1, nb)
        ]

    def across(block, e):
        return lax.ppermute(block, "seq", [(s, s ^ e) for s in range(nseq)])

    def gathered(block):
        return [block] + [across(block, e) for e in range(1, ngroups)]

    def handed(parts, step):
        return [
            lax.ppermute(
                parts[d],
                ("pipe", "seq"),
                [
                    (p * nseq + s, (p + step) % npipe * nseq + (s ^ (far(d, nb) * ngroups)))
                    for p in range(npipe)
                    for s in range(nseq)
                ],
            )
            for d in range(nb)
        ]

    def exchanged(parts):
        return list(parts[:1]) + [across(parts[e], e) for e in range(1, ngroups)]

    part = functools.partial
    def run(name, body, outs, scratch=(), direct=0):
        return call(body, outs, scratch, direct, name)

    def arrived(name, *parts):
        return run(name, arrived_body, [sds((8, LANE), F32)])(after=parts)

    pack = part(pack_tokens_body, nb, ngroups)
    norm = part(norm_body, nb, ngroups)
    join = part(join_body, nb, ngroups)
    scaled_msgs = [sds((chunks * t + SUB, LANE))] * nb
    tokens = [sds((tg, bd))]
    pieces = [sds((t, bd))] * nb
    rows_of = bd // ngroups
    part_of = bd // ngroups
    shares = [sds((tg, part_of))] * ngroups
    every = [sds((ngroups * tg, part_of))]
    by_position = [sds((nq, n, part_of))]

    def scratch(structs):
        return [pltpu.VMEM(s.shape, s.dtype) for s in structs]

    w_msgs = run("pack_weight", part(pack_weight_body, nb, ngroups), [sds((r4 + bl + ext, LANE))] * nb)(
        jnp.transpose(weight[0], (1, 0, 2)), left_blocks[0], right_blocks[0]
    )
    grad_shares = run(
        "split_grad", part(split_features_body, nb, ngroups), [sds((nb, t, part_of))] * ngroups
    )(grad_in[0], after=w_msgs[:1])
    sto_msgs = run("pack_saved", part(pack, True), scaled_msgs)(saved_in[0], after=grad_shares[:1])
    early = sto_msgs[:1]
    w_msgs, grad_shares, sto_msgs = within(w_msgs), exchanged(grad_shares), within(sto_msgs)
    (relay,) = run("relay", part(relay_body, nb, ngroups, r4, ext), [sds((nb * (r4 + ext + bl), LANE))])(
        *w_msgs, after=early
    )
    relays = gathered(relay)
    def pack_grad(name, which, after):
        body = part(pack_shares_body, nb, ngroups, which)
        return run(name, body, [sds((ngroups * t, part_of))] * len(which))(*grad_shares, after=[after])

    grad_msgs = pack_grad("pack_grad", range(nb - 1), relay)
    (sto_arrived,) = arrived("far_saved", grad_msgs[0], *sto_msgs[1:3])
    (sto_normin,) = run("norm_saved", norm, tokens)(*sto_msgs, gain, after=[sto_arrived])
    wk, mq, bd_left = run(
        "assemble",
        part(assemble_body, nb, ngroups, r, ext, bl),
        [sds((bd, bd)), sds((nq, n, n)), sds((nseq, LANE, LANE))],
        [pltpu.VMEM((nseq, ext, LANE), BF)],
    )(*relays, after=[sto_normin])
    sto_shares = run(
        "project_saved", part(project_shares_body, ngroups), shares, scratch(tokens)
    )(sto_normin, wk)
    grad_near = pack_grad("pack_grad_near", [nb - 1], sto_shares[0])
    cur_msgs = run("pack_act", part(pack, True), scaled_msgs)(act_in[0], after=grad_near)
    grad_msgs = within([*grad_msgs, *grad_near])
    (grad_arrived,) = arrived("far_grad", cur_msgs[0], *grad_msgs[1:3])
    (grad,) = run("take_grad", part(take_grad_body, nb, ngroups), every)(*grad_msgs, after=[grad_arrived])
    sto_shares, cur_msgs = exchanged(sto_shares), within(cur_msgs)
    sto_proj, sto_f, sto_mixed = run(
        "mix_saved", part(mix_shares_body, ngroups, bl), every + by_position + every, scratch(every)
    )(*sto_shares, mq, bd_left, after=[grad])
    *adj_shares, adj_f, adj_first = run(
        "backward", part(backward_body, nb, ngroups, bl), shares + by_position + every, scratch(every)
    )(grad, sto_proj, sto_mixed, mq, bd_left)
    adj_wait = adj_shares[:1]
    adj_shares = exchanged(adj_shares)
    tiles = run(
        "factor_grads",
        part(factor_grads_body, nb, ngroups, bl, ext),
        [sds((nb * (bl + ext), LANE))] * ngroups,
        scratch([sds((ngroups, nb * ext, LANE)), sds((ngroups, nb * bl, LANE))]),
    )(sto_f, adj_f, adj_first, sto_proj, after=adj_wait)
    tiles_wait = tiles[:1]
    (cur_arrived,) = arrived("far_act", tiles_wait[0], *cur_msgs[1:3])
    (cur_normin,) = run("norm_act", norm, tokens)(*cur_msgs, gain, after=[cur_arrived])
    cur_proj, cur_first = run("project_act", part(project_body, nb, ngroups), tokens * 2)(
        cur_normin, wk, bd_left
    )
    cur_firsts = gathered(cur_first)
    adj_proj, gain_part, *adj_parts = run(
        "adj_norm",
        part(adj_norm_body, nb, ngroups),
        tokens + [sds((1, bd), F32)] + pieces,
        scratch([sds((tg, bd), F32)]),
    )(sto_normin, wk, gain, *adj_shares, after=[cur_first])
    adj_wait = adj_parts[:1]
    adj_parts = within(adj_parts)
    own_gw, *sends = run(
        "weight_grad",
        part(weight_grad_body, nb, ngroups),
        [sds((rows_of, bd), F32)] + [sds((rows_of + SUB + nb * (bl + ext) // chunks, bd))] * (ngroups - 1),
        scratch([sds((bd, bd), F32)]),
    )(sto_normin, adj_proj, gain_part, *tiles[1:], after=adj_wait)
    recvs = [across(sends[e - 1], e) for e in range(1, ngroups)]
    (adj_arrived,) = arrived("far_adj", own_gw, *adj_parts[1:3])
    (cur_mixed,) = run(
        "mix_act", part(mix_body, ngroups, bl), tokens, scratch([sds((nq, n, bd))])
    )(*cur_firsts, mq, after=[adj_arrived])
    out_parts = run("output", part(output_body, nb, ngroups), pieces)(cur_mixed, cur_proj, *cur_msgs)
    (adj_x,) = run(
        "input_grad", part(input_grad_body, nb, ngroups), [sds((t, width))], scratch([sds((t, width), F32)])
    )(saved_in[0], grad_in[0], gain, *adj_parts, after=out_parts[:1])
    gw_parts = run(
        "weight_sum",
        part(weight_sum_body, nb, ngroups, bl, ext),
        [sds((r4 + bl + ext + SUB, LANE))] * nb,
        scratch([sds((rows_of, bd)), sds((ngroups, 1, bd), F32), sds((nb * (bl + ext), LANE))]),
    )(own_gw, gain_part, *recvs, tiles[0], after=[adj_x])
    gw_wait = gw_parts[:1]
    gw_parts = within(gw_parts)
    out_parts = handed(out_parts, 1)
    grad_handed = lax.ppermute(adj_x, "pipe", [(p, (p - 1) % npipe) for p in range(npipe)])
    handed_on, done = run("join_out", join, [sds((t, width)), sds((8, LANE), F32)])(
        *out_parts, after=gw_wait
    )
    grad_handed, done = run("store", store_body, [sds((t, width)), sds((8, LANE), F32)])(
        grad_handed, after=[done]
    )
    weight_grad, gain_grad, left_grad, right_grad = run(
        "join_weight",
        part(join_weight_body, nb, ngroups),
        [
            sds((r, nb, bd), F32),
            sds((1, width), F32),
            sds((left_blocks.shape[1], bl, bl), F32),
            sds((npos, ext, ext), F32),
        ],
        scratch([sds((nb, r, bd), F32)]),
    )(*gw_parts, after=[done])
    return (
        handed_on[None],
        grad_handed[None],
        weight_grad[None],
        gain_grad,
        left_grad[None],
        right_grad[None],
    )


def solution(mesh):
    tokens = P("pipe", "seq", None)
    factor = P("pipe", "seq", None, None)
    return jax.shard_map(
        shards,
        mesh=mesh,
        in_specs=(tokens, tokens, tokens, P("pipe", None), factor, factor, factor),
        out_specs=(tokens, tokens, factor, P("pipe", None), factor, factor),
        check_vma=False,
    )
```

```python
import functools

import jax
import jax.numpy as jnp
from jax import lax
from jax.experimental import pallas as pl
from jax.experimental.pallas import tpu as pltpu
from jax.sharding import PartitionSpec as P

BF = jnp.bfloat16
F32 = jnp.float32
LANE = 128
SUB = 16
EPS = 1e-06
COST = {"relay": 3, "far_saved": 3, "far_grad": 6.0, "norm_act": 3, "join_weight": 3, "join_out": 5, "far_adj": 2}
VMEM = 48 * 1024 * 1024


def position(ngroups):
    me = lax.axis_index("seq")
    return me % ngroups, me // ngroups


def far(d, nb):
    return (nb - d) % nb


def natural(pos, nb, ngroups, na):
    return ((pos // na % nb) * ngroups + pos // (nb * na)) * na + pos % na


def split3(x):
    hi = x.astype(BF).astype(F32)
    mid = (x - hi).astype(BF).astype(F32)
    return hi, mid, x - hi - mid


def eye(n):
    return lax.broadcasted_iota(jnp.int32, (n, n), 0) == lax.broadcasted_iota(jnp.int32, (n, n), 1)


def to_row(col):
    return jnp.sum(jnp.where(eye(col.shape[0]), col, 0.0), axis=0, keepdims=True)


def to_col(row):
    return jnp.sum(jnp.where(eye(row.shape[1]), row, 0.0), axis=1, keepdims=True)


def mm(a, b, ca=1, cb=0):
    return lax.dot_general(a, b, (((ca,), (cb,)), ((), ())), preferred_element_type=F32)


def rows(start, size):
    return pl.ds(pl.multiple_of(start, size), size)


def call(body, outs, scratch, direct, name):
    def run(*args, after=()):
        nin, nwait = len(args), len(after)
        vmem, anywhere = pl.BlockSpec(memory_space=pltpu.VMEM), pl.BlockSpec(memory_space=pl.ANY)

        def without_waits(*refs):
            return body(*refs[:nin], *refs[nin + nwait :])

        return pl.pallas_call(
            without_waits,
            out_shape=list(outs),
            in_specs=[anywhere] * direct + [vmem] * (nin - direct) + [anywhere] * nwait,
            out_specs=[pl.BlockSpec(memory_space=pltpu.HBM)] * direct + [vmem] * (len(outs) - direct),
            scratch_shapes=list(scratch),
            compiler_params=pltpu.CompilerParams(vmem_limit_bytes=VMEM),
            cost_estimate=pl.CostEstimate(
                flops=int(COST.get(name, 0.0) * 1e9), bytes_accessed=0, transcendentals=0
            ),
            name=name,
        )(*args, *after)

    return run


def sds(shape, dtype=BF):
    return jax.ShapeDtypeStruct(shape, dtype)


def pack_weight_body(nb, ngroups, w_ref, l_ref, r_ref, *outs):
    _, block = position(ngroups)
    r, bd = w_ref.shape[1], w_ref.shape[2]
    chunks = bd // LANE
    bl, ext = l_ref.shape[1], r_ref.shape[1]
    left = jnp.concatenate([l_ref[j].astype(F32) for j in range(l_ref.shape[0])], axis=1).astype(BF)
    right = jnp.concatenate([r_ref[j].astype(F32) for j in range(r_ref.shape[0])], axis=1).astype(BF)
    for d in range(nb):
        for ch in range(chunks):
            outs[d][ch * r : (ch + 1) * r, :] = w_ref[block ^ far(d, nb), :, ch * LANE : (ch + 1) * LANE]
        outs[d][chunks * r : chunks * r + bl, :] = left
        outs[d][chunks * r + bl :, :] = right


def pack_tokens_body(nb, ngroups, with_scale, x_ref, *outs, which=None):
    _, block = position(ngroups)
    t, width = x_ref.shape
    bd = width // nb
    chunks = bd // LANE
    if with_scale:
        x = x_ref[...].astype(F32)
        inv = lax.rsqrt(jnp.mean(x * x, axis=-1, keepdims=True) + EPS)
        parts = split3(to_row(inv))
        tile = jnp.concatenate(list(parts) + [jnp.zeros((SUB - 3, t), F32)], axis=0).astype(BF)
    for d, out in zip(which or range(nb), outs):
        for ch in range(chunks):
            lanes = pl.ds(pl.multiple_of((block ^ far(d, nb)) * bd + ch * LANE, LANE), LANE)
            out[ch * t : (ch + 1) * t, :] = x_ref[:, lanes]
        if with_scale:
            out[chunks * t :, :] = tile


def pick(n, part_of, part):
    row = lax.broadcasted_iota(jnp.int32, (n, part_of), 0)
    col = lax.broadcasted_iota(jnp.int32, (n, part_of), 1)
    return jnp.where(row == part * part_of + col, 1.0, 0.0).astype(BF)


def share_of(ref, first, n, part_of, part):
    if part_of % LANE == 0:
        return ref[:, pl.ds(pl.multiple_of(first + part * part_of, LANE), part_of)]
    return mm(ref[:, first : first + n], pick(n, part_of, part)).astype(BF)


def split_features_body(nb, ngroups, x_ref, *outs):
    group, _ = position(ngroups)
    part_of = outs[0].shape[2]
    bd = x_ref.shape[1] // nb
    for e in range(ngroups):
        for k in range(nb):
            outs[e][k] = share_of(x_ref, k * bd, bd, part_of, group ^ e)


def pack_shares_body(nb, ngroups, which, *refs):
    group, place = position(ngroups)
    shares, outs = refs[:ngroups], refs[ngroups:]
    t = shares[0].shape[1]
    for d, out in zip(which, outs):
        for e in range(ngroups):
            out[rows((group ^ e) * t, t), :] = shares[e][place ^ far(d, nb)]


def relay_body(nb, ngroups, r4, ext, *refs):
    _, place = position(ngroups)
    out = refs[nb]
    bl = refs[0].shape[0] - r4 - ext
    for d in range(nb):
        to = place ^ far(d, nb)
        out[rows(to * r4, r4), :] = refs[d][:r4, :]
        out[pl.ds(pl.multiple_of(nb * r4 + to * ext, ext), ext), :] = refs[d][r4 + bl :, :]
        out[pl.ds(pl.multiple_of(nb * (r4 + ext) + to * bl, bl), bl), :] = refs[d][r4 : r4 + bl, :]


def expand_matrix(ext, nb, ngroups, na):
    n = SUB * ext
    row = lax.broadcasted_iota(jnp.int32, (n, n), 0)
    col = lax.broadcasted_iota(jnp.int32, (n, n), 1)
    return jnp.where((row // ext == col % SUB) & (row % ext == natural(col // SUB, nb, ngroups, na)), 1.0, 0.0).astype(BF)


def same_position(n):
    row = lax.broadcasted_iota(jnp.int32, (n, n), 0)
    col = lax.broadcasted_iota(jnp.int32, (n, n), 1)
    return row % SUB == col % SUB


def assemble_body(nb, ngroups, r, ext, bl, *refs):
    group, _ = position(ngroups)
    na = LANE // bl
    relays = refs[:ngroups]
    wk_ref, mq_ref, bd_ref, all_ref = refs[ngroups:]
    chunks = wk_ref.shape[1] // LANE
    r4 = chunks * r
    for e in range(ngroups):
        g = group ^ e
        for c in range(nb):
            for ch in range(chunks):
                wk_ref[rows((c * ngroups + g) * r, r), ch * LANE : (ch + 1) * LANE] = relays[e][
                    c * r4 + ch * r : c * r4 + (ch + 1) * r, :
                ]
            all_ref[c * ngroups + g] = relays[e][nb * r4 + c * ext : nb * r4 + (c + 1) * ext, :]
    nq = mq_ref.shape[0]
    per = nb * ngroups // nq
    n = SUB * ext
    turn = expand_matrix(ext, nb, ngroups, na)
    spread = jnp.where(
        natural(lax.broadcasted_iota(jnp.int32, (n, ext), 0) // SUB, nb, ngroups, na)
        == lax.broadcasted_iota(jnp.int32, (n, ext), 1),
        1.0,
        0.0,
    ).astype(BF)
    same = same_position(n)
    for q in range(nq):
        tiles = jnp.concatenate([all_ref[q * per + i] for i in range(per)], axis=1)
        wide = mm(tiles, turn).astype(BF)
        mq_ref[q] = jnp.where(same, mm(spread, wide), 0.0).astype(BF)
    half_row = lax.broadcasted_iota(jnp.int32, (LANE, LANE), 0) // bl
    half_col = lax.broadcasted_iota(jnp.int32, (LANE, LANE), 1) // bl
    for e in range(ngroups):
        for c in range(nb):
            at = nb * (r4 + ext) + c * bl
            both = jnp.concatenate([relays[e][at : at + bl, :].astype(F32)] * na, axis=0)
            bd_ref[(group ^ e) * nb + c] = jnp.where(half_row == half_col, both, 0.0).astype(BF)


def unpack(msg, t, chunks):
    return jnp.concatenate([msg[ch * t : (ch + 1) * t, :] for ch in range(chunks)], axis=1)


def scale_of(msg, t, chunks):
    tile = msg[chunks * t : chunks * t + SUB, :].astype(F32)
    return to_col(tile[0:1] + tile[1:2] + tile[2:3])


def norm_body(nb, ngroups, *refs):
    _, place = position(ngroups)
    msgs = refs[:nb]
    gain_ref, normin_ref = refs[nb:]
    t = LANE
    bd = normin_ref.shape[1]
    chunks = bd // LANE
    gain = gain_ref[:, pl.ds(pl.multiple_of(place * bd, LANE), bd)]
    for d in range(nb):
        x = unpack(msgs[d], t, chunks).astype(F32)
        normed = x * scale_of(msgs[d], t, chunks)
        normin_ref[rows((place ^ far(d, nb)) * t, t), :] = (normed * gain).astype(BF)


def project_body(nb, ngroups, normin_ref, wk_ref, bd_ref, proj_ref, first_ref):
    group, _ = position(ngroups)
    t = LANE
    proj_ref[...] = mm(normin_ref[...], wk_ref[...]).astype(BF)
    for c in range(nb):
        at = slice(c * t, (c + 1) * t)
        first_ref[at, :] = mm(bd_ref[group * nb + c], proj_ref[at, :]).astype(BF)


def project_shares_body(ngroups, normin_ref, wk_ref, *refs):
    group, _ = position(ngroups)
    outs, proj_ref = refs[:ngroups], refs[ngroups]
    bd = wk_ref.shape[0]
    proj_ref[...] = mm(normin_ref[...], wk_ref[...]).astype(BF)
    for e in range(ngroups):
        outs[e][...] = share_of(proj_ref, 0, bd, bd // ngroups, group ^ e)


def gather_positions(group, bl, parts, out_ref):
    blocks = parts[0].shape[0] // bl
    for e, part in enumerate(parts):
        base = (group ^ e) * blocks * SUB
        for q in range(bl // SUB):
            for a in range(blocks):
                out_ref[q, pl.ds(pl.multiple_of(base + a * SUB, SUB), SUB), :] = part[
                    a * bl + q * SUB : a * bl + (q + 1) * SUB, :
                ]


def mix_body(ngroups, bl, *refs):
    group, _ = position(ngroups)
    firsts = refs[:ngroups]
    mq_ref, mixed_ref, f_ref = refs[ngroups:]
    gather_positions(group, bl, firsts, f_ref)
    blocks = firsts[0].shape[0] // bl
    own = rows(group * blocks * SUB, blocks * SUB)
    for q in range(bl // SUB):
        mixed = mm(mq_ref[q, own, :], f_ref[q]).astype(BF)
        for a in range(blocks):
            mixed_ref[a * bl + q * SUB : a * bl + (q + 1) * SUB, :] = mixed[a * SUB : (a + 1) * SUB, :]


def output_body(nb, ngroups, mixed_ref, proj_ref, *refs):
    _, place = position(ngroups)
    msgs, outs = refs[:nb], refs[nb:]
    t = LANE
    chunks = proj_ref.shape[1] // LANE
    for d in range(nb):
        at = rows((place ^ far(d, nb)) * t, t)
        x = unpack(msgs[d], t, chunks).astype(F32)
        outs[d][...] = (x + proj_ref[at, :].astype(F32) * mixed_ref[at, :].astype(F32)).astype(BF)


def to_positions(x_ref, out_ref, bl):
    for q in range(bl // SUB):
        for a in range(x_ref.shape[0] // bl):
            out_ref[q, a * SUB : (a + 1) * SUB, :] = x_ref[a * bl + q * SUB : a * bl + (q + 1) * SUB, :]


def from_positions(x, q, out_ref, bl):
    for a in range(out_ref.shape[0] // bl):
        out_ref[a * bl + q * SUB : a * bl + (q + 1) * SUB, :] = x[a * SUB : (a + 1) * SUB, :]


def mix_shares_body(ngroups, bl, *refs):
    group, _ = position(ngroups)
    parts = refs[:ngroups]
    mq_ref, bd_ref, proj_ref, f_ref, mixed_ref, first_ref = refs[ngroups:]
    t = LANE
    tg = parts[0].shape[0]
    for e in range(ngroups):
        proj_ref[rows((group ^ e) * tg, tg), :] = parts[e][...]
    for c in range(bd_ref.shape[0]):
        at = slice(c * t, (c + 1) * t)
        first_ref[at, :] = mm(bd_ref[c], proj_ref[at, :]).astype(BF)
    to_positions(first_ref, f_ref, bl)
    for q in range(bl // SUB):
        from_positions(mm(mq_ref[q], f_ref[q]).astype(BF), q, mixed_ref, bl)


def take_grad_body(nb, ngroups, *refs):
    _, place = position(ngroups)
    grad_ref = refs[nb]
    t = LANE
    for d in range(nb):
        for g in range(ngroups):
            grad_ref[rows((g * nb + (place ^ far(d, nb))) * t, t), :] = refs[d][g * t : (g + 1) * t, :]


def backward_body(nb, ngroups, bl, *refs):
    group, _ = position(ngroups)
    grad_ref, proj_ref, mixed_ref, mq_ref, bd_ref = refs[:5]
    outs = refs[5 : 5 + ngroups]
    a_ref, adj_first_ref, adj_ref = refs[5 + ngroups :]
    t = LANE
    adj_ref[...] = (grad_ref[...].astype(F32) * proj_ref[...].astype(F32)).astype(BF)
    to_positions(adj_ref, a_ref, bl)
    for q in range(bl // SUB):
        from_positions(mm(mq_ref[q], a_ref[q], 0, 0).astype(BF), q, adj_first_ref, bl)
    for c in range(bd_ref.shape[0]):
        at = slice(c * t, (c + 1) * t)
        grad = grad_ref[at, :].astype(F32)
        mixed = mixed_ref[at, :].astype(F32)
        adj_ref[at, :] = (grad * mixed + mm(bd_ref[c], adj_first_ref[at, :], 0, 0)).astype(BF)
    tg = nb * t
    for e in range(ngroups):
        outs[e][...] = adj_ref[rows((group ^ e) * tg, tg), :]


def factor_grads_body(nb, ngroups, bl, ext, f_ref, a_ref, adj_first_ref, proj_ref, *refs):
    group, _ = position(ngroups)
    outs, right_ref, left_ref = refs[:ngroups], refs[ngroups], refs[ngroups + 1]
    na = LANE // bl
    t = LANE
    nq = f_ref.shape[0]
    n = SUB * ext
    upper = lax.broadcasted_iota(jnp.int32, (bl, LANE), 1) < bl
    for g in range(ngroups):
        for c in range(nb):
            at = slice((g * nb + c) * t, (g * nb + c + 1) * t)
            both = mm(adj_first_ref[at, :], proj_ref[at, :], 1, 1)
            left_ref[g, c * bl : (c + 1) * bl, :] = jnp.where(upper, both[:bl, :], both[bl:, :]).astype(BF)
    turn = expand_matrix(ext, nb, ngroups, na)
    same = same_position(n)
    order = jnp.where(
        natural(lax.broadcasted_iota(jnp.int32, (ext, ext), 0), nb, ngroups, na)
        == lax.broadcasted_iota(jnp.int32, (ext, ext), 1),
        1.0,
        0.0,
    ).astype(BF)
    per = nb * ngroups // nq
    for q in range(nq):
        pairs = jnp.where(same, mm(a_ref[q], f_ref[q], 1, 1), 0.0)
        summed = jnp.sum(pairs.reshape(ext, SUB, n), axis=1).astype(BF)
        turned = mm(order, mm(summed, turn, 1, 1).astype(BF), 0, 0).astype(BF)
        for i in range(per):
            s = q * per + i
            right_ref[s % ngroups, (s // ngroups) * ext : (s // ngroups + 1) * ext, :] = turned[
                :, i * LANE : (i + 1) * LANE
            ]
    for e in range(ngroups):
        outs[e][: nb * bl, :] = left_ref[group ^ e]
        outs[e][nb * bl :, :] = right_ref[group ^ e]


def adj_norm_body(nb, ngroups, normin_ref, wk_ref, gain_ref, *refs):
    group, place = position(ngroups)
    shares, rest = refs[:ngroups], refs[ngroups:]
    adj_proj_ref, gain_part_ref, outs, adj_norm_ref = rest[0], rest[1], rest[2 : 2 + nb], rest[2 + nb]
    bd = wk_ref.shape[0]
    t = LANE
    part_of = bd // ngroups
    if part_of % LANE == 0:
        for e in range(ngroups):
            adj_proj_ref[:, pl.ds(pl.multiple_of((group ^ e) * part_of, LANE), part_of)] = shares[e][...]
    else:
        adj_proj = jnp.zeros(adj_proj_ref.shape, F32)
        for e in range(ngroups):
            adj_proj = adj_proj + mm(shares[e][...], pick(bd, part_of, group ^ e), 1, 1)
        adj_proj_ref[...] = adj_proj.astype(BF)
    adj_norm = mm(adj_proj_ref[...], wk_ref[...], 1, 1)
    adj_norm_ref[...] = adj_norm
    gain = gain_ref[:, pl.ds(pl.multiple_of(place * bd, LANE), bd)]
    gain_part_ref[...] = jnp.sum(adj_norm * normin_ref[...].astype(F32), axis=0, keepdims=True) / gain
    for d in range(nb):
        outs[d][...] = adj_norm_ref[rows((place ^ far(d, nb)) * t, t), :].astype(BF)


def weight_grad_body(nb, ngroups, normin_ref, adj_proj_ref, gain_part_ref, *refs):
    group, _ = position(ngroups)
    tiles, own_ref = refs[: ngroups - 1], refs[ngroups - 1]
    sends, gw_ref = refs[ngroups : 2 * ngroups - 1], refs[2 * ngroups - 1]
    share, bd = own_ref.shape
    r = share // nb
    gw_ref[...] = mm(normin_ref[...], adj_proj_ref[...], 0, 0)
    tile = jnp.concatenate(
        list(split3(gain_part_ref[...])) + [jnp.zeros((SUB - 3, bd), F32)], axis=0
    ).astype(BF)
    for c in range(nb):
        at = slice(c * r, (c + 1) * r)
        own_ref[at, :] = gw_ref[rows((c * ngroups + group) * r, r), :]
        for e in range(1, ngroups):
            sends[e - 1][at, :] = gw_ref[rows((c * ngroups + (group ^ e)) * r, r), :].astype(BF)
    for e in range(1, ngroups):
        sends[e - 1][share : share + SUB, :] = tile
        high = tiles[e - 1].shape[0] * LANE // bd
        for ch in range(bd // LANE):
            sends[e - 1][share + SUB :, ch * LANE : (ch + 1) * LANE] = tiles[e - 1][
                ch * high : (ch + 1) * high, :
            ]


def weight_sum_body(nb, ngroups, bl, ext, own_ref, gain_part_ref, *refs):
    group, place = position(ngroups)
    recvs, tiles_ref = refs[: ngroups - 1], refs[ngroups - 1]
    high = tiles_ref.shape[0] * LANE // own_ref.shape[1]
    outs = refs[ngroups : ngroups + nb]
    total_ref, gains_ref, sums_ref = refs[ngroups + nb :]
    share, bd = own_ref.shape
    chunks = bd // LANE
    r = share // nb
    total = own_ref[...]
    gains_ref[group] = gain_part_ref[...]
    for e in range(1, ngroups):
        total = total + recvs[e - 1][:share, :].astype(F32)
        three = recvs[e - 1][share : share + SUB, :].astype(F32)
        gains_ref[group ^ e] = three[0:1] + three[1:2] + three[2:3]
    total_ref[...] = total.astype(BF)
    for ch in range(chunks):
        at = slice(ch * high, (ch + 1) * high)
        tile_sum = tiles_ref[at, :].astype(F32)
        for recv in recvs:
            tile_sum = tile_sum + recv[share + SUB :, ch * LANE : (ch + 1) * LANE].astype(F32)
        sums_ref[at, :] = tile_sum.astype(BF)
    gain = gains_ref[0]
    for g in range(1, ngroups):
        gain = gain + gains_ref[g]
    three = split3(gain)
    parts = [p[:, ch * LANE : (ch + 1) * LANE] for p in three for ch in range(chunks)]
    tile = jnp.concatenate(parts + [jnp.zeros((SUB - len(parts), LANE), F32)], axis=0).astype(BF)
    for d in range(nb):
        to = place ^ far(d, nb)
        for ch in range(chunks):
            outs[d][ch * r : (ch + 1) * r, :] = total_ref[rows(to * r, r), ch * LANE : (ch + 1) * LANE]
        at = chunks * r
        outs[d][at : at + bl, :] = sums_ref[rows(to * bl, bl), :]
        outs[d][at + bl : at + bl + ext, :] = sums_ref[
            pl.ds(pl.multiple_of(nb * bl + to * ext, ext), ext), :
        ]
        outs[d][at + bl + ext :, :] = tile


def input_grad_body(nb, ngroups, x_ref, grad_ref, gain_ref, *refs):
    _, place = position(ngroups)
    parts, out, adj_ref = refs[:nb], refs[nb], refs[nb + 1]
    bd = parts[0].shape[1]
    for d in range(nb):
        adj_ref[:, pl.ds(pl.multiple_of((place ^ far(d, nb)) * bd, LANE), bd)] = parts[d][...].astype(F32)
    x = x_ref[...].astype(F32)
    inv = lax.rsqrt(jnp.mean(x * x, axis=-1, keepdims=True) + EPS)
    normed = x * inv
    scaled = adj_ref[...] * gain_ref[...]
    mean = jnp.mean(scaled * normed, axis=-1, keepdims=True)
    out[...] = (grad_ref[...].astype(F32) + inv * (scaled - normed * mean)).astype(BF)


def join_body(nb, ngroups, *refs):
    _, block = position(ngroups)
    out, done_ref = refs[nb:]
    done_ref[...] = jnp.zeros(done_ref.shape, done_ref.dtype)
    bd = refs[0].shape[1]
    for d in range(nb):
        out[:, pl.ds(pl.multiple_of((block ^ far(d, nb)) * bd, LANE), bd)] = refs[d][...]


def join_weight_body(nb, ngroups, *refs):
    _, block = position(ngroups)
    gw_ref, gain_ref, left_out, right_out, by_block = refs[nb:]
    r, _, bd = gw_ref.shape
    chunks = bd // LANE
    na, bl, _ = left_out.shape
    npos, ext, _ = right_out.shape
    at = chunks * r
    left = refs[0][at : at + bl, :].astype(F32)
    right = refs[0][at + bl : at + bl + ext, :].astype(F32)
    for d in range(1, nb):
        left = left + refs[d][at : at + bl, :].astype(F32)
        right = right + refs[d][at + bl : at + bl + ext, :].astype(F32)
    for j in range(na):
        left_out[j] = left[:, j * bl : (j + 1) * bl]
    for j in range(npos):
        right_out[j] = right[:, j * ext : (j + 1) * ext]
    for d in range(nb):
        k = block ^ far(d, nb)
        by_block[k] = unpack(refs[d], r, chunks).astype(F32)
        tile = refs[d][at + bl + ext :, :].astype(F32)
        for ch in range(chunks):
            gain_ref[:, pl.ds(pl.multiple_of(k * bd + ch * LANE, LANE), LANE)] = (
                tile[ch : ch + 1] + tile[chunks + ch : chunks + ch + 1] + tile[2 * chunks + ch : 2 * chunks + ch + 1]
            )
    for k in range(nb):
        gw_ref[:, k, :] = by_block[k]


def arrived_body(out_ref):
    out_ref[...] = jnp.zeros(out_ref.shape, out_ref.dtype)


def store_body(x_ref, out_ref, done_ref):
    out_ref[...] = x_ref[...]
    done_ref[...] = jnp.zeros(done_ref.shape, done_ref.dtype)


def shards(act_in, saved_in, grad_in, gain, weight, left_blocks, right_blocks):
    nseq = lax.axis_size("seq")
    npipe = lax.axis_size("pipe")
    _, t, width = act_in.shape
    _, r, nb, bd = weight.shape
    ngroups = nseq // nb
    bl = left_blocks.shape[2]
    ext = right_blocks.shape[2]
    npos = right_blocks.shape[1]
    chunks = bd // LANE
    tg = nb * t
    r4 = chunks * r
    nq = bl // SUB
    n = SUB * ext

    def within(parts):
        return [parts[0]] + [
            lax.ppermute(parts[d], "seq", [(s, s ^ (far(d, nb) * ngroups)) for s in range(nseq)])
            for d in range(1, nb)
        ]

    def across(block, e):
        return lax.ppermute(block, "seq", [(s, s ^ e) for s in range(nseq)])

    def gathered(block):
        return [block] + [across(block, e) for e in range(1, ngroups)]

    def handed(parts, step):
        return [
            lax.ppermute(
                parts[d],
                ("pipe", "seq"),
                [
                    (p * nseq + s, (p + step) % npipe * nseq + (s ^ (far(d, nb) * ngroups)))
                    for p in range(npipe)
                    for s in range(nseq)
                ],
            )
            for d in range(nb)
        ]

    def exchanged(parts):
        return list(parts[:1]) + [across(parts[e], e) for e in range(1, ngroups)]

    part = functools.partial
    def run(name, body, outs, scratch=(), direct=0):
        return call(body, outs, scratch, direct, name)

    def arrived(name, *parts):
        return run(name, arrived_body, [sds((8, LANE), F32)])(after=parts)

    pack = part(pack_tokens_body, nb, ngroups)
    norm = part(norm_body, nb, ngroups)
    join = part(join_body, nb, ngroups)
    scaled_msgs = [sds((chunks * t + SUB, LANE))] * nb
    tokens = [sds((tg, bd))]
    pieces = [sds((t, bd))] * nb
    rows_of = bd // ngroups
    part_of = bd // ngroups
    shares = [sds((tg, part_of))] * ngroups
    every = [sds((ngroups * tg, part_of))]
    by_position = [sds((nq, n, part_of))]

    def scratch(structs):
        return [pltpu.VMEM(s.shape, s.dtype) for s in structs]

    w_msgs = run("pack_weight", part(pack_weight_body, nb, ngroups), [sds((r4 + bl + ext, LANE))] * nb)(
        jnp.transpose(weight[0], (1, 0, 2)), left_blocks[0], right_blocks[0]
    )
    grad_shares = run(
        "split_grad", part(split_features_body, nb, ngroups), [sds((nb, t, part_of))] * ngroups
    )(grad_in[0], after=w_msgs[:1])
    sto_msgs = run("pack_saved", part(pack, True), scaled_msgs)(saved_in[0], after=grad_shares[:1])
    early = sto_msgs[:1]
    w_msgs, grad_shares, sto_msgs = within(w_msgs), exchanged(grad_shares), within(sto_msgs)
    (relay,) = run("relay", part(relay_body, nb, ngroups, r4, ext), [sds((nb * (r4 + ext + bl), LANE))])(
        *w_msgs, after=early
    )
    relays = gathered(relay)
    def pack_grad(name, which, after):
        body = part(pack_shares_body, nb, ngroups, which)
        return run(name, body, [sds((ngroups * t, part_of))] * len(which))(*grad_shares, after=[after])

    grad_msgs = pack_grad("pack_grad", range(nb - 1), relay)
    (sto_arrived,) = arrived("far_saved", grad_msgs[0], *sto_msgs[1:3])
    (sto_normin,) = run("norm_saved", norm, tokens)(*sto_msgs, gain, after=[sto_arrived])
    wk, mq, bd_left = run(
        "assemble",
        part(assemble_body, nb, ngroups, r, ext, bl),
        [sds((bd, bd)), sds((nq, n, n)), sds((nseq, LANE, LANE))],
        [pltpu.VMEM((nseq, ext, LANE), BF)],
    )(*relays, after=[sto_normin])
    sto_shares = run(
        "project_saved", part(project_shares_body, ngroups), shares, scratch(tokens)
    )(sto_normin, wk)
    grad_near = pack_grad("pack_grad_near", [nb - 1], sto_shares[0])
    cur_msgs = run("pack_act", part(pack, True), scaled_msgs[1:])(act_in[0], after=grad_near)
    grad_msgs = within([*grad_msgs, *grad_near])
    (grad_arrived,) = arrived("far_grad", cur_msgs[0], *grad_msgs[1:3])
    (grad,) = run("take_grad", part(take_grad_body, nb, ngroups), every)(*grad_msgs, after=[grad_arrived])
    sto_shares = exchanged(sto_shares)
    sto_proj, sto_f, sto_mixed = run(
        "mix_saved", part(mix_shares_body, ngroups, bl), every + by_position + every, scratch(every)
    )(*sto_shares, mq, bd_left, after=[grad])
    *adj_shares, adj_f, adj_first = run(
        "backward", part(backward_body, nb, ngroups, bl), shares + by_position + every, scratch(every)
    )(grad, sto_proj, sto_mixed, mq, bd_left)
    adj_wait = adj_shares[:1]
    cur_near = run("pack_act_near", part(pack, True, which=[nb - 1]), scaled_msgs[:1])(
        act_in[0], after=adj_wait
    )
    cur_msgs = within([*cur_msgs, *cur_near])
    adj_shares = exchanged(adj_shares)
    tiles = run(
        "factor_grads",
        part(factor_grads_body, nb, ngroups, bl, ext),
        [sds((nb * (bl + ext), LANE))] * ngroups,
        scratch([sds((ngroups, nb * ext, LANE)), sds((ngroups, nb * bl, LANE))]),
    )(sto_f, adj_f, adj_first, sto_proj, after=adj_wait)
    tiles_wait = tiles[:1]
    (cur_arrived,) = arrived("far_act", tiles_wait[0], *cur_msgs[1:3])
    (cur_normin,) = run("norm_act", norm, tokens)(*cur_msgs, gain, after=[cur_arrived])
    cur_proj, cur_first = run("project_act", part(project_body, nb, ngroups), tokens * 2)(
        cur_normin, wk, bd_left
    )
    cur_firsts = gathered(cur_first)
    adj_proj, gain_part, *adj_parts = run(
        "adj_norm",
        part(adj_norm_body, nb, ngroups),
        tokens + [sds((1, bd), F32)] + pieces,
        scratch([sds((tg, bd), F32)]),
    )(sto_normin, wk, gain, *adj_shares, after=[cur_first])
    adj_wait = adj_parts[:1]
    adj_parts = within(adj_parts)
    own_gw, *sends = run(
        "weight_grad",
        part(weight_grad_body, nb, ngroups),
        [sds((rows_of, bd), F32)] + [sds((rows_of + SUB + nb * (bl + ext) // chunks, bd))] * (ngroups - 1),
        scratch([sds((bd, bd), F32)]),
    )(sto_normin, adj_proj, gain_part, *tiles[1:], after=adj_wait)
    recvs = [across(sends[e - 1], e) for e in range(1, ngroups)]
    (adj_arrived,) = arrived("far_adj", own_gw, *adj_parts[1:3])
    (cur_mixed,) = run(
        "mix_act", part(mix_body, ngroups, bl), tokens, scratch([sds((nq, n, bd))])
    )(*cur_firsts, mq, after=[adj_arrived])
    out_parts = run("output", part(output_body, nb, ngroups), pieces)(cur_mixed, cur_proj, *cur_msgs)
    (adj_x,) = run(
        "input_grad", part(input_grad_body, nb, ngroups), [sds((t, width))], scratch([sds((t, width), F32)])
    )(saved_in[0], grad_in[0], gain, *adj_parts, after=out_parts[:1])
    gw_parts = run(
        "weight_sum",
        part(weight_sum_body, nb, ngroups, bl, ext),
        [sds((r4 + bl + ext + SUB, LANE))] * nb,
        scratch([sds((rows_of, bd)), sds((ngroups, 1, bd), F32), sds((nb * (bl + ext), LANE))]),
    )(own_gw, gain_part, *recvs, tiles[0], after=[adj_x])
    gw_wait = gw_parts[:1]
    gw_parts = within(gw_parts)
    out_parts = handed(out_parts, 1)
    grad_handed = lax.ppermute(adj_x, "pipe", [(p, (p - 1) % npipe) for p in range(npipe)])
    handed_on, done = run("join_out", join, [sds((t, width)), sds((8, LANE), F32)])(
        *out_parts, after=gw_wait
    )
    grad_handed, done = run("store", store_body, [sds((t, width)), sds((8, LANE), F32)])(
        grad_handed, after=[done]
    )
    weight_grad, gain_grad, left_grad, right_grad = run(
        "join_weight",
        part(join_weight_body, nb, ngroups),
        [
            sds((r, nb, bd), F32),
            sds((1, width), F32),
            sds((left_blocks.shape[1], bl, bl), F32),
            sds((npos, ext, ext), F32),
        ],
        scratch([sds((nb, r, bd), F32)]),
    )(*gw_parts, after=[done])
    return (
        handed_on[None],
        grad_handed[None],
        weight_grad[None],
        gain_grad,
        left_grad[None],
        right_grad[None],
    )


def solution(mesh):
    tokens = P("pipe", "seq", None)
    factor = P("pipe", "seq", None, None)
    return jax.shard_map(
        shards,
        mesh=mesh,
        in_specs=(tokens, tokens, tokens, P("pipe", None), factor, factor, factor),
        out_specs=(tokens, tokens, factor, P("pipe", None), factor, factor),
        check_vma=False,
    )
```
